128 devices in a mesh: slab: 4 (over x), leaf: 32 (over y, z, core).
Axes of the slice: x: 4, y: 4, z: 4, core: 2. Of those that a mesh axis runs over, the one named last changes fastest.
Arguments:
- right_sides: bfloat16 [32, 524288], P(None, ('slab', 'leaf')), may hold values from -6 to 6
- left_sides: bfloat16 [32, 524288], P(None, ('slab', 'leaf')), may hold values from -6 to 6
- near_blocks: bfloat16 [4096, 8, 128, 128], P(('slab', 'leaf')), may hold values from -0.1875 to 0.1875
- near_columns: int32 [4096, 8], P(('slab', 'leaf')), may hold values from 0 to 4095, as said below
- cluster_points: int32 [4096], P(('slab', 'leaf')), may hold values from 64 to 128, as said below
- leaf_basis: bfloat16 [4096, 64, 128], P(('slab', 'leaf')), may hold values from -0.5 to 0.5
- transfer: float32 [4096, 64, 128], P(('slab', 'leaf')), may hold values from -0.625 to 0.625
- far_parents: int32 [128, 96], P(('slab', 'leaf')), may hold values from 0 to 127, as said below
- far_count: int32 [128], P(('slab', 'leaf')), may hold values from 48 to 96, as said below
- coupling: float32 [128, 96, 128, 128], P(('slab', 'leaf')), may hold values from -0.1875 to 0.1875
- slab_transfer: float32 [128, 128, 128], P(('slab', 'leaf')), may hold values from -0.5 to 0.5
- apex_coupling: float32 [4, 4, 128, 128], replicated, may hold values from -0.75 to 0.75
Outputs:
- product: float32 [32, 524288], P(None, ('slab', 'leaf'))
- adjoint_product: float32 [32, 524288], P(None, ('slab', 'leaf'))
The draws below stay inside these ranges and needn't reach their ends.
Inputs may be any that keep to these rules, and one draw needn't show every extreme that they name: `near_columns`: row i holds 8 different clusters, i among them, all inside the window of 9 consecutive clusters centred on i, moved inward where it would pass an end of 0 to 4095. `cluster_points`: some cluster has exactly 128 points and some exactly 64. `far_parents`: row p holds 96 different parents, none equal to p; only the first far_count[p] are used. `far_count`: some parent uses all 96 slots and some exactly 48.
All inputs are finite; a program needn't handle non-finite values.
Results may differ from the reference program's by a relative error of at most 0.0024.
Values may be sent and summed in bfloat16 or wider, within the bound.
No kernel may reach another device: no remote copies, remote signals or barrier semaphores. Data moves between devices by JAX's collectives and lax.ppermute only.
A program may use at most 128 MiB of HBM per device.

```python
import jax
import jax.numpy as jnp
from jax import lax

B = 128
R = 32
K = 64
K2 = 128
K3 = 128
NN = 8
HW = 4
CL = 32
PARENTS = 128
NF = 96
SLABS = 4
PER_SLAB = 32
NC = 4096
N = 524288


def draw_near_columns(key, part):
    window = 2 * HW + 1
    row_index = jnp.arange(NC, dtype=jnp.int32)
    window_start = jnp.clip(row_index - HW, 0, NC - window)
    scores = jax.random.randint(key, (NC, window), 0, 1 << 16, dtype=jnp.int32) * window + jnp.arange(window, dtype=jnp.int32)[None, :]
    own_slot = (row_index - window_start)[:, None] == jnp.arange(window, dtype=jnp.int32)[None, :]
    scores = jnp.where(own_slot, -1, scores)
    ranking = jnp.argsort(scores, axis=1)[:, :NN].astype(jnp.int32)
    return (window_start[:, None] + ranking).astype(jnp.int32)


def draw_cluster_points(key, part):
    values = jax.random.randint(key, (NC,), B // 2, B + 1, dtype=jnp.int32)
    top_slot = jax.random.randint(jax.random.fold_in(key, 1), (), 0, NC, dtype=jnp.int32)
    low_slot = (top_slot + 1) % NC
    return values.at[top_slot].set(B).at[low_slot].set(B // 2).astype(jnp.int32)


def draw_far_parents(key, part):
    scores = jax.random.randint(key, (PARENTS, PARENTS), 0, 1 << 20, dtype=jnp.int32) * PARENTS + jnp.arange(PARENTS, dtype=jnp.int32)[None, :]
    scores = jnp.where(jnp.eye(PARENTS, dtype=jnp.bool_), 1 << 30, scores)
    return jnp.argsort(scores, axis=1)[:, :NF].astype(jnp.int32)


def draw_far_count(key, part):
    values = jax.random.randint(key, (PARENTS,), NF // 2, NF + 1, dtype=jnp.int32)
    top_slot = jax.random.randint(jax.random.fold_in(key, 2), (), 0, PARENTS, dtype=jnp.int32)
    low_slot = (top_slot + 1) % PARENTS
    return values.at[top_slot].set(NF).at[low_slot].set(NF // 2).astype(jnp.int32)


def level_of(stream_key, dims, cuts, smallest, high):
    def one(axis_at, shards_of):
        heights = jax.random.uniform(jax.random.fold_in(jax.random.fold_in(stream_key, 6), axis_at), (shards_of,), jnp.float32, smallest / len(cuts), high / len(cuts))
        return jnp.repeat(jnp.exp(heights), dims[axis_at] // shards_of).reshape((-1,) + (1,) * (len(dims) - axis_at - 1))

    gain = one(*cuts[0])
    for cut in cuts[1:]:
        gain = gain * one(*cut)
    return gain


def noise(stream_key, dims, scale, most, cuts=(), kind=jnp.bfloat16):
    gain = level_of(stream_key, dims, cuts, -0.22, 0.18) if cuts else 1.0
    array = jax.random.normal(stream_key, dims, jnp.float32) * scale * gain
    return jnp.minimum(jnp.maximum(array, -most), most).astype(kind)


def setup_inputs(seed: int = 0) -> dict:
    seeds = jax.random.split(jax.random.key(seed), 13)
    return {
        "right_sides": noise(seeds[0], (R, N), 1.0, 6.0, ((1, 128),)),
        "left_sides": noise(seeds[1], (R, N), 1.0, 6.0, ((1, 128),)),
        "near_blocks": noise(seeds[2], (NC, NN, B, B), (B * NN) ** -0.5, 0.1875, ((0, 128),)),
        "near_columns": draw_near_columns(jax.random.fold_in(seeds[12], 71), 0),
        "cluster_points": draw_cluster_points(jax.random.fold_in(seeds[12], 71), 0),
        "leaf_basis": noise(seeds[5], (NC, K, B), B ** -0.5, 0.5, ((0, 128),)),
        "transfer": noise(seeds[6], (NC, K, K2), ((CL * K * K2) ** -0.25), 0.625, ((0, 128),), jnp.float32),
        "far_parents": draw_far_parents(jax.random.fold_in(seeds[12], 71), 0),
        "far_count": draw_far_count(jax.random.fold_in(seeds[12], 71), 0),
        "coupling": noise(seeds[9], (PARENTS, NF, K2, K2), ((NF * K2 // 2) ** -0.5), 0.1875, ((0, 128),), jnp.float32),
        "slab_transfer": noise(seeds[10], (PARENTS, K2, K3), ((PER_SLAB * K2 * K3) ** -0.25), 0.5, ((0, 128),), jnp.float32),
        "apex_coupling": noise(seeds[11], (SLABS, SLABS, K3, K3), (((SLABS - 1) * K3) ** -0.5), 0.75, (), jnp.float32),
    }


def reference(right_sides, left_sides, near_blocks, near_columns, cluster_points, leaf_basis, transfer, far_parents, far_count, coupling, slab_transfer, apex_coupling):
    uppermost_level = lax.Precision.HIGHEST
    point_mask = jnp.arange(B, dtype=jnp.int32)[None, :] < cluster_points[:, None]
    zero_bf = jnp.zeros((), jnp.bfloat16)
    masked_right = jnp.where(point_mask[None], right_sides.reshape(R, NC, B), zero_bf)
    masked_left = jnp.where(point_mask[None], left_sides.reshape(R, NC, B), zero_bf)
    group_blocks = near_blocks.reshape(PARENTS, CL, NN, B, B)
    group_columns = near_columns.reshape(PARENTS, CL, NN)
    group_left = jnp.transpose(masked_left.reshape(R, PARENTS, CL, B), (1, 0, 2, 3))

    def near_forward(pieces):
        blocks, columns = pieces
        picked = jnp.take(masked_right, columns, axis=1).astype(jnp.float32)
        return jnp.einsum("csab,rcsb->rca", blocks.astype(jnp.float32), picked, precision=uppermost_level)

    near_out = lax.map(near_forward, (group_blocks, group_columns))
    near_out = jnp.transpose(near_out, (1, 0, 2, 3)).reshape(R, NC, B)

    def near_transposed(total, pieces):
        blocks, columns, lefts = pieces
        contrib = jnp.einsum("csab,rca->csrb", blocks.astype(jnp.float32), lefts.astype(jnp.float32), precision=uppermost_level)
        total = total.at[columns.reshape(-1)].add(contrib.reshape(CL * NN, R, B))
        return total, None

    near_back, _ = lax.scan(near_transposed, jnp.zeros((NC, R, B), jnp.float32), (group_blocks, group_columns, group_left))
    near_back = jnp.transpose(near_back, (1, 0, 2))

    basis_wide = leaf_basis.astype(jnp.float32)
    leaf_right = jnp.einsum("ckb,rcb->ckr", basis_wide, masked_right.astype(jnp.float32), precision=uppermost_level)
    leaf_left = jnp.einsum("ckb,rcb->ckr", basis_wide, masked_left.astype(jnp.float32), precision=uppermost_level)
    parent_right = jnp.einsum("ckq,ckr->cqr", transfer, leaf_right, precision=uppermost_level).reshape(PARENTS, CL, K2, R).sum(axis=1)
    parent_left = jnp.einsum("ckq,ckr->cqr", transfer, leaf_left, precision=uppermost_level).reshape(PARENTS, CL, K2, R).sum(axis=1)

    live = (jnp.arange(NF, dtype=jnp.int32)[None, :] < far_count[:, None]).astype(jnp.float32)
    far_right = jnp.einsum("pf,pfab,pfbr->par", live, coupling, parent_right[far_parents], precision=uppermost_level)
    outward = jnp.einsum("pf,pfab,par->pfbr", live, coupling, parent_left, precision=uppermost_level)
    far_left = jnp.zeros((PARENTS, K2, R), jnp.float32).at[far_parents.reshape(-1)].add(outward.reshape(PARENTS * NF, K2, R))

    slab_right = jnp.einsum("pqt,pqr->ptr", slab_transfer, parent_right, precision=uppermost_level).reshape(SLABS, PER_SLAB, K3, R).sum(axis=1)
    slab_left_factor = jnp.einsum("pqt,pqr->ptr", slab_transfer, parent_left, precision=uppermost_level).reshape(SLABS, PER_SLAB, K3, R).sum(axis=1)
    remaining_slabs = 1.0 - jnp.eye(SLABS, dtype=jnp.float32)
    apex_right = jnp.einsum("st,stab,tbr->sar", remaining_slabs, apex_coupling, slab_right, precision=uppermost_level)
    apex_left = jnp.einsum("uc,ucnh,unx->chx", remaining_slabs, apex_coupling, slab_left_factor, precision=uppermost_level)
    hat_right = far_right + jnp.einsum("pqt,ptr->pqr", slab_transfer, jnp.repeat(apex_right, PER_SLAB, axis=0), precision=uppermost_level)
    hat_left = far_left + jnp.einsum("pqt,ptr->pqr", slab_transfer, jnp.repeat(apex_left, PER_SLAB, axis=0), precision=uppermost_level)

    down_right = jnp.einsum("ckq,cqr->ckr", transfer, jnp.repeat(hat_right, CL, axis=0), precision=uppermost_level).astype(jnp.bfloat16)
    down_left = jnp.einsum("ckq,cqr->ckr", transfer, jnp.repeat(hat_left, CL, axis=0), precision=uppermost_level).astype(jnp.bfloat16)
    far_out = jnp.einsum("ckb,ckr->rcb", basis_wide, down_right.astype(jnp.float32), precision=uppermost_level)
    far_back = jnp.einsum("ckb,ckr->rcb", basis_wide, down_left.astype(jnp.float32), precision=uppermost_level)
    zero_wide = jnp.zeros((), jnp.float32)
    product = jnp.where(point_mask[None], near_out + far_out, zero_wide).reshape(R, N)
    adjoint_product = jnp.where(point_mask[None], near_back + far_back, zero_wide).reshape(R, N)
    return product, adjoint_product
```

```python
import jax
import jax.numpy as jnp
import numpy as np
from jax import lax
from jax.experimental import pallas as pl
from jax.experimental.pallas import tpu as pltpu
from jax.sharding import PartitionSpec as P

B = 128
HW = 4
AXES = ("slab", "leaf")
BF = jnp.bfloat16
F32 = jnp.float32

CORE, Z1, Z3, Y1, Y3, X1, X3 = 1, 2, 6, 8, 24, 32, 96
REDUCE_ORDER = (CORE, Y1, Y3, Z1, Z3, X1, X3)
GATHER_ORDER = (X1, X3, Z3, Z1, Y1, Y3, CORE)


def swapped(block, mask):
    route = [(i, i ^ mask) for i in range(lax.axis_size(AXES))]
    return lax.ppermute(block, AXES, route)


def passed_along(block, distance):
    devices = range(lax.axis_size(AXES))
    route = [(i - distance, i) for i in devices if i - distance in devices]
    return lax.ppermute(block, AXES, route)


def slot_of(difference, order, first_is_high):
    slot = jnp.zeros_like(difference)
    for step, mask in enumerate(order):
        if mask == CORE:
            bit = difference & 1
        else:
            shift = {Z1: 1, Z3: 1, Y1: 3, Y3: 3, X1: 5, X3: 5}[mask]
            low, high = (difference >> shift) & 1, (difference >> (shift + 1)) & 1
            bit = high if mask in (Z3, Y3, X3) else low ^ high
        place = len(order) - 1 - step if first_is_high else step
        slot = slot | (bit << place)
    return slot


def two(value):
    high = value.astype(BF)
    return high, (value - high.astype(F32)).astype(BF)


def two_outside(value):
    high = lax.reduce_precision(value, 8, 7)
    return high.astype(BF), (value - high).astype(BF)


NN = (((1,), (0,)), ((), ()))
NT = (((1,), (1,)), ((), ()))


def dot(a, b, how):
    return lax.dot_general(a, b, how, preferred_element_type=F32)


def dot3(a, b, how):
    (ah, al), (bh, bl) = two(a), two(b)
    left = jnp.concatenate([ah, al, ah], axis=1)
    right = jnp.concatenate([bh, bh, bl], axis=1 if how is NT else 0)
    return dot(left, right, how)


def up_kernel(
    points, right, left, basis, transfer, lift, mright, mleft, pright, pleft, shares
):
    clusters = basis.shape[0]
    rhs = right.shape[0]
    lane = lax.broadcasted_iota(jnp.int32, (rhs, B), 1)
    total = jnp.zeros((2 * rhs, B), F32)
    for c in range(clusters):
        mask = lane < points[c]
        xr = jnp.where(mask, right[:, c * B : (c + 1) * B].astype(F32), 0.0).astype(BF)
        xl = jnp.where(mask, left[:, c * B : (c + 1) * B].astype(F32), 0.0).astype(BF)
        mright[c] = xr
        mleft[c] = xl
        leaf = dot(jnp.concatenate([xr, xl], axis=0), basis[c], NT)
        total = total + dot3(leaf, transfer[c], NN)
    pright[...] = total[:rhs].astype(BF)
    pleft[...] = total[rhs:]
    shares[...] = dot3(total, lift[0], NN)


def outward_kernel(count, slots, pleft, coupling, keep, send):
    step = pl.program_id(0)
    per = coupling.shape[1]
    half = keep.shape[0]

    @pl.when(step == 0)
    def _():
        keep[...] = jnp.zeros_like(keep)
        send[...] = jnp.zeros_like(send)

    ph, plow = two(pleft[...])
    rhs = ph.shape[0]
    wide = jnp.concatenate([ph, plow], axis=0)
    for g in range(per):
        f = step * per + g
        ch, cl = two(coupling[0, g])
        main = dot(wide, ch, NN)
        value = main[:rhs] + main[rhs:] + dot(ph, cl, NN)
        slot = slots[0, f]
        live = f < count[0]

        @pl.when(live & (slot < half))
        def _():
            keep[slot] = value

        @pl.when(live & (slot >= half))
        def _():
            send[slot - half] = value


def near_kernel(offsets, first, extended, mleft, blocks, out, back):
    step = pl.program_id(0)
    per, slots = blocks.shape[:2]

    @pl.when(step == 0)
    def _():
        back[...] = jnp.zeros_like(back)

    for g in range(per):
        c = step * per + g
        xl = mleft[c]
        total = jnp.zeros((xl.shape[0], B), F32)
        for s in range(slots):
            place = offsets[c, s] - first[0]
            block = blocks[g, s]
            total = total + dot(extended[place], block, NT)
            back[place] += dot(xl, block, NN)
        out[c] = total


def forward_kernel(count, slots, gathered, coupling, out):
    step = pl.program_id(0)
    per = coupling.shape[1]

    @pl.when(step == 0)
    def _():
        out[...] = jnp.zeros_like(out)

    total = jnp.zeros_like(out)
    for g in range(per):
        f = step * per + g
        ch, cl = two(coupling[0, g])
        value = gathered[slots[0, f]]
        part = dot(
            jnp.concatenate([value, value], axis=1), jnp.concatenate([ch, cl], axis=1), NT
        )
        total = total + jnp.where(f < count[0], part, 0.0)
    out[...] += total


def down_kernel(
    points,
    far_right,
    far_left,
    slabs,
    apex_row,
    apex_column,
    lift,
    transfer,
    basis,
    near_out,
    near_back,
    from_prev,
    from_next,
    product,
    adjoint,
):
    rhs = far_right.shape[0]
    clusters = basis.shape[0]
    top_right = jnp.zeros((rhs, B), F32)
    top_left = jnp.zeros((rhs, B), F32)
    for t in range(3):
        top_right = top_right + dot3(slabs[2 * t], apex_row[t], NT)
        top_left = top_left + dot3(slabs[2 * t + 1], apex_column[t], NN)
    hats = jnp.concatenate([far_right[...], far_left[...]], axis=0) + dot3(
        jnp.concatenate([top_right, top_left], axis=0), lift[0], NT
    )
    hh, hl = two(hats)
    hat3 = jnp.concatenate([hh, hl, hh], axis=1)
    lane = lax.broadcasted_iota(jnp.int32, (rhs, B), 1)
    for c in range(clusters):
        th, tl = two(transfer[c])
        down = dot(hat3, jnp.concatenate([th, th, tl], axis=1), NT)
        dh, dl = two(down)
        far = dot(
            jnp.concatenate([dh, dl], axis=1),
            jnp.concatenate([basis[c], basis[c]], axis=0),
            NN,
        )
        mask = lane < points[c]
        back = near_back[HW + c]
        if c < HW:
            back = back + from_prev[c].astype(F32)
        if c >= clusters - HW:
            back = back + from_next[c - clusters + HW].astype(F32)
        product[:, c * B : (c + 1) * B] = jnp.where(mask, near_out[c] + far[:rhs], 0.0)
        adjoint[:, c * B : (c + 1) * B] = jnp.where(mask, back + far[rhs:], 0.0)


SMEM = pl.BlockSpec(memory_space=pltpu.SMEM)
VMEM = pl.BlockSpec(memory_space=pltpu.VMEM)
PARAMS = pltpu.CompilerParams(vmem_limit_bytes=48 * 1024 * 1024)


def shape(dims, kind):
    return jax.ShapeDtypeStruct(dims, kind)


def cost(flops, nbytes):
    return pl.CostEstimate(flops=int(flops), bytes_accessed=int(nbytes), transcendentals=0)


def shards(
    right_sides,
    left_sides,
    near_blocks,
    near_columns,
    cluster_points,
    leaf_basis,
    transfer,
    far_parents,
    far_count,
    coupling,
    slab_transfer,
    apex_coupling,
):
    rhs = right_sides.shape[0]
    clusters, near_slots = near_blocks.shape[:2]
    far_slots = coupling.shape[1]
    me = lax.axis_index(AXES)
    slab = lax.axis_index("slab")
    devices = lax.axis_size(AXES)
    block = (rhs, B)

    mright, mleft, pright, pleft, shares = pl.pallas_call(
        up_kernel,
        out_shape=(
            shape((clusters, *block), BF),
            shape((clusters, *block), BF),
            shape(block, BF),
            shape(block, F32),
            shape((2 * rhs, B), F32),
        ),
        in_specs=[SMEM] + [VMEM] * 5,
        out_specs=(VMEM,) * 5,
        compiler_params=PARAMS,
        cost_estimate=cost(2e8, 3e6),
        name="up",
    )(cluster_points, right_sides, left_sides, leaf_basis, transfer, slab_transfer)

    before = passed_along(mright[clusters - HW :], 1)
    after = passed_along(mright[:HW], -1)

    gathered = pright[None]
    for mask in GATHER_ORDER:
        gathered = jnp.concatenate([gathered, swapped(gathered, mask)], axis=0)

    difference = far_parents ^ me
    per = 16
    keep, send = pl.pallas_call(
        outward_kernel,
        grid=(far_slots // per,),
        out_shape=(shape((devices // 2, *block), F32),) * 2,
        in_specs=[
            SMEM,
            SMEM,
            pl.BlockSpec(block, lambda i: (0, 0)),
            pl.BlockSpec((1, per, B, B), lambda i: (0, i, 0, 0)),
        ],
        out_specs=(pl.BlockSpec((devices // 2, *block), lambda i: (0, 0, 0)),) * 2,
        compiler_params=PARAMS,
        cost_estimate=cost(3e8, 7e6),
        name="outward",
    )(far_count, slot_of(difference, REDUCE_ORDER, True), pleft, coupling)
    sums = shares.reshape(2, *block)
    partial = keep + swapped(send, CORE)
    sums = sums + swapped(sums, CORE)
    others = []
    for step, mask in enumerate(REDUCE_ORDER[1:]):
        n = partial.shape[0] // 2
        going = partial[n:]
        parts = [going.astype(BF)] if step < 2 else list(two_outside(going))
        sent = jnp.concatenate([sums, *others], axis=0) if mask == X3 else sums
        parts += list(two_outside(sent))
        came = swapped(jnp.concatenate(parts, axis=0), mask).astype(F32)
        if step < 2:
            partial = partial[:n] + came[:n]
        else:
            partial = partial[:n] + (came[:n] + came[n : 2 * n])
            n = 2 * n
        m = sent.shape[0]
        came_sums = came[n : n + m] + came[n + m : n + 2 * m]
        if mask in (X1, X3):
            others.append(came_sums)
        else:
            sums = sums + came_sums
    far_left = partial[0]
    slabs = jnp.concatenate(others, axis=0)

    extended = jnp.concatenate([before, mright, after], axis=0)
    per = 4
    near_out, near_back = pl.pallas_call(
        near_kernel,
        grid=(clusters // per,),
        out_shape=(
            shape((clusters, *block), F32),
            shape((clusters + 2 * HW, *block), F32),
        ),
        in_specs=[
            SMEM,
            SMEM,
            pl.BlockSpec((clusters + 2 * HW, *block), lambda i: (0, 0, 0)),
            pl.BlockSpec((clusters, *block), lambda i: (0, 0, 0)),
            pl.BlockSpec((per, near_slots, B, B), lambda i: (i, 0, 0, 0)),
        ],
        out_specs=(
            pl.BlockSpec((clusters, *block), lambda i: (0, 0, 0)),
            pl.BlockSpec((clusters + 2 * HW, *block), lambda i: (0, 0, 0)),
        ),
        compiler_params=PARAMS,
        cost_estimate=cost(6e8, 9e6),
        name="near",
    )(near_columns, (me * clusters - HW)[None], extended, mleft, near_blocks)
    from_next = passed_along(near_back[:HW].astype(BF), -1)
    from_prev = passed_along(near_back[clusters + HW :].astype(BF), 1)

    per = 16
    far_right = pl.pallas_call(
        forward_kernel,
        grid=(far_slots // per,),
        out_shape=shape(block, F32),
        in_specs=[
            SMEM,
            SMEM,
            pl.BlockSpec((devices, *block), lambda i: (0, 0, 0)),
            pl.BlockSpec((1, per, B, B), lambda i: (0, i, 0, 0)),
        ],
        out_specs=pl.BlockSpec(block, lambda i: (0, 0)),
        compiler_params=PARAMS,
        cost_estimate=cost(3e8, 7e6),
        name="forward",
    )(far_count, slot_of(difference, GATHER_ORDER, False), gathered, coupling)

    order = slab ^ jnp.array([1, 3, 2], jnp.int32)
    apex_row = jnp.take(lax.dynamic_index_in_dim(apex_coupling, slab, 0, False), order, axis=0)
    apex_column = jnp.take(lax.dynamic_index_in_dim(apex_coupling, slab, 1, False), order, axis=0)
    return pl.pallas_call(
        down_kernel,
        out_shape=(shape((rhs, clusters * B), F32),) * 2,
        in_specs=[SMEM] + [VMEM] * 12,
        out_specs=(VMEM,) * 2,
        compiler_params=PARAMS,
        cost_estimate=cost(4e8, 5e6),
        name="down",
    )(
        cluster_points,
        far_right,
        far_left,
        slabs,
        apex_row,
        apex_column,
        slab_transfer,
        transfer,
        leaf_basis,
        near_out,
        near_back,
        from_prev,
        from_next,
    )


def solution(mesh):
    return jax.shard_map(
        shards,
        mesh=mesh,
        in_specs=(
            P(None, AXES),
            P(None, AXES),
            P(AXES, None, None, None),
            P(AXES, None),
            P(AXES),
            P(AXES, None, None),
            P(AXES, None, None),
            P(AXES, None),
            P(AXES),
            P(AXES, None, None, None),
            P(AXES, None, None),
            P(),
        ),
        out_specs=(P(None, AXES), P(None, AXES)),
        check_vma=False,
    )
```

```python
import functools

import jax
import jax.numpy as jnp
from jax import lax
from jax.experimental import pallas as pl
from jax.experimental.pallas import tpu as pltpu
from jax.sharding import PartitionSpec as P

B = 128
HW = 4
AXES = ("slab", "leaf")
BF = jnp.bfloat16
F32 = jnp.float32

CORE, Z1, Z3, Y1, Y3, X1, X3 = 1, 2, 6, 8, 24, 32, 96
REDUCE_ORDER = (CORE, Y1, Y3, Z1, Z3, X1, X3)
GATHER_ORDER = (X1, X3, Z3, Z1, Y1, Y3, CORE)


def swapped(block, mask):
    route = [(i, i ^ mask) for i in range(lax.axis_size(AXES))]
    return lax.ppermute(block, AXES, route)


def passed_along(block, distance):
    devices = range(lax.axis_size(AXES))
    route = [(i - distance, i) for i in devices if i - distance in devices]
    return lax.ppermute(block, AXES, route)


def slot_of(difference, order, first_is_high):
    slot = jnp.zeros_like(difference)
    for step, mask in enumerate(order):
        if mask == CORE:
            bit = difference & 1
        else:
            shift = {Z1: 1, Z3: 1, Y1: 3, Y3: 3, X1: 5, X3: 5}[mask]
            low, high = (difference >> shift) & 1, (difference >> (shift + 1)) & 1
            bit = high if mask in (Z3, Y3, X3) else low ^ high
        place = len(order) - 1 - step if first_is_high else step
        slot = slot | (bit << place)
    return slot


def two(value):
    high = value.astype(BF)
    return high, (value - high.astype(F32)).astype(BF)


NN = (((1,), (0,)), ((), ()))
NT = (((1,), (1,)), ((), ()))


def dot(a, b, how):
    return lax.dot_general(a, b, how, preferred_element_type=F32)


def dot3(a, b, how):
    (ah, al), (bh, bl) = two(a), two(b)
    left = jnp.concatenate([ah, al, ah], axis=1)
    right = jnp.concatenate([bh, bh, bl], axis=1 if how is NT else 0)
    return dot(left, right, how)


def stacked(value):
    high, low = two(value)
    upper = jnp.concatenate([high, high], axis=1)
    return jnp.concatenate([upper, jnp.concatenate([low, jnp.zeros_like(low)], axis=1)], axis=0)


def both(value):
    half = value.shape[0] // 2
    return value[:half] + value[half:]


def diagonal(a, b):
    upper = jnp.concatenate([a, jnp.zeros_like(a)], axis=1)
    return jnp.concatenate([upper, jnp.concatenate([jnp.zeros_like(b), b], axis=1)], axis=0)


def pair_mask(points, c, rows):
    lane = lax.broadcasted_iota(jnp.int32, (rows, 2 * B), 1)
    return lane < jnp.where(lane < B, points[c], B + points[c + 1])


def up_kernel(
    points, right, left, basis, transfer, lift, mright, mleft, pright, pleft, shares, total
):
    step = pl.program_id(0)
    per = basis.shape[0]
    rhs = right.shape[0]
    part = jnp.zeros((4 * rhs, B), F32)
    for g in range(0, per, 2):
        mask = pair_mask(points, step * per + g, rhs)
        columns = slice(g * B, (g + 2) * B)
        xr = jnp.where(mask, right[:, columns].astype(F32), 0.0).astype(BF)
        xl = jnp.where(mask, left[:, columns].astype(F32), 0.0).astype(BF)
        for q in range(2):
            mright[g + q] = xr[:, q * B : (q + 1) * B]
            mleft[g + q] = xl[:, q * B : (q + 1) * B]
        leaf = dot(jnp.concatenate([xr, xl], axis=0), diagonal(basis[g], basis[g + 1]), NT)
        high, low = two(jnp.concatenate([transfer[g], transfer[g + 1]], axis=0))
        part = part + dot(stacked(leaf), jnp.concatenate([high, low], axis=0), NN)
    part = both(part)

    @pl.when(step == 0)
    def _():
        total[...] = part

    @pl.when(step > 0)
    def _():
        total[...] += part

    @pl.when(step == pl.num_programs(0) - 1)
    def _():
        pright[0] = total[:rhs].astype(BF)
        pleft[...] = total[rhs:]
        shares[...] = dot3(total[...], lift[0], NN)


def outward_kernel(count, slots, pleft, shares, coupling, keep, send, sums):
    step = pl.program_id(0)
    per = coupling.shape[1]
    rhs = pleft.shape[0]
    half = keep.shape[0] - 1

    @pl.when(step == 0)
    def _():
        keep[...] = jnp.zeros_like(keep)
        send[...] = jnp.zeros_like(send)
        for q in range(2):
            value = shares[q * rhs : (q + 1) * rhs]
            send[half + 1 + q] = value
            sums[q] = value

    wide = stacked(pleft[...])
    group = 8
    for start in range(0, per, group):
        values = []
        for g in range(start, start + group, 2):
            (ah, al), (bh, bl) = two(coupling[0, g]), two(coupling[0, g + 1])
            high, low = (jnp.concatenate(pair, axis=1) for pair in ((ah, bh), (al, bl)))
            value = both(dot(wide, jnp.concatenate([high, low], axis=0), NN))
            values += [value[:, :B], value[:, B:]]
        for q, value in enumerate(values):
            f = step * per + start + q
            slot = jnp.where(f < count[0], slots[0, f], half)
            other = jnp.where(f < count[0], slots[0, f] - half, -1)
            keep[jnp.minimum(slot, half)] = value
            send[jnp.where(other >= 0, other, half)] = value


def fold_kernel(exact, exact_next, add, came, partial, sums, payload, keep, sums_next):
    n = 2 * keep.shape[0]
    m = sums.shape[0]
    if came.dtype == F32:
        total = partial[:n] + came[:n]
        got = came[n + 1 : n + 1 + m]
    else:
        total = partial[...] + came[:n].astype(F32)
        start = n
        if exact:
            total = total + came[n : 2 * n].astype(F32)
            start = 2 * n
        got = came[start : start + m].astype(F32) + came[start + m : start + 2 * m].astype(F32)
    if add:
        sums_next[...] = sums[...] + got
    else:
        sums_next[:m] = sums[...]
        sums_next[m:] = got
    keep[...] = total[: n // 2]
    high, low = two(total[n // 2 :])
    place = n // 2
    payload[:place] = high
    if exact_next:
        payload[place : 2 * place] = low
        place = 2 * place
    high, low = two(sums_next[...])
    k = high.shape[0]
    payload[place : place + k] = high
    payload[place + k :] = low


def grow_kernel(gathered, came, out):
    n = gathered.shape[0]
    out[:n] = gathered[...]
    out[n:] = came[...]


def near_kernel(columns, first, mright, mleft, blocks, out, back, to_prev, to_next):
    step = pl.program_id(0)
    per, slots = blocks.shape[:2]
    clusters, rhs = mright.shape[:2]

    @pl.when(step == 0)
    def _():
        back[...] = jnp.zeros_like(back)

    group = 4
    for start in range(0, per, group):
        done = []
        for g in range(start, start + group):
            c = step * per + g
            row = jnp.concatenate([blocks[g, s] for s in range(slots)], axis=1)
            places = [columns[s, c] - first[0] for s in range(slots)]
            inside = []
            for place in places:
                own = place - HW
                value = mright[jnp.clip(own, 0, clusters - 1)]
                is_own = (own >= 0) & (own < clusters)
                inside.append(jnp.where(is_own, value, jnp.zeros_like(value)))
            out[c] = dot(row, jnp.concatenate(inside, axis=1), NT).T
            done.append((places, dot(mleft[c], row, NN)))
        for places, value in done:
            held = [back[place] for place in places]
            for s, place in enumerate(places):
                back[place] = held[s] + value[:, s * B : (s + 1) * B]

    @pl.when(step == pl.num_programs(0) - 1)
    def _():
        to_prev[:HW] = mright[:HW]
        to_prev[HW:] = back[:HW].astype(BF)
        to_next[:HW] = mright[clusters - HW :]
        to_next[HW:] = back[clusters + HW :].astype(BF)


def edge_kernel(columns, first, from_prev, from_next, low_blocks, high_blocks, out):
    slots = low_blocks.shape[1]
    clusters = columns.shape[1]
    for g in range(2 * HW):
        low = g < HW
        c = g if low else clusters - 2 * HW + g
        blocks, halo = (low_blocks, from_prev) if low else (high_blocks, from_next)
        row = jnp.concatenate([blocks[g % HW, s] for s in range(slots)], axis=1)
        values = []
        for s in range(slots):
            place = columns[s, c] - first[0]
            place = place if low else place - (clusters + HW)
            value = halo[jnp.clip(place, 0, HW - 1)]
            is_there = (place >= 0) & (place < HW)
            values.append(jnp.where(is_there, value, jnp.zeros_like(value)))
        out[g] = dot(row, jnp.concatenate(values, axis=1), NT).T


def forward_kernel(count, slots, own, came, coupling, out, total):
    step = pl.program_id(0)
    per = coupling.shape[1]
    half = own.shape[0]
    rows, values = [], []
    for g in range(per):
        f = step * per + g
        slot = slots[0, f]
        a = own[jnp.minimum(slot, half - 1)]
        b = came[jnp.maximum(slot - half, 0)]
        value = jnp.where(slot < half, a, b)
        value = jnp.where(f < count[0], value, jnp.zeros_like(value))
        values += [value, value]
        rows += two(coupling[0, g])
    part = dot(jnp.concatenate(rows, axis=1), jnp.concatenate(values, axis=1), NT)

    @pl.when(step == 0)
    def _():
        total[...] = part

    @pl.when(step > 0)
    def _():
        total[...] += part

    @pl.when(step == pl.num_programs(0) - 1)
    def _():
        out[...] = total[...].T


def down_kernel(
    points,
    place,
    far_right,
    partial,
    sums,
    came,
    apex,
    lift,
    transfer,
    basis,
    near_out,
    near_back,
    edge_out,
    from_prev,
    from_next,
    product,
    adjoint,
    hats,
):
    step = pl.program_id(0)
    per = basis.shape[0]
    clusters, rhs = near_out.shape[:2]

    @pl.when(step == 0)
    def _():
        slab = place[0]
        got = came[2:6].astype(F32) + came[6:10].astype(F32)
        slabs = [sums[2], sums[3], got[0], got[1], got[2], got[3]]
        top_right = jnp.zeros((rhs, B), F32)
        top_left = jnp.zeros((rhs, B), F32)
        for t, mask in enumerate((1, 3, 2)):
            top_right = top_right + dot3(slabs[2 * t], apex[slab, slab ^ mask], NT)
            top_left = top_left + dot3(slabs[2 * t + 1], apex[slab ^ mask, slab], NN)
        far_left = partial[0] + (came[0].astype(F32) + came[1].astype(F32))
        hats[...] = stacked(
            jnp.concatenate([far_right[...], far_left], axis=0)
            + dot3(jnp.concatenate([top_right, top_left], axis=0), lift[0], NT)
        )

    for g in range(0, per, 2):
        c = step * per + g
        high, low = two(jnp.concatenate([transfer[g], transfer[g + 1]], axis=0))
        down = both(dot(hats[...], jnp.concatenate([high, low], axis=1), NT))
        high, low = two(down)
        two_bases = diagonal(basis[g], basis[g + 1])
        far = dot(
            jnp.concatenate([high, low], axis=1),
            jnp.concatenate([two_bases, two_bases], axis=0),
            NN,
        )
        mask = pair_mask(points, c, rhs)
        columns = slice(g * B, (g + 2) * B)
        near = jnp.concatenate([near_out[c], near_out[c + 1]], axis=1)
        back = jnp.concatenate([near_back[HW + c], near_back[HW + c + 1]], axis=1)
        product[:, columns] = jnp.where(mask, near + far[:rhs], 0.0)
        adjoint[:, columns] = jnp.where(mask, back + far[rhs:], 0.0)

    def edge(g, c, halo):
        mask = lax.broadcasted_iota(jnp.int32, (rhs, B), 1) < points[c]
        columns = slice((c % per) * B, (c % per + 1) * B)
        product[:, columns] += jnp.where(mask, edge_out[g], 0.0)
        adjoint[:, columns] += jnp.where(mask, halo[HW + g % HW].astype(F32), 0.0)

    @pl.when(step == 0)
    def _():
        for g in range(HW):
            edge(g, g, from_prev)

    @pl.when(step == pl.num_programs(0) - 1)
    def _():
        for g in range(HW):
            edge(HW + g, clusters - HW + g, from_next)


SMEM = pl.BlockSpec(memory_space=pltpu.SMEM)
VMEM = pl.BlockSpec(memory_space=pltpu.VMEM)
MIB = 1024 * 1024


def shape(dims, kind):
    return jax.ShapeDtypeStruct(dims, kind)


def whole(*dims):
    return pl.BlockSpec(dims, lambda *_: (0,) * len(dims))


def call(kernel, name, grid, ins, outs, args, us, scratch=(), vmem=20):
    results = pl.pallas_call(
        kernel,
        grid=grid,
        out_shape=tuple(shape(dims, kind) for _, dims, kind in outs),
        in_specs=ins,
        out_specs=tuple(spec for spec, _, _ in outs),
        scratch_shapes=list(scratch),
        compiler_params=pltpu.CompilerParams(vmem_limit_bytes=vmem * MIB),
        cost_estimate=pl.CostEstimate(
            flops=1000, bytes_accessed=int(us * 3.6e6), transcendentals=0
        ),
        name=name,
    )(*args)
    return results


def shards(
    right_sides,
    left_sides,
    near_blocks,
    near_columns,
    cluster_points,
    leaf_basis,
    transfer,
    far_parents,
    far_count,
    coupling,
    slab_transfer,
    apex_coupling,
):
    rhs = right_sides.shape[0]
    clusters, near_slots = near_blocks.shape[:2]
    far_slots = coupling.shape[1]
    rank = leaf_basis.shape[1]
    me = lax.axis_index(AXES)
    slab = lax.axis_index("slab")
    devices = lax.axis_size(AXES)
    block = (rhs, B)
    all_clusters = (clusters, *block)
    half = devices // 2

    per = 16
    sides = pl.BlockSpec((rhs, per * B), lambda i: (0, i))
    bases = pl.BlockSpec((per, rank, B), lambda i: (i, 0, 0))
    some_clusters = pl.BlockSpec((per, *block), lambda i: (i, 0, 0))
    mright, mleft, pright, pleft, shares = call(
        up_kernel,
        "up",
        (clusters // per,),
        [SMEM, sides, sides, bases, bases, whole(1, B, B)],
        [
            (some_clusters, all_clusters, BF),
            (some_clusters, all_clusters, BF),
            (whole(1, *block), (1, *block), BF),
            (whole(*block), block, F32),
            (whole(2 * rhs, B), (2 * rhs, B), F32),
        ],
        (cluster_points, right_sides, left_sides, leaf_basis, transfer, slab_transfer),
        us=3,
        scratch=[pltpu.VMEM((2 * rhs, B), F32)],
        vmem=60,
    )

    difference = far_parents ^ me
    reduce_slots = slot_of(difference, REDUCE_ORDER, True)
    gather_slots = slot_of(difference, GATHER_ORDER, False)

    gathered = pright
    for mask in GATHER_ORDER[:-1]:
        came = swapped(gathered, mask)
        n = gathered.shape[0]
        dims = (2 * n, *block)
        (gathered,) = call(
            grow_kernel, "grow", (), [VMEM] * 2, [(VMEM, dims, BF)], (gathered, came), us=0.6
        )
    gathered_came = swapped(gathered, CORE)

    per = 48
    couplings = pl.BlockSpec((1, per, B, B), lambda i: (0, i, 0, 0))
    partial, sent, sums = call(
        outward_kernel,
        "outward",
        (far_slots // per,),
        [SMEM, SMEM, whole(*block), whole(2 * rhs, B), couplings],
        [
            (whole(half + 1, *block), (half + 1, *block), F32),
            (whole(half + 3, *block), (half + 3, *block), F32),
            (whole(2, *block), (2, *block), F32),
        ],
        (far_count, reduce_slots, pleft, shares, coupling),
        us=5,
    )
    came = swapped(sent, CORE)
    n = half
    for step, mask in enumerate(REDUCE_ORDER[1:]):
        exact_next = step >= 2
        add = REDUCE_ORDER[step] not in (X1, X3)
        m = 2 if add else 4
        rows = n // 2 * (2 if exact_next else 1) + 2 * m
        payload, partial, sums = call(
            functools.partial(fold_kernel, step >= 3, exact_next, add),
            "fold",
            (),
            [VMEM] * 3,
            [
                (VMEM, (rows, *block), BF),
                (VMEM, (n // 2, *block), F32),
                (VMEM, (m, *block), F32),
            ],
            (came, partial, sums),
            us=0.8,
        )
        came = swapped(payload, mask)
        n = n // 2

    columns = near_columns.T
    first = (me * clusters - HW)[None]
    per = 16
    halo = (2 * HW, *block)
    near_out, near_back, to_prev, to_next = call(
        near_kernel,
        "near",
        (clusters // per,),
        [
            SMEM,
            SMEM,
            whole(*all_clusters),
            whole(*all_clusters),
            pl.BlockSpec((per, near_slots, B, B), lambda i: (i, 0, 0, 0)),
        ],
        [
            (whole(*all_clusters), all_clusters, F32),
            (whole(clusters + 2 * HW, *block), (clusters + 2 * HW, *block), F32),
            (whole(*halo), halo, BF),
            (whole(*halo), halo, BF),
        ],
        (columns, first, mright, mleft, near_blocks),
        us=7,
    )
    from_next = passed_along(to_prev, -1)
    from_prev = passed_along(to_next, 1)
    last = clusters // HW - 1
    (edge_out,) = call(
        edge_kernel,
        "edge",
        (1,),
        [
            SMEM,
            SMEM,
            whole(*halo),
            whole(*halo),
            pl.BlockSpec((HW, near_slots, B, B), lambda i: (0, 0, 0, 0)),
            pl.BlockSpec((HW, near_slots, B, B), lambda i: (last, 0, 0, 0)),
        ],
        [(whole(*halo), halo, F32)],
        (columns, first, from_prev, from_next, near_blocks, near_blocks),
        us=2.5,
    )

    per = 48
    (far_right,) = call(
        forward_kernel,
        "forward",
        (far_slots // per,),
        [SMEM, SMEM, whole(half, *block), whole(half, *block), couplings],
        [(whole(*block), block, F32)],
        (far_count, gather_slots, gathered, gathered_came, coupling),
        us=5,
        scratch=[pltpu.VMEM((B, rhs), F32)],
    )

    per = 16
    sides = pl.BlockSpec((rhs, per * B), lambda i: (0, i))
    return call(
        down_kernel,
        "down",
        (clusters // per,),
        [
            SMEM,
            SMEM,
            whole(*block),
            whole(1, *block),
            whole(4, *block),
            whole(10, *block),
            whole(*apex_coupling.shape),
            whole(1, B, B),
            bases,
            bases,
            whole(*all_clusters),
            whole(clusters + 2 * HW, *block),
            whole(*halo),
            whole(*halo),
            whole(*halo),
        ],
        [(sides, (rhs, clusters * B), F32)] * 2,
        (
            cluster_points,
            slab[None],
            far_right,
            partial,
            sums,
            came,
            apex_coupling,
            slab_transfer,
            transfer,
            leaf_basis,
            near_out,
            near_back,
            edge_out,
            from_prev,
            from_next,
        ),
        us=4,
        scratch=[pltpu.VMEM((4 * rhs, 2 * B), BF)],
    )


def solution(mesh):
    return jax.shard_map(
        shards,
        mesh=mesh,
        in_specs=(
            P(None, AXES),
            P(None, AXES),
            P(AXES, None, None, None),
            P(AXES, None),
            P(AXES),
            P(AXES, None, None),
            P(AXES, None, None),
            P(AXES, None),
            P(AXES),
            P(AXES, None, None, None),
            P(AXES, None, None),
            P(),
        ),
        out_specs=(P(None, AXES), P(None, AXES)),
        check_vma=False,
    )
```

```python
import functools

import jax
import jax.numpy as jnp
import numpy as np
from jax import lax
from jax.experimental import pallas as pl
from jax.experimental.pallas import tpu as pltpu
from jax.sharding import PartitionSpec as P

B = 128
HW = 4
AXES = ("slab", "leaf")
BF = jnp.bfloat16
F32 = jnp.float32

Z, Y, X = 1, 3, 5
STEPS = ((Y, 0), (Y, 1), (Z, 0), (Z, 1), (X, 0), (X, 1))


def routed(block, step):
    axis, turn = step
    route = []
    for i in range(lax.axis_size(AXES)):
        pairing = 1 if (i & 1) == turn else 3
        route.append((i, i ^ (pairing << axis)))
    return lax.ppermute(block, AXES, route)


def to_other_core(block):
    return lax.ppermute(block, AXES, [(i, i ^ 1) for i in range(lax.axis_size(AXES))])


def passed_along(block, distance):
    devices = range(lax.axis_size(AXES))
    route = [(i - distance, i) for i in devices if i - distance in devices]
    return lax.ppermute(block, AXES, route)


def slot_tables(devices):
    reduce = np.zeros((2, devices), np.int32)
    gather = np.zeros((2, devices), np.int32)
    for core in range(2):
        for difference in range(devices):
            other = difference & 1
            for place, (axis, turn) in enumerate(STEPS):
                low, high = (difference >> axis) & 1, (difference >> (axis + 1)) & 1
                by_one = turn == core ^ other
                bit = low ^ high if by_one else high
                reduce[core, difference] |= bit << (len(STEPS) - 1 - place)
                gather[core, difference] |= bit << place
            reduce[core, difference] |= other << len(STEPS)
            gather[core, difference] |= other << len(STEPS)
    return reduce.reshape(-1), gather.reshape(-1)


def slot_in(table, parents, f, me, devices):
    return table[(me & 1) * devices + (parents[0, f] ^ me)]


def two(value):
    high = value.astype(BF)
    return high, (value - high.astype(F32)).astype(BF)


NN = (((1,), (0,)), ((), ()))
NT = (((1,), (1,)), ((), ()))


def dot(a, b, how):
    return lax.dot_general(a, b, how, preferred_element_type=F32)


def dot3(a, b, how):
    (ah, al), (bh, bl) = two(a), two(b)
    left = jnp.concatenate([ah, al, ah], axis=1)
    right = jnp.concatenate([bh, bh, bl], axis=1 if how is NT else 0)
    return dot(left, right, how)


def stacked(value):
    high, low = two(value)
    upper = jnp.concatenate([high, high], axis=1)
    return jnp.concatenate([upper, jnp.concatenate([low, jnp.zeros_like(low)], axis=1)], axis=0)


def both(value):
    half = value.shape[0] // 2
    return value[:half] + value[half:]


def diagonal(a, b):
    upper = jnp.concatenate([a, jnp.zeros_like(a)], axis=1)
    return jnp.concatenate([upper, jnp.concatenate([jnp.zeros_like(b), b], axis=1)], axis=0)


def pair_mask(points, c, rows):
    lane = lax.broadcasted_iota(jnp.int32, (rows, 2 * B), 1)
    return lane < jnp.where(lane < B, points[c], B + points[c + 1])


def rise_kernel(
    place,
    count,
    points_hbm,
    parents_hbm,
    table_hbm,
    right_hbm,
    left_hbm,
    basis_hbm,
    transfer_hbm,
    lift_hbm,
    coupling_hbm,
    mright,
    mleft,
    pright,
    keep,
    send,
    sums,
    points,
    parents,
    table,
    right,
    left,
    basis,
    transfer,
    lift,
    coupling,
    done,
):
    rhs = right.shape[0]
    clusters = basis.shape[0]
    far_slots = coupling.shape[1]
    half = keep.shape[0] - 1
    pieces, far_pieces = 2, 4
    count_of = iter(range(done.shape[0]))

    def fetch(source, target, index):
        return pltpu.make_async_copy(source.at[index], target.at[index], done.at[next(count_of)])

    per = clusters // pieces
    early = []
    for j in range(pieces):
        some = pl.ds(j * per, per)
        columns = (slice(None), pl.ds(j * per * B, per * B))
        early.append(
            [
                fetch(right_hbm, right, columns),
                fetch(left_hbm, left, columns),
                fetch(basis_hbm, basis, some),
                fetch(transfer_hbm, transfer, some),
            ]
        )
    early[0].append(fetch(points_hbm, points, slice(None)))
    early[1].append(fetch(parents_hbm, parents, slice(None)))
    early[1].append(fetch(table_hbm, table, slice(None)))
    early[1].append(fetch(lift_hbm, lift, slice(None)))
    far_per = far_slots // far_pieces
    late = [
        fetch(coupling_hbm, coupling, (slice(None), pl.ds(j * far_per, far_per)))
        for j in range(far_pieces)
    ]
    for copy in [*early[0], *early[1]]:
        copy.start()
    keep[...] = jnp.zeros_like(keep)
    send[...] = jnp.zeros_like(send)

    part = jnp.zeros((4 * rhs, B), F32)
    for j in range(pieces):
        for copy in early[j]:
            copy.wait()
        if j == 0:
            for copy in late:
                copy.start()
        for c in range(j * per, (j + 1) * per, 2):
            mask = pair_mask(points, c, rhs)
            columns = slice(c * B, (c + 2) * B)
            xr = jnp.where(mask, right[:, columns].astype(F32), 0.0).astype(BF)
            xl = jnp.where(mask, left[:, columns].astype(F32), 0.0).astype(BF)
            for q in range(2):
                mright[c + q] = xr[:, q * B : (q + 1) * B]
                mleft[c + q] = xl[:, q * B : (q + 1) * B]
            leaf = dot(jnp.concatenate([xr, xl], axis=0), diagonal(basis[c], basis[c + 1]), NT)
            high, low = two(jnp.concatenate([transfer[c], transfer[c + 1]], axis=0))
            part = part + dot(stacked(leaf), jnp.concatenate([high, low], axis=0), NN)
    total = both(part)
    pright[0] = total[:rhs].astype(BF)
    shares = dot3(total, lift[0], NN)
    for q in range(2):
        value = shares[q * rhs : (q + 1) * rhs]
        send[half + 1 + q] = value
        sums[q] = value

    wide = stacked(total[rhs:])
    me = place[0]
    group = 8
    for j in range(far_pieces):
        late[j].wait()
        for start in range(j * far_per, (j + 1) * far_per, group):
            values = []
            for f in range(start, start + group, 2):
                (ah, al), (bh, bl) = two(coupling[0, f]), two(coupling[0, f + 1])
                high, low = (jnp.concatenate(pair, axis=1) for pair in ((ah, bh), (al, bl)))
                value = both(dot(wide, jnp.concatenate([high, low], axis=0), NN))
                values += [value[:, :B], value[:, B:]]
            for q, value in enumerate(values):
                f = start + q
                slot = slot_in(table, parents, f, me, 2 * half)
                live = f < count[0]
                own = jnp.where(live & (slot < half), slot, half)
                other = jnp.where(live & (slot >= half), slot - half, half)
                keep[own] = value
                send[other] = value


def fold_kernel(exact, exact_next, add, cores, came, partial, sums, gathered, *rest):
    payload, keep, sums_next, gathered_next = rest[-4:]
    n = 2 * keep.shape[0]
    m = sums.shape[0]
    a = gathered.shape[0]
    if cores:
        total = partial[:n] + came[:n]
        got = came[n + 1 : n + 1 + m]
        gathered_next[...] = gathered[...]
    else:
        total = partial[...] + came[:n].astype(F32)
        start = n
        if exact:
            total = total + came[n : 2 * n].astype(F32)
            start = 2 * n
        got = came[start : start + m].astype(F32) + came[start + m : start + 2 * m].astype(F32)
        gathered_next[:a] = gathered[...]
        gathered_next[a:] = came[start + 2 * m :]
    if add:
        sums_next[...] = sums[...] + got
    else:
        sums_next[:m] = sums[...]
        sums_next[m:] = got
    keep[...] = total[: n // 2]
    high, low = two(total[n // 2 :])
    start = n // 2
    payload[:start] = high
    if exact_next:
        payload[start : 2 * start] = low
        start = 2 * start
    high, low = two(sums_next[...])
    k = high.shape[0]
    payload[start : start + k] = high
    payload[start + k : start + 2 * k] = low
    payload[start + 2 * k :] = gathered_next[...]


def tail_kernel(start, came, out):
    out[...] = came[start:]


def near_kernel(columns, first, mright, mleft, blocks, _, out, back, to_prev, to_next):
    step = pl.program_id(0)
    per, slots = blocks.shape[:2]
    clusters, rhs = mright.shape[:2]

    @pl.when(step == 0)
    def _():
        back[...] = jnp.zeros_like(back)

    group = 4
    for start in range(0, per, group):
        done = []
        for g in range(start, start + group):
            c = step * per + g
            row = jnp.concatenate([blocks[g, s] for s in range(slots)], axis=1)
            places = [columns[s, c] - first[0] for s in range(slots)]
            inside = []
            for place in places:
                own = place - HW
                value = mright[jnp.clip(own, 0, clusters - 1)]
                is_own = (own >= 0) & (own < clusters)
                inside.append(jnp.where(is_own, value, jnp.zeros_like(value)))
            out[c] = dot(row, jnp.concatenate(inside, axis=1), NT).T
            done.append((places, dot(mleft[c], row, NN)))
        for places, value in done:
            held = [back[place] for place in places]
            for s, place in enumerate(places):
                back[place] = held[s] + value[:, s * B : (s + 1) * B]

    @pl.when(step == pl.num_programs(0) - 1)
    def _():
        to_prev[:HW] = mright[:HW]
        to_prev[HW:] = back[:HW].astype(BF)
        to_next[:HW] = mright[clusters - HW :]
        to_next[HW:] = back[clusters + HW :].astype(BF)


def edge_kernel(columns, first, from_prev, from_next, low_blocks, high_blocks, out):
    slots = low_blocks.shape[1]
    clusters = columns.shape[1]
    for g in range(2 * HW):
        low = g < HW
        c = g if low else clusters - 2 * HW + g
        blocks, halo = (low_blocks, from_prev) if low else (high_blocks, from_next)
        row = jnp.concatenate([blocks[g % HW, s] for s in range(slots)], axis=1)
        values = []
        for s in range(slots):
            place = columns[s, c] - first[0]
            place = place if low else place - (clusters + HW)
            value = halo[jnp.clip(place, 0, HW - 1)]
            is_there = (place >= 0) & (place < HW)
            values.append(jnp.where(is_there, value, jnp.zeros_like(value)))
        out[g] = dot(row, jnp.concatenate(values, axis=1), NT).T


def forward_kernel(place, count, parents, table, own, came, own_other, other, coupling, out, all_of):
    far_slots = coupling.shape[1]
    quarter = own.shape[0]
    all_of[:quarter] = own[...]
    all_of[quarter : 2 * quarter] = came[came.shape[0] - quarter :]
    all_of[2 * quarter : 3 * quarter] = own_other[...]
    all_of[3 * quarter :] = other[...]
    me = place[0]
    total = jnp.zeros((B, own.shape[1]), F32)
    group = 48
    for start in range(0, far_slots, group):
        rows, values = [], []
        for f in range(start, start + group):
            value = all_of[slot_in(table, parents, f, me, 4 * quarter)]
            value = jnp.where(f < count[0], value, jnp.zeros_like(value))
            values += [value, value]
            rows += two(coupling[0, f])
        total = total + dot(
            jnp.concatenate(rows, axis=1), jnp.concatenate(values, axis=1), NT
        )
    out[...] = total.T


def down_kernel(
    points,
    place,
    far_right,
    partial,
    sums,
    came,
    apex,
    lift,
    transfer,
    basis,
    near_out,
    near_back,
    edge_out,
    from_prev,
    from_next,
    product,
    adjoint,
    hats,
):
    step = pl.program_id(0)
    per = basis.shape[0]
    clusters, rhs = near_out.shape[:2]

    @pl.when(step == 0)
    def _():
        core = place[0] & 1
        slab = place[0] >> X
        got = came[2:6].astype(F32) + came[6:10].astype(F32)
        slabs = [sums[2], sums[3], got[0], got[1], got[2], got[3]]
        top_right = jnp.zeros((rhs, B), F32)
        top_left = jnp.zeros((rhs, B), F32)
        for t, mask in enumerate((1 + 2 * core, 3 - 2 * core, 2)):
            top_right = top_right + dot3(slabs[2 * t], apex[slab, slab ^ mask], NT)
            top_left = top_left + dot3(slabs[2 * t + 1], apex[slab ^ mask, slab], NN)
        far_left = partial[0] + (came[0].astype(F32) + came[1].astype(F32))
        hats[...] = stacked(
            jnp.concatenate([far_right[...], far_left], axis=0)
            + dot3(jnp.concatenate([top_right, top_left], axis=0), lift[0], NT)
        )

    for g in range(0, per, 2):
        c = step * per + g
        high, low = two(jnp.concatenate([transfer[g], transfer[g + 1]], axis=0))
        down = both(dot(hats[...], jnp.concatenate([high, low], axis=1), NT))
        high, low = two(down)
        two_bases = diagonal(basis[g], basis[g + 1])
        far = dot(
            jnp.concatenate([high, low], axis=1),
            jnp.concatenate([two_bases, two_bases], axis=0),
            NN,
        )
        mask = pair_mask(points, c, rhs)
        columns = slice(g * B, (g + 2) * B)
        near = jnp.concatenate([near_out[c], near_out[c + 1]], axis=1)
        back = jnp.concatenate([near_back[HW + c], near_back[HW + c + 1]], axis=1)
        product[:, columns] = jnp.where(mask, near + far[:rhs], 0.0)
        adjoint[:, columns] = jnp.where(mask, back + far[rhs:], 0.0)

    def edge(g, c, halo):
        mask = lax.broadcasted_iota(jnp.int32, (rhs, B), 1) < points[c]
        columns = slice((c % per) * B, (c % per + 1) * B)
        product[:, columns] += jnp.where(mask, edge_out[g], 0.0)
        adjoint[:, columns] += jnp.where(mask, halo[HW + g % HW].astype(F32), 0.0)

    @pl.when(step == 0)
    def _():
        for g in range(HW):
            edge(g, g, from_prev)

    @pl.when(step == pl.num_programs(0) - 1)
    def _():
        for g in range(HW):
            edge(HW + g, clusters - HW + g, from_next)


SMEM = pl.BlockSpec(memory_space=pltpu.SMEM)
HBM = pl.BlockSpec(memory_space=pltpu.HBM)
ANY = pl.BlockSpec(memory_space=pl.ANY)
VMEM = pl.BlockSpec(memory_space=pltpu.VMEM)
MIB = 1024 * 1024


def shape(dims, kind):
    return jax.ShapeDtypeStruct(dims, kind)


def whole(*dims):
    return pl.BlockSpec(dims, lambda *_: (0,) * len(dims))


def call(kernel, name, grid, ins, outs, args, us, scratch=(), vmem=20):
    results = pl.pallas_call(
        kernel,
        grid=grid,
        out_shape=tuple(shape(dims, kind) for _, dims, kind in outs),
        in_specs=ins,
        out_specs=tuple(spec for spec, _, _ in outs),
        scratch_shapes=list(scratch),
        compiler_params=pltpu.CompilerParams(vmem_limit_bytes=vmem * MIB),
        cost_estimate=pl.CostEstimate(
            flops=1000, bytes_accessed=int(us * 3.6e6), transcendentals=0
        ),
        name=name,
    )(*args)
    return results


def shards(
    right_sides,
    left_sides,
    near_blocks,
    near_columns,
    cluster_points,
    leaf_basis,
    transfer,
    far_parents,
    far_count,
    coupling,
    slab_transfer,
    apex_coupling,
):
    rhs = right_sides.shape[0]
    clusters, near_slots = near_blocks.shape[:2]
    far_slots = coupling.shape[1]
    rank = leaf_basis.shape[1]
    me = lax.axis_index(AXES)
    devices = lax.axis_size(AXES)
    block = (rhs, B)
    all_clusters = (clusters, *block)
    half = devices // 2
    place = me.astype(jnp.int32)[None]
    reduce_table, gather_table = (jnp.asarray(table) for table in slot_tables(devices))

    mright, mleft, gathered, partial, sent, sums = call(
        rise_kernel,
        "rise",
        (),
        [SMEM] * 2 + [HBM] * 9,
        [
            (VMEM, all_clusters, BF),
            (VMEM, all_clusters, BF),
            (VMEM, (1, *block), BF),
            (VMEM, (half + 1, *block), F32),
            (VMEM, (half + 3, *block), F32),
            (VMEM, (2, *block), F32),
        ],
        (
            place,
            far_count,
            *(
                pltpu.with_memory_space_constraint(value, pltpu.HBM)
                for value in (
                    cluster_points,
                    far_parents,
                    reduce_table,
                    right_sides,
                    left_sides,
                    leaf_basis,
                    transfer,
                    slab_transfer,
                    coupling,
                )
            ),
        ),
        us=5,
        scratch=[
            pltpu.SMEM(cluster_points.shape, jnp.int32),
            pltpu.SMEM(far_parents.shape, jnp.int32),
            pltpu.SMEM(reduce_table.shape, jnp.int32),
            pltpu.VMEM(right_sides.shape, BF),
            pltpu.VMEM(left_sides.shape, BF),
            pltpu.VMEM(leaf_basis.shape, BF),
            pltpu.VMEM(transfer.shape, F32),
            pltpu.VMEM(slab_transfer.shape, F32),
            pltpu.VMEM(coupling.shape, F32),
            pltpu.SemaphoreType.DMA((16,)),
        ],
    )

    def fold(step, came, partial, sums, gathered, after=()):
        n = half >> step
        exact_next = step >= 2
        add = step == 0 or STEPS[step - 1][0] != X
        m = 2 if add else 4
        a = 1 << step
        rows = n // 2 * (2 if exact_next else 1) + 2 * m + a
        return call(
            functools.partial(fold_kernel, step >= 3, exact_next, add, step == 0),
            "fold",
            (),
            [VMEM] * 4 + [ANY] * len(after),
            [
                (VMEM, (rows, *block), BF),
                (VMEM, (n // 2, *block), F32),
                (VMEM, (m, *block), F32),
                (VMEM, (a, *block), BF),
            ],
            (came, partial, sums, gathered, *after),
            us=0.3,
        )

    came = to_other_core(sent)
    payload, partial, sums, gathered = fold(0, came, partial, sums, gathered)
    came = routed(payload, STEPS[0])

    columns = near_columns.T
    first = place * clusters - HW
    per = 16
    halo = (2 * HW, *block)
    near_out, near_back, to_prev, to_next = call(
        near_kernel,
        "near",
        (clusters // per,),
        [
            SMEM,
            SMEM,
            whole(*all_clusters),
            whole(*all_clusters),
            pl.BlockSpec((per, near_slots, B, B), lambda i: (i, 0, 0, 0)),
            ANY,
        ],
        [
            (whole(*all_clusters), all_clusters, F32),
            (whole(clusters + 2 * HW, *block), (clusters + 2 * HW, *block), F32),
            (whole(*halo), halo, BF),
            (whole(*halo), halo, BF),
        ],
        (columns, first, mright, mleft, near_blocks, payload),
        us=5,
    )
    payload, partial, sums, gathered = fold(1, came, partial, sums, gathered, (near_out,))
    came = routed(payload, STEPS[1])
    from_next = passed_along(to_prev, -1)
    from_prev = passed_along(to_next, 1)
    payload, partial, sums, gathered = fold(2, came, partial, sums, gathered)
    came = routed(payload, STEPS[2])
    payload, partial, sums, gathered = fold(3, came, partial, sums, gathered)
    came = routed(payload, STEPS[3])
    last = clusters // HW - 1
    (edge_out,) = call(
        edge_kernel,
        "edge",
        (1,),
        [
            SMEM,
            SMEM,
            whole(*halo),
            whole(*halo),
            pl.BlockSpec((HW, near_slots, B, B), lambda i: (0, 0, 0, 0)),
            pl.BlockSpec((HW, near_slots, B, B), lambda i: (last, 0, 0, 0)),
        ],
        [(whole(*halo), halo, F32)],
        (columns, first, from_prev, from_next, near_blocks, near_blocks),
        us=2,
    )
    payload, partial, sums, gathered = fold(4, came, partial, sums, gathered, (edge_out,))
    came = routed(payload, STEPS[4])
    payload, partial, sums, gathered = fold(5, came, partial, sums, gathered)
    came = routed(payload, STEPS[5])
    gathered_other = to_other_core(gathered)
    quarter = (half // 2, *block)
    (came_last,) = call(
        functools.partial(tail_kernel, 10),
        "tail",
        (),
        [VMEM],
        [(VMEM, quarter, BF)],
        (came,),
        us=0.3,
    )
    other = to_other_core(came_last)

    (far_right,) = call(
        forward_kernel,
        "forward",
        (),
        [SMEM] * 4 + [VMEM] * 5,
        [(VMEM, block, F32)],
        (
            place,
            far_count,
            far_parents,
            gather_table,
            gathered,
            came,
            gathered_other,
            other,
            coupling,
        ),
        us=3,
        scratch=[pltpu.VMEM((devices, *block), BF)],
    )

    per = 16
    sides = pl.BlockSpec((rhs, per * B), lambda i: (0, i))
    bases = pl.BlockSpec((per, rank, B), lambda i: (i, 0, 0))
    return call(
        down_kernel,
        "down",
        (clusters // per,),
        [
            SMEM,
            SMEM,
            whole(*block),
            whole(1, *block),
            whole(4, *block),
            whole(42, *block),
            whole(*apex_coupling.shape),
            whole(1, B, B),
            bases,
            bases,
            whole(*all_clusters),
            whole(clusters + 2 * HW, *block),
            whole(*halo),
            whole(*halo),
            whole(*halo),
        ],
        [(sides, (rhs, clusters * B), F32)] * 2,
        (
            cluster_points,
            place,
            far_right,
            partial,
            sums,
            came,
            apex_coupling,
            slab_transfer,
            transfer,
            leaf_basis,
            near_out,
            near_back,
            edge_out,
            from_prev,
            from_next,
        ),
        us=4,
        scratch=[pltpu.VMEM((4 * rhs, 2 * B), BF)],
    )


def solution(mesh):
    return jax.shard_map(
        shards,
        mesh=mesh,
        in_specs=(
            P(None, AXES),
            P(None, AXES),
            P(AXES, None, None, None),
            P(AXES, None),
            P(AXES),
            P(AXES, None, None),
            P(AXES, None, None),
            P(AXES, None),
            P(AXES),
            P(AXES, None, None, None),
            P(AXES, None, None),
            P(),
        ),
        out_specs=(P(None, AXES), P(None, AXES)),
        check_vma=False,
    )
```

```python
import functools

import jax
import jax.numpy as jnp
import numpy as np
from jax import lax
from jax.experimental import pallas as pl
from jax.experimental.pallas import tpu as pltpu
from jax.sharding import PartitionSpec as P

B = 128
HW = 4
AXES = ("slab", "leaf")
BF = jnp.bfloat16
F32 = jnp.float32

Z, Y, X = 1, 3, 5
STEPS = ((Y, 0), (Y, 1), (Z, 0), (Z, 1), (X, 0), (X, 1))
GATHER_STEPS = (*STEPS[4:], *STEPS[:4])


def routed(block, step):
    axis, turn = step
    route = []
    for i in range(lax.axis_size(AXES)):
        pairing = 1 if (i & 1) == turn else 3
        route.append((i, i ^ (pairing << axis)))
    return lax.ppermute(block, AXES, route)


def to_other_core(block):
    return lax.ppermute(block, AXES, [(i, i ^ 1) for i in range(lax.axis_size(AXES))])


def passed_along(block, distance):
    devices = range(lax.axis_size(AXES))
    route = [(i - distance, i) for i in devices if i - distance in devices]
    return lax.ppermute(block, AXES, route)


def slot_tables(devices):
    def table(order):
        slots = np.zeros((2, devices), np.int32)
        for core in range(2):
            for difference in range(devices):
                other = difference & 1
                for place, (axis, turn) in enumerate(order):
                    low, high = (difference >> axis) & 1, (difference >> (axis + 1)) & 1
                    by_one = turn == core ^ other
                    slots[core, difference] |= (low ^ high if by_one else high) << place
                slots[core, difference] |= other << len(order)
        return jnp.asarray(slots.reshape(-1))

    return table(STEPS[::-1]), table(GATHER_STEPS)


def slot_in(table, parents, f, me, devices):
    return table[(me & 1) * devices + (parents[0, f] ^ me)]


def two(value):
    high = value.astype(BF)
    return high, (value - high.astype(F32)).astype(BF)


NN = (((1,), (0,)), ((), ()))
NT = (((1,), (1,)), ((), ()))


def dot(a, b, how):
    return lax.dot_general(a, b, how, preferred_element_type=F32)


def dot3(a, b, how):
    (ah, al), (bh, bl) = two(a), two(b)
    left = jnp.concatenate([ah, al, ah], axis=1)
    right = jnp.concatenate([bh, bh, bl], axis=1 if how is NT else 0)
    return dot(left, right, how)


def stacked(value):
    high, low = two(value)
    upper = jnp.concatenate([high, high], axis=1)
    return jnp.concatenate([upper, jnp.concatenate([low, jnp.zeros_like(low)], axis=1)], axis=0)


def both(value):
    half = value.shape[0] // 2
    return value[:half] + value[half:]


def diagonal(a, b):
    upper = jnp.concatenate([a, jnp.zeros_like(a)], axis=1)
    return jnp.concatenate([upper, jnp.concatenate([jnp.zeros_like(b), b], axis=1)], axis=0)


def pair_mask(points, c, rows):
    lane = lax.broadcasted_iota(jnp.int32, (rows, 2 * B), 1)
    return lane < jnp.where(lane < B, points[c], B + points[c + 1])


def moved(place, axis, first_sends_odd, x_first, held, at_first, at_second):
    me = place[0]
    up = (me & 1) == (1 if x_first else 0)
    y, z = (me >> Y) & 3, (me >> Z) & 3
    last = jnp.where(up, 3, 0)
    if axis == Z:
        moves = z >= 0
    elif axis == Y:
        moves = z == last
    else:
        where = last if x_first else 3 - last
        moves = (y == where) & (z == where)
    odd = ((me >> axis) & 1) == 1
    by_first = ~odd if first_sends_odd else odd
    return jnp.where(moves, jnp.where(by_first, at_first, at_second), held)


def leaf_kernel(
    place,
    points_hbm,
    right_hbm,
    left_hbm,
    basis_hbm,
    transfer_hbm,
    lift_hbm,
    mright,
    mleft,
    pleft,
    sums,
    ahead,
    inchip,
    points,
    right,
    left,
    basis,
    transfer,
    lift,
    done,
):
    rhs = right.shape[0]
    clusters = basis.shape[0]
    pieces = 2
    count_of = iter(range(done.shape[0]))

    def fetch(source, target, index):
        return pltpu.make_async_copy(source.at[index], target.at[index], done.at[next(count_of)])

    per = clusters // pieces
    copies = []
    for j in range(pieces):
        some = pl.ds(j * per, per)
        columns = (slice(None), pl.ds(j * per * B, per * B))
        copies.append(
            [
                fetch(right_hbm, right, columns),
                fetch(left_hbm, left, columns),
                fetch(basis_hbm, basis, some),
                fetch(transfer_hbm, transfer, some),
            ]
        )
    copies[0].append(fetch(points_hbm, points, slice(None)))
    copies[1].append(fetch(lift_hbm, lift, slice(None)))
    for copy in [*copies[0], *copies[1]]:
        copy.start()
    part = jnp.zeros((4 * rhs, B), F32)
    for j in range(pieces):
        for copy in copies[j]:
            copy.wait()
        for c in range(j * per, (j + 1) * per, 2):
            mask = pair_mask(points, c, rhs)
            columns = slice(c * B, (c + 2) * B)
            xr = jnp.where(mask, right[:, columns].astype(F32), 0.0).astype(BF)
            xl = jnp.where(mask, left[:, columns].astype(F32), 0.0).astype(BF)
            for q in range(2):
                mright[c + q] = xr[:, q * B : (q + 1) * B]
                mleft[c + q] = xl[:, q * B : (q + 1) * B]
            leaf = dot(jnp.concatenate([xr, xl], axis=0), diagonal(basis[c], basis[c + 1]), NT)
            high, low = two(jnp.concatenate([transfer[c], transfer[c + 1]], axis=0))
            part = part + dot(stacked(leaf), jnp.concatenate([high, low], axis=0), NN)
    total = both(part)
    pleft[...] = total[rhs:]
    shares = dot3(total, lift[0], NN)
    sums[0] = shares[:rhs]
    sums[1] = shares[rhs:]
    ahead[0] = total[:rhs].astype(BF)
    core = place[0] & 1
    ahead[1:] = mright[pl.ds(core * (clusters - HW), HW)]
    inchip[...] = mright[pl.ds((1 - core) * (clusters - HW), HW)]


def outward_kernel(place, count, parents, table, pleft, sums, coupling, keep, send):
    far_slots = coupling.shape[1]
    half = keep.shape[0] - 1
    keep[...] = jnp.zeros_like(keep)
    send[: half + 1] = jnp.zeros((half + 1, *send.shape[1:]), F32)
    send[half + 1 :] = sums[...]
    wide = stacked(pleft[...])
    me = place[0]
    group = 8
    for start in range(0, far_slots, group):
        values = []
        for f in range(start, start + group, 2):
            (ah, al), (bh, bl) = two(coupling[0, f]), two(coupling[0, f + 1])
            high, low = (jnp.concatenate(pair, axis=1) for pair in ((ah, bh), (al, bl)))
            value = both(dot(wide, jnp.concatenate([high, low], axis=0), NN))
            values += [value[:, :B], value[:, B:]]
        for q, value in enumerate(values):
            f = start + q
            slot = slot_in(table, parents, f, me, 2 * half)
            live = f < count[0]
            keep[jnp.where(live & (slot < half), slot, half)] = value
            send[jnp.where(live & (slot >= half), slot - half, half)] = value


def grow_kernel(ahead, came, out):
    out[0] = ahead[0]
    out[1] = came[0]
    out[2:] = ahead[1:]


def lay_out(payload, going, exact, sums, *rest):
    high, low = two(going)
    start = going.shape[0]
    payload[:start] = high
    if exact:
        payload[start : 2 * start] = low
        start = 2 * start
    for part in (*two(sums), *rest):
        payload[start : start + part.shape[0]] = part
        start = start + part.shape[0]


def first_fold_kernel(
    place, came, partial, sums, ahead, came_ahead, grown, came_grown, back,
    payload, keep, sums_next, gathered, halo, tail,
):
    n = 2 * keep.shape[0]
    total = partial[:n] + came[:n]
    keep[...] = total[: n // 2]
    sums_next[...] = sums[...] + came[n + 1 :]
    gathered[:2] = grown[:2]
    gathered[2:] = came_grown[:2]
    halo[...] = moved(place, X, True, True, ahead[1:], came_ahead[1:], came_grown[2:])
    tail[...] = back[pl.ds((1 - (place[0] & 1)) * HW, HW)]
    lay_out(payload, total[n // 2 :], False, sums_next[...], gathered[...], halo[...], tail[...])


def fold_kernel(step, *refs):
    refs = iter(refs)
    place, came, partial, sums = (next(refs) for _ in range(4))
    axis, turn = STEPS[step - 1]
    gathers = axis != X
    gathers_next = STEPS[step][0] != X
    gathered, halo = (next(refs), next(refs)) if gathers else (None, None)
    tail = next(refs)
    before = next(refs) if turn else None
    inchip = next(refs) if gathers and not gathers_next else None
    next(refs)
    payload, keep, sums_next = (next(refs) for _ in range(3))
    n = partial.shape[0]
    m = sums.shape[0]
    total = partial[...] + came[:n].astype(F32)
    start = n
    if step >= 3:
        total = total + came[n : 2 * n].astype(F32)
        start = 2 * n
    got = came[start : start + m].astype(F32) + came[start + m : start + 2 * m].astype(F32)
    start = start + 2 * m
    if gathers:
        sums_next[...] = sums[...] + got
    else:
        sums_next[:m] = sums[...]
        sums_next[m:] = got
    keep[...] = total[: n // 2]
    end = came.shape[0]
    parts = []
    if gathers:
        a = gathered.shape[0]
        gathered_next = next(refs)
        gathered_next[:a] = gathered[...]
        gathered_next[a : 2 * a] = came[start : start + a]
        halo_now = halo[...]
    tail_now = tail[...]
    if turn:
        last = before.shape[0]
        halo_now = moved(
            place, axis, True, True, halo_now,
            before[last - 2 * HW : last - HW], came[end - 2 * HW : end - HW],
        )
        tail_now = moved(
            place, axis, False, False, tail_now, before[last - HW :], came[end - HW :]
        )
        if gathers_next:
            next(refs)[...] = halo_now
        next(refs)[...] = tail_now
    if gathers_next:
        parts = [gathered_next[...], halo_now]
    elif gathers:
        gathered_next[2 * a : 2 * a + HW] = halo_now
        gathered_next[2 * a + HW :] = inchip[...]
    lay_out(payload, total[n // 2 :], step >= 2, sums_next[...], *parts, tail_now)


def rows_of(blocks, c):
    return jnp.concatenate([blocks[c, s] for s in range(blocks.shape[1])], axis=1)


def add_back(columns, first, mleft, blocks, clusters, back):
    done = []
    for c in clusters:
        places = [columns[s, c] - first[0] for s in range(blocks.shape[1])]
        done.append((places, dot(mleft[c], rows_of(blocks, c), NN)))
    for places, value in done:
        held = [back[place] for place in places]
        for s, place in enumerate(places):
            back[place] = held[s] + value[:, s * B : (s + 1) * B]


def near_outer_kernel(columns, first, mleft, blocks, back, sent):
    clusters = mleft.shape[0]
    back[...] = jnp.zeros_like(back)
    add_back(columns, first, mleft, blocks, range(HW), back)
    add_back(columns, first, mleft, blocks, range(clusters - HW, clusters), back)
    sent[:HW] = back[:HW].astype(BF)
    sent[HW:] = back[clusters + HW :].astype(BF)


def near_kernel(columns, first, mright, mleft, blocks, back_outer, _, out, back):
    clusters = mright.shape[0]
    slots = blocks.shape[1]
    back[...] = back_outer[...]
    for start in range(0, clusters, 4):
        group = range(start, start + 4)
        for c in group:
            inside = []
            for s in range(slots):
                own = columns[s, c] - first[0] - HW
                value = mright[jnp.clip(own, 0, clusters - 1)]
                is_own = (own >= 0) & (own < clusters)
                inside.append(jnp.where(is_own, value, jnp.zeros_like(value)))
            out[c] = dot(rows_of(blocks, c), jnp.concatenate(inside, axis=1), NT).T
        if HW <= start < clusters - HW:
            add_back(columns, first, mleft, blocks, group, back)


def edge_kernel(place, columns, first, other, blocks, _, out):
    slots = blocks.shape[1]
    clusters = columns.shape[1]
    core = place[0] & 1
    start = other.shape[0] - 2 * HW
    for g in range(2 * HW):
        low = g < HW
        c = g if low else clusters - 2 * HW + g
        halo = start + HW * (core if low else 1 - core)
        values = []
        for s in range(slots):
            row = columns[s, c] - first[0] - (0 if low else clusters + HW)
            value = other[halo + jnp.clip(row, 0, HW - 1)]
            is_there = (row >= 0) & (row < HW)
            values.append(jnp.where(is_there, value, jnp.zeros_like(value)))
        out[g] = dot(rows_of(blocks, c), jnp.concatenate(values, axis=1), NT).T


def forward_kernel(place, count, parents, table, own, other, coupling, out, all_of):
    far_slots = coupling.shape[1]
    half = all_of.shape[0] // 2
    all_of[:half] = own[:half]
    all_of[half:] = other[:half]
    me = place[0]
    total = jnp.zeros((B, own.shape[1]), F32)
    group = 48
    for start in range(0, far_slots, group):
        rows, values = [], []
        for f in range(start, start + group):
            value = all_of[slot_in(table, parents, f, me, 2 * half)]
            value = jnp.where(f < count[0], value, jnp.zeros_like(value))
            values += [value, value]
            rows += two(coupling[0, f])
        total = total + dot(
            jnp.concatenate(rows, axis=1), jnp.concatenate(values, axis=1), NT
        )
    out[...] = total.T


def down_kernel(
    points,
    place,
    far_right,
    partial,
    sums,
    came,
    apex,
    lift,
    transfer,
    basis,
    near_out,
    near_back,
    edge_out,
    back_came,
    tail,
    before,
    product,
    adjoint,
    hats,
):
    step = pl.program_id(0)
    per = basis.shape[0]
    clusters, rhs = near_out.shape[:2]

    @pl.when(step == 0)
    def _():
        core = place[0] & 1
        slab = place[0] >> X
        got = came[2:6].astype(F32) + came[6:10].astype(F32)
        slabs = [sums[2], sums[3], got[0], got[1], got[2], got[3]]
        top_right = jnp.zeros((rhs, B), F32)
        top_left = jnp.zeros((rhs, B), F32)
        for t, mask in enumerate((1 + 2 * core, 3 - 2 * core, 2)):
            top_right = top_right + dot3(slabs[2 * t], apex[slab, slab ^ mask], NT)
            top_left = top_left + dot3(slabs[2 * t + 1], apex[slab ^ mask, slab], NN)
        far_left = partial[0] + (came[0].astype(F32) + came[1].astype(F32))
        hats[...] = stacked(
            jnp.concatenate([far_right[...], far_left], axis=0)
            + dot3(jnp.concatenate([top_right, top_left], axis=0), lift[0], NT)
        )

    for g in range(0, per, 2):
        c = step * per + g
        high, low = two(jnp.concatenate([transfer[g], transfer[g + 1]], axis=0))
        down = both(dot(hats[...], jnp.concatenate([high, low], axis=1), NT))
        high, low = two(down)
        two_bases = diagonal(basis[g], basis[g + 1])
        far = dot(
            jnp.concatenate([high, low], axis=1),
            jnp.concatenate([two_bases, two_bases], axis=0),
            NN,
        )
        mask = pair_mask(points, c, rhs)
        columns = slice(g * B, (g + 2) * B)
        near = jnp.concatenate([near_out[c], near_out[c + 1]], axis=1)
        back = jnp.concatenate([near_back[HW + c], near_back[HW + c + 1]], axis=1)
        product[:, columns] = jnp.where(mask, near + far[:rhs], 0.0)
        adjoint[:, columns] = jnp.where(mask, back + far[rhs:], 0.0)

    core = place[0] & 1
    rows = before.shape[0]
    far_tail = moved(place, X, False, False, tail[...], before[rows - HW :], came[10:])
    near_tail = back_came[pl.ds(core * HW, HW)]

    def edge(g, c, low):
        mask = lax.broadcasted_iota(jnp.int32, (rhs, B), 1) < points[c]
        columns = slice((c % per) * B, (c % per + 1) * B)
        product[:, columns] += jnp.where(mask, edge_out[g], 0.0)
        tail_is_far = (core == 0) if low else (core == 1)
        value = jnp.where(tail_is_far, far_tail[g % HW], near_tail[g % HW]).astype(F32)
        adjoint[:, columns] += jnp.where(mask, value, 0.0)

    @pl.when(step == 0)
    def _():
        for g in range(HW):
            edge(g, g, True)

    @pl.when(step == pl.num_programs(0) - 1)
    def _():
        for g in range(HW):
            edge(HW + g, clusters - HW + g, False)


SMEM = pl.BlockSpec(memory_space=pltpu.SMEM)
HBM = pl.BlockSpec(memory_space=pltpu.HBM)
ANY = pl.BlockSpec(memory_space=pl.ANY)
VMEM = pl.BlockSpec(memory_space=pltpu.VMEM)
MIB = 1024 * 1024


def shape(dims, kind):
    return jax.ShapeDtypeStruct(dims, kind)


def whole(*dims):
    return pl.BlockSpec(dims, lambda *_: (0,) * len(dims))


def call(kernel, name, grid, ins, outs, args, us, scratch=(), vmem=20):
    results = pl.pallas_call(
        kernel,
        grid=grid,
        out_shape=tuple(shape(dims, kind) for _, dims, kind in outs),
        in_specs=ins,
        out_specs=tuple(spec for spec, _, _ in outs),
        scratch_shapes=list(scratch),
        compiler_params=pltpu.CompilerParams(vmem_limit_bytes=vmem * MIB),
        cost_estimate=pl.CostEstimate(
            flops=1000, bytes_accessed=int(us * 3.6e6), transcendentals=0
        ),
        name=name,
    )(*args)
    return results


def shards(
    right_sides,
    left_sides,
    near_blocks,
    near_columns,
    cluster_points,
    leaf_basis,
    transfer,
    far_parents,
    far_count,
    coupling,
    slab_transfer,
    apex_coupling,
):
    rhs = right_sides.shape[0]
    clusters = near_blocks.shape[0]
    rank = leaf_basis.shape[1]
    me = lax.axis_index(AXES)
    devices = lax.axis_size(AXES)
    block = (rhs, B)
    all_clusters = (clusters, *block)
    half = devices // 2
    place = me.astype(jnp.int32)[None]
    first = place * clusters - HW
    columns = near_columns.T
    reduce_table, gather_table = slot_tables(devices)

    def rows(n, kind=BF):
        return (VMEM, (n, *block), kind)

    mright, mleft, pleft, sums, ahead, inchip = call(
        leaf_kernel,
        "leaf",
        (),
        [SMEM] + [HBM] * 6,
        [rows(clusters), rows(clusters), (VMEM, block, F32), rows(2, F32), rows(1 + HW), rows(HW)],
        (
            place,
            *(
                pltpu.with_memory_space_constraint(value, pltpu.HBM)
                for value in (
                    cluster_points,
                    right_sides,
                    left_sides,
                    leaf_basis,
                    transfer,
                    slab_transfer,
                )
            ),
        ),
        us=3,
        scratch=[
            pltpu.SMEM(cluster_points.shape, jnp.int32),
            pltpu.VMEM(right_sides.shape, BF),
            pltpu.VMEM(left_sides.shape, BF),
            pltpu.VMEM(leaf_basis.shape, BF),
            pltpu.VMEM(transfer.shape, F32),
            pltpu.VMEM(slab_transfer.shape, F32),
            pltpu.SemaphoreType.DMA((10,)),
        ],
    )
    came_ahead = routed(ahead, GATHER_STEPS[0])

    partial, sent = call(
        outward_kernel,
        "outward",
        (),
        [SMEM] * 4 + [VMEM] * 3,
        [rows(half + 1, F32), rows(half + 3, F32)],
        (place, far_count, far_parents, reduce_table, pleft, sums, coupling),
        us=2,
    )
    came = to_other_core(sent)
    (grown,) = call(
        grow_kernel, "grow", (), [VMEM] * 2, [rows(2 + HW)], (ahead, came_ahead), us=0.2
    )
    came_grown = routed(grown, GATHER_STEPS[1])
    back_outer, back_sent = call(
        near_outer_kernel,
        "near_outer",
        (),
        [SMEM] * 2 + [VMEM] * 2,
        [rows(clusters + 2 * HW, F32), rows(2 * HW)],
        (columns, first, mleft, near_blocks),
        us=1,
    )
    back_came = to_other_core(back_sent)

    payload, partial, sums, gathered, halo, tail = call(
        first_fold_kernel,
        "first_fold",
        (),
        [SMEM] + [VMEM] * 8,
        [
            rows(half // 2 + 4 + 4 + 2 * HW),
            rows(half // 2, F32),
            rows(2, F32),
            rows(4),
            rows(HW),
            rows(HW),
        ],
        (place, came, partial, sums, ahead, came_ahead, grown, came_grown, back_came),
        us=0.3,
    )
    came = routed(payload, STEPS[0])
    before = None
    after = payload
    for step in range(1, len(STEPS)):
        axis, turn = STEPS[step - 1]
        gathers, gathers_next = axis != X, STEPS[step][0] != X
        if step == 1:
            near_out, near_back = call(
                near_kernel,
                "near",
                (),
                [SMEM] * 2 + [VMEM] * 4 + [ANY],
                [rows(clusters, F32), rows(clusters + 2 * HW, F32)],
                (columns, first, mright, mleft, near_blocks, back_outer, payload),
                us=4,
            )
            after = near_out
        if step == 5:
            gathered_other = to_other_core(gathered)
            (far_right,) = call(
                forward_kernel,
                "forward",
                (),
                [SMEM] * 4 + [VMEM] * 3,
                [(VMEM, block, F32)],
                (
                    place,
                    far_count,
                    far_parents,
                    gather_table,
                    gathered,
                    gathered_other,
                    coupling,
                ),
                us=2.5,
                scratch=[pltpu.VMEM((devices, *block), BF)],
            )
            after = far_right
        n = half >> step
        m = 2 if gathers else 4
        a = 4 << (step - 1)
        size = n // 2 * (2 if step >= 2 else 1) + 2 * m + HW
        args = [place, came, partial, sums]
        outs = [None, rows(n // 2, F32), rows(m, F32)]
        if gathers:
            args += [gathered, halo]
            outs.append(rows(2 * a if gathers_next else 2 * a + 2 * HW))
        args.append(tail)
        if turn:
            args.append(before)
            outs += [rows(HW)] * (2 if gathers_next else 1)
        if gathers and not gathers_next:
            args.append(inchip)
        if gathers_next:
            size += 2 * a + HW
        outs[0] = rows(size)
        made = call(
            functools.partial(fold_kernel, step),
            "fold",
            (),
            [SMEM] + [VMEM] * (len(args) - 1) + [ANY],
            outs,
            (*args, after),
            us=0.3,
        )
        payload, partial, sums, *made = made
        if gathers:
            gathered, *made = made
        if turn and gathers_next:
            halo, *made = made
        if turn:
            (tail,) = made
        before = came
        came = routed(payload, STEPS[step])

    (edge_out,) = call(
        edge_kernel,
        "edge",
        (),
        [SMEM] * 3 + [VMEM] * 2 + [ANY],
        [rows(2 * HW, F32)],
        (place, columns, first, gathered_other, near_blocks, payload),
        us=1.5,
    )

    per = 16
    sides = pl.BlockSpec((rhs, per * B), lambda i: (0, i))
    bases = pl.BlockSpec((per, rank, B), lambda i: (i, 0, 0))
    return call(
        down_kernel,
        "down",
        (clusters // per,),
        [
            SMEM,
            SMEM,
            whole(*block),
            whole(1, *block),
            whole(4, *block),
            whole(*came.shape),
            whole(*apex_coupling.shape),
            whole(1, B, B),
            bases,
            bases,
            whole(*all_clusters),
            whole(clusters + 2 * HW, *block),
            whole(*edge_out.shape),
            whole(*back_came.shape),
            whole(*tail.shape),
            whole(*before.shape),
        ],
        [(sides, (rhs, clusters * B), F32)] * 2,
        (
            cluster_points,
            place,
            far_right,
            partial,
            sums,
            came,
            apex_coupling,
            slab_transfer,
            transfer,
            leaf_basis,
            near_out,
            near_back,
            edge_out,
            back_came,
            tail,
            before,
        ),
        us=4,
        scratch=[pltpu.VMEM((4 * rhs, 2 * B), BF)],
    )


def solution(mesh):
    return jax.shard_map(
        shards,
        mesh=mesh,
        in_specs=(
            P(None, AXES),
            P(None, AXES),
            P(AXES, None, None, None),
            P(AXES, None),
            P(AXES),
            P(AXES, None, None),
            P(AXES, None, None),
            P(AXES, None),
            P(AXES),
            P(AXES, None, None, None),
            P(AXES, None, None),
            P(),
        ),
        out_specs=(P(None, AXES), P(None, AXES)),
        check_vma=False,
    )
```

```python
import functools

import jax
import jax.numpy as jnp
import numpy as np
from jax import lax
from jax.experimental import pallas as pl
from jax.experimental.pallas import tpu as pltpu
from jax.sharding import PartitionSpec as P

B = 128
HW = 4
AXES = ("slab", "leaf")
BF = jnp.bfloat16
F32 = jnp.float32

Z, Y, X = 1, 3, 5
STEPS = ((Y, 0), (Y, 1), (Z, 0), (Z, 1), (X, 0), (X, 1))
GATHER_STEPS = (STEPS[5], *STEPS[:5])


def routed(block, step):
    axis, turn = step
    route = []
    for i in range(lax.axis_size(AXES)):
        pairing = 1 if (i & 1) == turn else 3
        route.append((i, i ^ (pairing << axis)))
    return lax.ppermute(block, AXES, route)


def to_other_core(block):
    return lax.ppermute(block, AXES, [(i, i ^ 1) for i in range(lax.axis_size(AXES))])


def passed_along(block, distance):
    devices = range(lax.axis_size(AXES))
    route = [(i - distance, i) for i in devices if i - distance in devices]
    return lax.ppermute(block, AXES, route)


def slot_tables(devices):
    def table(order):
        slots = np.zeros((2, devices), np.int32)
        for core in range(2):
            for difference in range(devices):
                other = difference & 1
                for place, (axis, turn) in enumerate(order):
                    low, high = (difference >> axis) & 1, (difference >> (axis + 1)) & 1
                    by_one = turn == core ^ other
                    slots[core, difference] |= (low ^ high if by_one else high) << place
                slots[core, difference] |= other << len(order)
        return jnp.asarray(slots.reshape(-1))

    return table(STEPS[::-1]), table(GATHER_STEPS)


def slot_in(table, parents, f, me, devices):
    return table[(me & 1) * devices + (parents[0, f] ^ me)]


def two(value):
    high = value.astype(BF)
    return high, (value - high.astype(F32)).astype(BF)


NN = (((1,), (0,)), ((), ()))
NT = (((1,), (1,)), ((), ()))


def dot(a, b, how):
    return lax.dot_general(a, b, how, preferred_element_type=F32)


def dot3(a, b, how):
    (ah, al), (bh, bl) = two(a), two(b)
    left = jnp.concatenate([ah, al, ah], axis=1)
    right = jnp.concatenate([bh, bh, bl], axis=1 if how is NT else 0)
    return dot(left, right, how)


def stacked(value):
    high, low = two(value)
    upper = jnp.concatenate([high, high], axis=1)
    return jnp.concatenate([upper, jnp.concatenate([low, jnp.zeros_like(low)], axis=1)], axis=0)


def both(value):
    half = value.shape[0] // 2
    return value[:half] + value[half:]


def diagonal(a, b):
    upper = jnp.concatenate([a, jnp.zeros_like(a)], axis=1)
    return jnp.concatenate([upper, jnp.concatenate([jnp.zeros_like(b), b], axis=1)], axis=0)


def pair_mask(points, c, rows):
    lane = lax.broadcasted_iota(jnp.int32, (rows, 2 * B), 1)
    return lane < jnp.where(lane < B, points[c], B + points[c + 1])


def moved(place, axis, held, at_first, at_second):
    me = place[0]
    y, z = (me >> Y) & 3, (me >> Z) & 3
    last = 3 * (1 - (me & 1))
    if axis == Z:
        moves = z >= 0
    elif axis == Y:
        moves = z == last
    else:
        moves = (y == 3 - last) & (z == 3 - last)
    odd = ((me >> axis) & 1) == 1
    return jnp.where(moves, jnp.where(odd, at_first, at_second), held)


def rise_kernel(
    place,
    count,
    points_hbm,
    parents_hbm,
    table_hbm,
    right_hbm,
    left_hbm,
    basis_hbm,
    transfer_hbm,
    lift_hbm,
    coupling_hbm,
    mright,
    mleft,
    pright,
    keep,
    send,
    sums,
    points,
    parents,
    table,
    right,
    left,
    basis,
    transfer,
    lift,
    coupling,
    done,
):
    rhs = right.shape[0]
    clusters = basis.shape[0]
    far_slots = coupling.shape[1]
    half = keep.shape[0] - 1
    pieces, far_pieces = 2, 4
    count_of = iter(range(done.shape[0]))

    def fetch(source, target, index):
        return pltpu.make_async_copy(source.at[index], target.at[index], done.at[next(count_of)])

    per = clusters // pieces
    early = []
    for j in range(pieces):
        some = pl.ds(j * per, per)
        columns = (slice(None), pl.ds(j * per * B, per * B))
        early.append(
            [
                fetch(right_hbm, right, columns),
                fetch(left_hbm, left, columns),
                fetch(basis_hbm, basis, some),
                fetch(transfer_hbm, transfer, some),
            ]
        )
    early[0].append(fetch(points_hbm, points, slice(None)))
    early[1].append(fetch(parents_hbm, parents, slice(None)))
    early[1].append(fetch(table_hbm, table, slice(None)))
    early[1].append(fetch(lift_hbm, lift, slice(None)))
    far_per = far_slots // far_pieces
    late = [
        fetch(coupling_hbm, coupling, (slice(None), pl.ds(j * far_per, far_per)))
        for j in range(far_pieces)
    ]
    for copy in [*early[0], *early[1]]:
        copy.start()
    keep[...] = jnp.zeros_like(keep)
    send[...] = jnp.zeros_like(send)

    part = jnp.zeros((4 * rhs, B), F32)
    for j in range(pieces):
        for copy in early[j]:
            copy.wait()
        if j == 0:
            for copy in late:
                copy.start()
        for c in range(j * per, (j + 1) * per, 2):
            mask = pair_mask(points, c, rhs)
            columns = slice(c * B, (c + 2) * B)
            xr = jnp.where(mask, right[:, columns].astype(F32), 0.0).astype(BF)
            xl = jnp.where(mask, left[:, columns].astype(F32), 0.0).astype(BF)
            for q in range(2):
                mright[c + q] = xr[:, q * B : (q + 1) * B]
                mleft[c + q] = xl[:, q * B : (q + 1) * B]
            leaf = dot(jnp.concatenate([xr, xl], axis=0), diagonal(basis[c], basis[c + 1]), NT)
            high, low = two(jnp.concatenate([transfer[c], transfer[c + 1]], axis=0))
            part = part + dot(stacked(leaf), jnp.concatenate([high, low], axis=0), NN)
    total = both(part)
    pright[0] = total[:rhs].astype(BF)
    shares = dot3(total, lift[0], NN)
    for q in range(2):
        value = shares[q * rhs : (q + 1) * rhs]
        send[half + 1 + q] = value
        sums[q] = value

    wide = stacked(total[rhs:])
    me = place[0]
    group = 8
    for j in range(far_pieces):
        late[j].wait()
        for start in range(j * far_per, (j + 1) * far_per, group):
            values = []
            for f in range(start, start + group, 2):
                (ah, al), (bh, bl) = two(coupling[0, f]), two(coupling[0, f + 1])
                high, low = (jnp.concatenate(pair, axis=1) for pair in ((ah, bh), (al, bl)))
                value = both(dot(wide, jnp.concatenate([high, low], axis=0), NN))
                values += [value[:, :B], value[:, B:]]
            for q, value in enumerate(values):
                f = start + q
                slot = slot_in(table, parents, f, me, 2 * half)
                live = f < count[0]
                own = jnp.where(live & (slot < half), slot, half)
                other = jnp.where(live & (slot >= half), slot - half, half)
                keep[own] = value
                send[other] = value

def lay_out(payload, going, exact, sums, *rest):
    high, low = two(going)
    start = going.shape[0]
    payload[:start] = high
    if exact:
        payload[start : 2 * start] = low
        start = 2 * start
    for part in (*two(sums), *rest):
        payload[start : start + part.shape[0]] = part
        start = start + part.shape[0]


def fold_kernel(step, *refs):
    refs = list(refs)
    place, came, partial, sums = refs[:4]
    del refs[:4]
    payload, keep, sums_next = refs[-5:-2]
    gathered_next, halo_next = refs[-2:]
    gathered = refs[0]
    a = gathered.shape[0]
    n = 2 * keep.shape[0]
    m = sums.shape[0]
    gathered_next[:a] = gathered[...]
    if step == 0:
        came_own, pair = refs[1:3]
        total = partial[:n] + came[:n]
        got = came[n + 1 :]
        gathered_next[a:] = came_own[...]
        other = HW * (1 - (place[0] & 1))
        halo_next[:HW] = pair[pl.ds(other, HW)]
        halo_next[HW:] = pair[pl.ds(2 * HW + other, HW)]
    else:
        halo = refs[1]
        total = partial[...] + came[:n].astype(F32)
        start = n
        if step >= 3:
            total = total + came[n : 2 * n].astype(F32)
            start = 2 * n
        got = came[start : start + m].astype(F32) + came[start + m : start + 2 * m].astype(F32)
        start = start + 2 * m
        gathered_next[a:] = came[start : start + a]
        axis, turn = STEPS[step - 1]
        if turn:
            before = refs[2]
            halo_next[...] = moved(
                place, axis, halo[...], before[before.shape[0] - 2 * HW :], came[start + a :]
            )
        else:
            halo_next[...] = halo[...]
    if sums_next.shape[0] == m:
        sums_next[...] = sums[...] + got
    else:
        sums_next[:m] = sums[...]
        sums_next[m:] = got
    keep[...] = total[: n // 2]
    parts = [halo_next[...]]
    if step < 5:
        parts = [gathered_next[...], *parts]
    lay_out(payload, total[n // 2 :], step >= 2, sums_next[...], *parts)


def rows_of(blocks, c):
    return jnp.concatenate([blocks[c, s] for s in range(blocks.shape[1])], axis=1)


def add_back(columns, first, mleft, blocks, clusters, back):
    done = []
    for c in clusters:
        places = [columns[s, c] - first[0] for s in range(blocks.shape[1])]
        done.append((places, dot(mleft[c], rows_of(blocks, c), NN)))
    for places, value in done:
        held = [back[place] for place in places]
        for s, place in enumerate(places):
            back[place] = held[s] + value[:, s * B : (s + 1) * B]


def near_outer_kernel(columns, first, mright, mleft, blocks, back, sent):
    clusters = mleft.shape[0]
    back[...] = jnp.zeros_like(back)
    add_back(columns, first, mleft, blocks, range(HW), back)
    add_back(columns, first, mleft, blocks, range(clusters - HW, clusters), back)
    sent[:HW] = mright[:HW]
    sent[HW : 2 * HW] = mright[clusters - HW :]
    sent[2 * HW : 3 * HW] = back[:HW].astype(BF)
    sent[3 * HW :] = back[clusters + HW :].astype(BF)


def near_kernel(columns, first, mright, mleft, blocks, back_outer, _, out, back):
    clusters = mright.shape[0]
    slots = blocks.shape[1]
    back[...] = back_outer[...]
    for start in range(0, clusters, 4):
        group = range(start, start + 4)
        for c in group:
            inside = []
            for s in range(slots):
                own = columns[s, c] - first[0] - HW
                value = mright[jnp.clip(own, 0, clusters - 1)]
                is_own = (own >= 0) & (own < clusters)
                inside.append(jnp.where(is_own, value, jnp.zeros_like(value)))
            out[c] = dot(rows_of(blocks, c), jnp.concatenate(inside, axis=1), NT).T
        if HW <= start < clusters - HW:
            add_back(columns, first, mleft, blocks, group, back)


def edge(low, columns, first, halo, blocks, out):
    slots = blocks.shape[1]
    clusters = columns.shape[1]
    start = jnp.where(low, 0, clusters - HW)
    row_start = first[0] + jnp.where(low, 0, clusters + HW)
    for g in range(HW):
        c = start + g
        values = []
        for s in range(slots):
            row = columns[s, c] - row_start
            value = halo[jnp.clip(row, 0, HW - 1)]
            is_there = (row >= 0) & (row < HW)
            values.append(jnp.where(is_there, value, jnp.zeros_like(value)))
        out[g] = dot(rows_of(blocks, c), jnp.concatenate(values, axis=1), NT).T


def edge_pair_kernel(place, columns, first, pair, blocks, _, out, back, halo):
    core = place[0] & 1
    halo[...] = pair[pl.ds(HW * core, HW)]
    edge(core == 1, columns, first, halo, blocks, out)
    back[...] = pair[pl.ds(2 * HW + HW * core, HW)].astype(F32)


def edge_chain_kernel(place, columns, first, held, before, came, blocks, _, out, back, halo):
    core = place[0] & 1
    value = moved(
        place, X, held[...], before[before.shape[0] - 2 * HW :], came[came.shape[0] - 2 * HW :]
    )
    halo[...] = value[:HW]
    edge(core == 0, columns, first, halo, blocks, out)
    back[...] = value[HW:].astype(F32)


def forward_kernel(place, count, parents, table, own, other, coupling, _, out, all_of):
    far_slots = coupling.shape[1]
    half = all_of.shape[0] // 2
    all_of[:half] = own[:half]
    all_of[half:] = other[:half]
    me = place[0]
    total = jnp.zeros((B, own.shape[1]), F32)
    group = 48
    for start in range(0, far_slots, group):
        rows, values = [], []
        for f in range(start, start + group):
            value = all_of[slot_in(table, parents, f, me, 2 * half)]
            value = jnp.where(f < count[0], value, jnp.zeros_like(value))
            values += [value, value]
            rows += two(coupling[0, f])
        total = total + dot(
            jnp.concatenate(rows, axis=1), jnp.concatenate(values, axis=1), NT
        )
    out[...] = total.T


def down_kernel(
    points,
    place,
    far_right,
    partial,
    sums,
    came,
    apex,
    lift,
    transfer,
    basis,
    near_out,
    near_back,
    pair_out,
    pair_back,
    chain_out,
    chain_back,
    product,
    adjoint,
    hats,
):
    step = pl.program_id(0)
    per = basis.shape[0]
    clusters, rhs = near_out.shape[:2]

    @pl.when(step == 0)
    def _():
        core = place[0] & 1
        slab = place[0] >> X
        got = came[2:6].astype(F32) + came[6:10].astype(F32)
        slabs = [sums[2], sums[3], got[0], got[1], got[2], got[3]]
        top_right = jnp.zeros((rhs, B), F32)
        top_left = jnp.zeros((rhs, B), F32)
        for t, mask in enumerate((1 + 2 * core, 3 - 2 * core, 2)):
            top_right = top_right + dot3(slabs[2 * t], apex[slab, slab ^ mask], NT)
            top_left = top_left + dot3(slabs[2 * t + 1], apex[slab ^ mask, slab], NN)
        far_left = partial[0] + (came[0].astype(F32) + came[1].astype(F32))
        hats[...] = stacked(
            jnp.concatenate([far_right[...], far_left], axis=0)
            + dot3(jnp.concatenate([top_right, top_left], axis=0), lift[0], NT)
        )

    for g in range(0, per, 2):
        c = step * per + g
        high, low = two(jnp.concatenate([transfer[g], transfer[g + 1]], axis=0))
        down = both(dot(hats[...], jnp.concatenate([high, low], axis=1), NT))
        high, low = two(down)
        two_bases = diagonal(basis[g], basis[g + 1])
        far = dot(
            jnp.concatenate([high, low], axis=1),
            jnp.concatenate([two_bases, two_bases], axis=0),
            NN,
        )
        mask = pair_mask(points, c, rhs)
        columns = slice(g * B, (g + 2) * B)
        near = jnp.concatenate([near_out[c], near_out[c + 1]], axis=1)
        back = jnp.concatenate([near_back[HW + c], near_back[HW + c + 1]], axis=1)
        product[:, columns] = jnp.where(mask, near + far[:rhs], 0.0)
        adjoint[:, columns] = jnp.where(mask, back + far[rhs:], 0.0)

    def add_edge(c, low):
        mask = lax.broadcasted_iota(jnp.int32, (rhs, B), 1) < points[c]
        columns = slice((c % per) * B, (c % per + 1) * B)
        g = c % HW
        in_chip = (place[0] & 1) == (1 if low else 0)
        out = jnp.where(in_chip, pair_out[g], chain_out[g])
        back = jnp.where(in_chip, pair_back[g], chain_back[g])
        product[:, columns] += jnp.where(mask, out, 0.0)
        adjoint[:, columns] += jnp.where(mask, back, 0.0)

    @pl.when(step == 0)
    def _():
        for c in range(HW):
            add_edge(c, True)

    @pl.when(step == pl.num_programs(0) - 1)
    def _():
        for c in range(clusters - HW, clusters):
            add_edge(c, False)


SMEM = pl.BlockSpec(memory_space=pltpu.SMEM)
HBM = pl.BlockSpec(memory_space=pltpu.HBM)
ANY = pl.BlockSpec(memory_space=pl.ANY)
VMEM = pl.BlockSpec(memory_space=pltpu.VMEM)
MIB = 1024 * 1024


def shape(dims, kind):
    return jax.ShapeDtypeStruct(dims, kind)


def whole(*dims):
    return pl.BlockSpec(dims, lambda *_: (0,) * len(dims))


def call(kernel, name, grid, ins, outs, args, us, scratch=(), vmem=20):
    results = pl.pallas_call(
        kernel,
        grid=grid,
        out_shape=tuple(shape(dims, kind) for _, dims, kind in outs),
        in_specs=ins,
        out_specs=tuple(spec for spec, _, _ in outs),
        scratch_shapes=list(scratch),
        compiler_params=pltpu.CompilerParams(vmem_limit_bytes=vmem * MIB),
        cost_estimate=pl.CostEstimate(
            flops=1000, bytes_accessed=int(us * 3.6e6), transcendentals=0
        ),
        name=name,
    )(*args)
    return results


def shards(
    right_sides,
    left_sides,
    near_blocks,
    near_columns,
    cluster_points,
    leaf_basis,
    transfer,
    far_parents,
    far_count,
    coupling,
    slab_transfer,
    apex_coupling,
):
    rhs = right_sides.shape[0]
    clusters = near_blocks.shape[0]
    rank = leaf_basis.shape[1]
    me = lax.axis_index(AXES)
    devices = lax.axis_size(AXES)
    block = (rhs, B)
    all_clusters = (clusters, *block)
    half = devices // 2
    place = me.astype(jnp.int32)[None]
    first = place * clusters - HW
    columns = near_columns.T
    reduce_table, gather_table = slot_tables(devices)

    def rows(n, kind=BF):
        return (VMEM, (n, *block), kind)

    def at_rest(*values):
        return [pltpu.with_memory_space_constraint(value, pltpu.HBM) for value in values]

    mright, mleft, own, partial, sent, sums = call(
        rise_kernel,
        "rise",
        (),
        [SMEM] * 2 + [HBM] * 9,
        [
            rows(clusters),
            rows(clusters),
            rows(1),
            rows(half + 1, F32),
            rows(half + 3, F32),
            rows(2, F32),
        ],
        (
            place,
            far_count,
            *at_rest(
                cluster_points,
                far_parents,
                reduce_table,
                right_sides,
                left_sides,
                leaf_basis,
                transfer,
                slab_transfer,
                coupling,
            ),
        ),
        us=5,
        scratch=[
            pltpu.SMEM(cluster_points.shape, jnp.int32),
            pltpu.SMEM(far_parents.shape, jnp.int32),
            pltpu.SMEM(reduce_table.shape, jnp.int32),
            pltpu.VMEM(right_sides.shape, BF),
            pltpu.VMEM(left_sides.shape, BF),
            pltpu.VMEM(leaf_basis.shape, BF),
            pltpu.VMEM(transfer.shape, F32),
            pltpu.VMEM(slab_transfer.shape, F32),
            pltpu.VMEM(coupling.shape, F32),
            pltpu.SemaphoreType.DMA((16,)),
        ],
    )
    came = to_other_core(sent)
    came_own = routed(own, GATHER_STEPS[0])
    back_outer, pair_sent = call(
        near_outer_kernel,
        "near_outer",
        (),
        [SMEM] * 2 + [VMEM] * 3,
        [rows(clusters + 2 * HW, F32), rows(4 * HW)],
        (columns, first, mright, mleft, near_blocks),
        us=1,
    )
    pair = to_other_core(pair_sent)

    def fold(step, came, partial, sums, gathered, *rest, after):
        n = half >> step
        m = 2 if step == 0 or STEPS[step - 1][0] != X else 4
        a = 2 << step
        size = n // 2 * (2 if step >= 2 else 1) + 2 * m + 2 * HW + (a if step < 5 else 0)
        args = (place, came, partial, sums, gathered, *rest)
        return call(
            lambda *refs: fold_kernel(step, *refs[: len(args)], *refs[len(args) + 1 :]),
            "fold",
            (),
            [SMEM] + [VMEM] * (len(args) - 1) + [ANY],
            [rows(size), rows(n // 2, F32), rows(m, F32), rows(a), rows(2 * HW)],
            (*args, after),
            us=0.3,
        )

    payload, partial, sums, gathered, halo = fold(
        0, came, partial, sums, own, came_own, pair, after=back_outer
    )
    came = routed(payload, STEPS[0])
    near_out, near_back = call(
        near_kernel,
        "near",
        (),
        [SMEM] * 2 + [VMEM] * 4 + [ANY],
        [rows(clusters, F32), rows(clusters + 2 * HW, F32)],
        (columns, first, mright, mleft, near_blocks, back_outer, payload),
        us=4,
    )
    after = near_out
    before = came
    for step in range(1, len(STEPS)):
        rest = (halo, before) if STEPS[step - 1][1] else (halo,)
        before = came
        payload, partial, sums, gathered, halo = fold(
            step, came, partial, sums, gathered, *rest, after=after
        )
        came = routed(payload, STEPS[step])
        after = payload
        if step == 1:
            pair_out, pair_back = call(
                edge_pair_kernel,
                "edge_pair",
                (),
                [SMEM] * 3 + [VMEM] * 2 + [ANY],
                [rows(HW, F32)] * 2,
                (place, columns, first, pair, near_blocks, payload),
                us=0.8,
                scratch=[pltpu.VMEM((HW, *block), BF)],
            )
            after = pair_out
    gathered_other = to_other_core(gathered)
    (far_right,) = call(
        forward_kernel,
        "forward",
        (),
        [SMEM] * 4 + [VMEM] * 3 + [ANY],
        [(VMEM, block, F32)],
        (
            place,
            far_count,
            far_parents,
            gather_table,
            gathered,
            gathered_other,
            coupling,
            payload,
        ),
        us=2.5,
        scratch=[pltpu.VMEM((devices, *block), BF)],
    )
    chain_out, chain_back = call(
        edge_chain_kernel,
        "edge_chain",
        (),
        [SMEM] * 3 + [VMEM] * 4 + [ANY],
        [rows(HW, F32)] * 2,
        (place, columns, first, halo, before, came, near_blocks, far_right),
        us=0.8,
        scratch=[pltpu.VMEM((HW, *block), BF)],
    )

    per = 16
    sides = pl.BlockSpec((rhs, per * B), lambda i: (0, i))
    bases = pl.BlockSpec((per, rank, B), lambda i: (i, 0, 0))
    return call(
        down_kernel,
        "down",
        (clusters // per,),
        [
            SMEM,
            SMEM,
            whole(*block),
            whole(1, *block),
            whole(4, *block),
            whole(*came.shape),
            whole(*apex_coupling.shape),
            whole(1, B, B),
            bases,
            bases,
            whole(*all_clusters),
            whole(clusters + 2 * HW, *block),
            *[whole(HW, *block)] * 4,
        ],
        [(sides, (rhs, clusters * B), F32)] * 2,
        (
            cluster_points,
            place,
            far_right,
            partial,
            sums,
            came,
            apex_coupling,
            slab_transfer,
            transfer,
            leaf_basis,
            near_out,
            near_back,
            pair_out,
            pair_back,
            chain_out,
            chain_back,
        ),
        us=4,
        scratch=[pltpu.VMEM((4 * rhs, 2 * B), BF)],
    )


def solution(mesh):
    return jax.shard_map(
        shards,
        mesh=mesh,
        in_specs=(
            P(None, AXES),
            P(None, AXES),
            P(AXES, None, None, None),
            P(AXES, None),
            P(AXES),
            P(AXES, None, None),
            P(AXES, None, None),
            P(AXES, None),
            P(AXES),
            P(AXES, None, None, None),
            P(AXES, None, None),
            P(),
        ),
        out_specs=(P(None, AXES), P(None, AXES)),
        check_vma=False,
    )
```

```python
import functools

import jax
import jax.numpy as jnp
import numpy as np
from jax import lax
from jax.experimental import pallas as pl
from jax.experimental.pallas import tpu as pltpu
from jax.sharding import PartitionSpec as P

B = 128
HW = 4
AXES = ("slab", "leaf")
BF = jnp.bfloat16
F32 = jnp.float32

Z, Y, X = 1, 3, 5
CORE_1 = {Y: Z, Z: Y, X: X}
STEPS = ((Y, 0), (Y, 1), (Z, 0), (Z, 1), (X, 0), (X, 1))
GATHER_STEPS = (STEPS[5], *STEPS[:5])


def routed(block, step):
    axis, turn = step
    route = []
    for i in range(lax.axis_size(AXES)):
        pairing = 1 if (i & 1) == turn else 3
        route.append((i, i ^ (pairing << (CORE_1[axis] if i & 1 else axis))))
    return lax.ppermute(block, AXES, route)


def to_other_core(block):
    return lax.ppermute(block, AXES, [(i, i ^ 1) for i in range(lax.axis_size(AXES))])


def passed_along(block, distance):
    devices = range(lax.axis_size(AXES))
    route = [(i - distance, i) for i in devices if i - distance in devices]
    return lax.ppermute(block, AXES, route)


def slot_tables(devices):
    def table(order):
        slots = np.zeros((2, devices), np.int32)
        for core in range(2):
            for difference in range(devices):
                other = difference & 1
                for place, (axis, turn) in enumerate(order):
                    axis = CORE_1[axis] if core ^ other else axis
                    low, high = (difference >> axis) & 1, (difference >> (axis + 1)) & 1
                    by_one = turn == core ^ other
                    slots[core, difference] |= (low ^ high if by_one else high) << place
                slots[core, difference] |= other << len(order)
        return jnp.asarray(slots.reshape(-1))

    return table(STEPS[::-1]), table(GATHER_STEPS)


def slot_in(table, parents, f, me, devices):
    return table[(me & 1) * devices + (parents[0, f] ^ me)]


def two(value):
    high = value.astype(BF)
    return high, (value - high.astype(F32)).astype(BF)


NN = (((1,), (0,)), ((), ()))
NT = (((1,), (1,)), ((), ()))


def dot(a, b, how):
    return lax.dot_general(a, b, how, preferred_element_type=F32)


def dot3(a, b, how):
    (ah, al), (bh, bl) = two(a), two(b)
    left = jnp.concatenate([ah, al, ah], axis=1)
    right = jnp.concatenate([bh, bh, bl], axis=1 if how is NT else 0)
    return dot(left, right, how)


def stacked(value):
    high, low = two(value)
    upper = jnp.concatenate([high, high], axis=1)
    return jnp.concatenate([upper, jnp.concatenate([low, jnp.zeros_like(low)], axis=1)], axis=0)


def both(value):
    half = value.shape[0] // 2
    return value[:half] + value[half:]


def diagonal(a, b):
    upper = jnp.concatenate([a, jnp.zeros_like(a)], axis=1)
    return jnp.concatenate([upper, jnp.concatenate([jnp.zeros_like(b), b], axis=1)], axis=0)


def pair_mask(points, c, rows):
    lane = lax.broadcasted_iota(jnp.int32, (rows, 2 * B), 1)
    return lane < jnp.where(lane < B, points[c], B + points[c + 1])


def moved(place, axis, held, at_first, at_second):
    me = place[0]
    core_0 = (me & 1) == 0
    y, z = (me >> Y) & 3, (me >> Z) & 3
    if axis == Y:
        moves = ~core_0 | (z == 3)
    elif axis == Z:
        moves = core_0 | (z == 3)
    else:
        end = jnp.where(core_0, 0, 3)
        moves = (y == end) & (z == end)
    odd = ((me >> jnp.where(core_0, axis, CORE_1[axis])) & 1) == 1
    return jnp.where(moves, jnp.where(odd, at_first, at_second), held)


def rise_kernel(
    place,
    count,
    points_hbm,
    parents_hbm,
    table_hbm,
    right_hbm,
    left_hbm,
    basis_hbm,
    transfer_hbm,
    lift_hbm,
    coupling_hbm,
    mright,
    mleft,
    pright,
    keep,
    send,
    sums,
    points,
    parents,
    table,
    right,
    left,
    basis,
    transfer,
    lift,
    coupling,
    done,
):
    rhs = right.shape[0]
    clusters = basis.shape[0]
    far_slots = coupling.shape[1]
    half = keep.shape[0] - 1
    pieces, far_pieces = 2, 4
    count_of = iter(range(done.shape[0]))

    def fetch(source, target, index):
        return pltpu.make_async_copy(source.at[index], target.at[index], done.at[next(count_of)])

    per = clusters // pieces
    early = []
    for j in range(pieces):
        some = pl.ds(j * per, per)
        columns = (slice(None), pl.ds(j * per * B, per * B))
        early.append(
            [
                fetch(right_hbm, right, columns),
                fetch(left_hbm, left, columns),
                fetch(basis_hbm, basis, some),
                fetch(transfer_hbm, transfer, some),
            ]
        )
    early[0].append(fetch(points_hbm, points, slice(None)))
    early[1].append(fetch(parents_hbm, parents, slice(None)))
    early[1].append(fetch(table_hbm, table, slice(None)))
    early[1].append(fetch(lift_hbm, lift, slice(None)))
    far_per = far_slots // far_pieces
    late = [
        fetch(coupling_hbm, coupling, (slice(None), pl.ds(j * far_per, far_per)))
        for j in range(far_pieces)
    ]
    for copy in [*early[0], *early[1]]:
        copy.start()
    keep[...] = jnp.zeros_like(keep)
    send[...] = jnp.zeros_like(send)

    part = jnp.zeros((4 * rhs, B), F32)
    for j in range(pieces):
        for copy in early[j]:
            copy.wait()
        if j == 0:
            for copy in late:
                copy.start()
        for c in range(j * per, (j + 1) * per, 2):
            mask = pair_mask(points, c, rhs)
            columns = slice(c * B, (c + 2) * B)
            xr = jnp.where(mask, right[:, columns].astype(F32), 0.0).astype(BF)
            xl = jnp.where(mask, left[:, columns].astype(F32), 0.0).astype(BF)
            for q in range(2):
                mright[c + q] = xr[:, q * B : (q + 1) * B]
                mleft[c + q] = xl[:, q * B : (q + 1) * B]
            leaf = dot(jnp.concatenate([xr, xl], axis=0), diagonal(basis[c], basis[c + 1]), NT)
            high, low = two(jnp.concatenate([transfer[c], transfer[c + 1]], axis=0))
            part = part + dot(stacked(leaf), jnp.concatenate([high, low], axis=0), NN)
    total = both(part)
    pright[0] = total[:rhs].astype(BF)
    shares = dot3(total, lift[0], NN)
    for q in range(2):
        value = shares[q * rhs : (q + 1) * rhs]
        send[half + 1 + q] = value
        sums[q] = value

    wide = stacked(total[rhs:])
    me = place[0]
    group = 8
    for j in range(far_pieces):
        late[j].wait()
        for start in range(j * far_per, (j + 1) * far_per, group):
            values = []
            for f in range(start, start + group, 2):
                (ah, al), (bh, bl) = two(coupling[0, f]), two(coupling[0, f + 1])
                high, low = (jnp.concatenate(pair, axis=1) for pair in ((ah, bh), (al, bl)))
                value = both(dot(wide, jnp.concatenate([high, low], axis=0), NN))
                values += [value[:, :B], value[:, B:]]
            for q, value in enumerate(values):
                f = start + q
                slot = slot_in(table, parents, f, me, 2 * half)
                live = f < count[0]
                own = jnp.where(live & (slot < half), slot, half)
                other = jnp.where(live & (slot >= half), slot - half, half)
                keep[own] = value
                send[other] = value

def lay_out(payload, going, exact, sums, *rest):
    high, low = two(going)
    start = going.shape[0]
    payload[:start] = high
    if exact:
        payload[start : 2 * start] = low
        start = 2 * start
    for part in (*two(sums), *rest):
        payload[start : start + part.shape[0]] = part
        start = start + part.shape[0]


def fold_kernel(step, *refs):
    refs = list(refs)
    place, came, partial, sums = refs[:4]
    del refs[:4]
    payload, keep, sums_next = refs[-5:-2]
    gathered_next, halo_next = refs[-2:]
    gathered = refs[0]
    a = gathered.shape[0]
    n = 2 * keep.shape[0]
    m = sums.shape[0]
    gathered_next[:a] = gathered[...]
    if step == 0:
        came_own, pair = refs[1:3]
        total = partial[:n] + came[:n]
        got = came[n + 1 :]
        gathered_next[a:] = came_own[...]
        other = HW * (1 - (place[0] & 1))
        halo_next[:HW] = pair[pl.ds(other, HW)]
        halo_next[HW:] = pair[pl.ds(2 * HW + other, HW)]
    else:
        halo = refs[1]
        total = partial[...] + came[:n].astype(F32)
        start = n
        if step >= 3:
            total = total + came[n : 2 * n].astype(F32)
            start = 2 * n
        got = came[start : start + m].astype(F32) + came[start + m : start + 2 * m].astype(F32)
        start = start + 2 * m
        gathered_next[a:] = came[start : start + a]
        axis, turn = STEPS[step - 1]
        if turn:
            before = refs[2]
            halo_next[...] = moved(
                place, axis, halo[...], before[before.shape[0] - 2 * HW :], came[start + a :]
            )
        else:
            halo_next[...] = halo[...]
    if sums_next.shape[0] == m:
        sums_next[...] = sums[...] + got
    else:
        sums_next[:m] = sums[...]
        sums_next[m:] = got
    keep[...] = total[: n // 2]
    parts = [halo_next[...]]
    if step < 5:
        parts = [gathered_next[...], *parts]
    lay_out(payload, total[n // 2 :], step >= 2, sums_next[...], *parts)


def rows_of(blocks, c):
    return jnp.concatenate([blocks[c, s] for s in range(blocks.shape[1])], axis=1)


def add_back(columns, first, mleft, blocks, clusters, back):
    done = []
    for c in clusters:
        places = [columns[s, c] - first[0] for s in range(blocks.shape[1])]
        done.append((places, dot(mleft[c], rows_of(blocks, c), NN)))
    for places, value in done:
        held = [back[place] for place in places]
        for s, place in enumerate(places):
            back[place] = held[s] + value[:, s * B : (s + 1) * B]


def near_outer_kernel(columns, first, mright, mleft, blocks, back, sent):
    clusters = mleft.shape[0]
    back[...] = jnp.zeros_like(back)
    add_back(columns, first, mleft, blocks, range(HW), back)
    add_back(columns, first, mleft, blocks, range(clusters - HW, clusters), back)
    sent[:HW] = mright[:HW]
    sent[HW : 2 * HW] = mright[clusters - HW :]
    sent[2 * HW : 3 * HW] = back[:HW].astype(BF)
    sent[3 * HW :] = back[clusters + HW :].astype(BF)


def near_kernel(columns, first, mright, mleft, blocks, back_outer, _, out, back):
    clusters = mright.shape[0]
    slots = blocks.shape[1]
    back[...] = back_outer[...]
    for start in range(0, clusters, 4):
        group = range(start, start + 4)
        for c in group:
            inside = []
            for s in range(slots):
                own = columns[s, c] - first[0] - HW
                value = mright[jnp.clip(own, 0, clusters - 1)]
                is_own = (own >= 0) & (own < clusters)
                inside.append(jnp.where(is_own, value, jnp.zeros_like(value)))
            out[c] = dot(rows_of(blocks, c), jnp.concatenate(inside, axis=1), NT).T
        if HW <= start < clusters - HW:
            add_back(columns, first, mleft, blocks, group, back)


def edge(low, columns, first, halo, blocks, out):
    slots = blocks.shape[1]
    clusters = columns.shape[1]
    start = jnp.where(low, 0, clusters - HW)
    row_start = first[0] + jnp.where(low, 0, clusters + HW)
    for g in range(HW):
        c = start + g
        values = []
        for s in range(slots):
            row = columns[s, c] - row_start
            value = halo[jnp.clip(row, 0, HW - 1)]
            is_there = (row >= 0) & (row < HW)
            values.append(jnp.where(is_there, value, jnp.zeros_like(value)))
        out[g] = dot(rows_of(blocks, c), jnp.concatenate(values, axis=1), NT).T


def edge_pair_kernel(place, columns, first, pair, blocks, _, out, back, halo):
    core = place[0] & 1
    halo[...] = pair[pl.ds(HW * core, HW)]
    edge(core == 1, columns, first, halo, blocks, out)
    back[...] = pair[pl.ds(2 * HW + HW * core, HW)].astype(F32)


def forward_kernel(place, count, parents, table, own, other, coupling, *rest):
    out, all_of = rest[-2:]
    far_slots = coupling.shape[1]
    half = all_of.shape[0] // 2
    all_of[:half] = own[:half]
    all_of[half:] = other[:half]
    me = place[0]
    total = jnp.zeros((B, own.shape[1]), F32)
    group = 48
    for start in range(0, far_slots, group):
        rows, values = [], []
        for f in range(start, start + group):
            value = all_of[slot_in(table, parents, f, me, 2 * half)]
            value = jnp.where(f < count[0], value, jnp.zeros_like(value))
            values += [value, value]
            rows += two(coupling[0, f])
        total = total + dot(
            jnp.concatenate(rows, axis=1), jnp.concatenate(values, axis=1), NT
        )
    out[...] = total.T


def down_kernel(
    place,
    points,
    columns,
    first,
    far_right,
    partial,
    sums,
    came,
    apex,
    lift,
    transfer,
    basis,
    near_out,
    near_back,
    pair_out,
    pair_back,
    held,
    before,
    blocks,
    product_hbm,
    adjoint_hbm,
    product,
    adjoint,
    halo,
    chain_out,
    done,
):
    clusters, rhs = near_out.shape[:2]
    core = place[0] & 1
    slab = place[0] >> X
    got = came[2:6].astype(F32) + came[6:10].astype(F32)
    slabs = [sums[2], sums[3], got[0], got[1], got[2], got[3]]
    top_right = jnp.zeros((rhs, B), F32)
    top_left = jnp.zeros((rhs, B), F32)
    for t, mask in enumerate((1 + 2 * core, 3 - 2 * core, 2)):
        top_right = top_right + dot3(slabs[2 * t], apex[slab, slab ^ mask], NT)
        top_left = top_left + dot3(slabs[2 * t + 1], apex[slab ^ mask, slab], NN)
    far_left = partial[0] + (came[0].astype(F32) + came[1].astype(F32))
    hats = stacked(
        jnp.concatenate([far_right[...], far_left], axis=0)
        + dot3(jnp.concatenate([top_right, top_left], axis=0), lift[0], NT)
    )

    message = moved(
        place, X, held[...], before[before.shape[0] - 2 * HW :], came[came.shape[0] - 2 * HW :]
    )
    halo[...] = message[:HW]
    chain_back = message[HW:].astype(F32)
    edge(core == 0, columns, first, halo, blocks, chain_out)

    pieces = done.shape[0] // 2
    per = clusters // pieces
    copies = []
    for j in range(pieces):
        for c in range(j * per, (j + 1) * per, 2):
            high, low = two(jnp.concatenate([transfer[c], transfer[c + 1]], axis=0))
            down = both(dot(hats, jnp.concatenate([high, low], axis=1), NT))
            high, low = two(down)
            two_bases = diagonal(basis[c], basis[c + 1])
            far = dot(
                jnp.concatenate([high, low], axis=1),
                jnp.concatenate([two_bases, two_bases], axis=0),
                NN,
            )
            for q in range(2):
                k, g = c + q, (c + q) % HW
                out, back = near_out[k], near_back[HW + k]
                if k < HW or k >= clusters - HW:
                    in_chip = core == (1 if k < HW else 0)
                    out = out + jnp.where(in_chip, pair_out[g], chain_out[g])
                    back = back + jnp.where(in_chip, pair_back[g], chain_back[g])
                mask = lax.broadcasted_iota(jnp.int32, (rhs, B), 1) < points[k]
                lanes = slice(q * B, (q + 1) * B)
                place_of = slice(k * B, (k + 1) * B)
                product[:, place_of] = jnp.where(mask, out + far[:rhs, lanes], 0.0)
                adjoint[:, place_of] = jnp.where(mask, back + far[rhs:, lanes], 0.0)
        index = (slice(None), pl.ds(j * per * B, per * B))
        for q, (source, target) in enumerate(((product, product_hbm), (adjoint, adjoint_hbm))):
            copy = pltpu.make_async_copy(source.at[index], target.at[index], done.at[2 * j + q])
            copy.start()
            copies.append(copy)
    for copy in copies:
        copy.wait()


SMEM = pl.BlockSpec(memory_space=pltpu.SMEM)
HBM = pl.BlockSpec(memory_space=pltpu.HBM)
ANY = pl.BlockSpec(memory_space=pl.ANY)
VMEM = pl.BlockSpec(memory_space=pltpu.VMEM)
MIB = 1024 * 1024


def shape(dims, kind):
    return jax.ShapeDtypeStruct(dims, kind)


def whole(*dims):
    return pl.BlockSpec(dims, lambda *_: (0,) * len(dims))


def call(kernel, name, grid, ins, outs, args, us, scratch=(), vmem=20):
    results = pl.pallas_call(
        kernel,
        grid=grid,
        out_shape=tuple(shape(dims, kind) for _, dims, kind in outs),
        in_specs=ins,
        out_specs=tuple(spec for spec, _, _ in outs),
        scratch_shapes=list(scratch),
        compiler_params=pltpu.CompilerParams(vmem_limit_bytes=vmem * MIB),
        cost_estimate=pl.CostEstimate(
            flops=1000, bytes_accessed=int(us * 3.6e6), transcendentals=0
        ),
        name=name,
    )(*args)
    return results


def shards(
    right_sides,
    left_sides,
    near_blocks,
    near_columns,
    cluster_points,
    leaf_basis,
    transfer,
    far_parents,
    far_count,
    coupling,
    slab_transfer,
    apex_coupling,
):
    rhs = right_sides.shape[0]
    clusters = near_blocks.shape[0]
    me = lax.axis_index(AXES)
    devices = lax.axis_size(AXES)
    block = (rhs, B)
    all_clusters = (clusters, *block)
    half = devices // 2
    place = me.astype(jnp.int32)[None]
    first = place * clusters - HW
    columns = near_columns.T
    reduce_table, gather_table = slot_tables(devices)

    def rows(n, kind=BF):
        return (VMEM, (n, *block), kind)

    def at_rest(*values):
        return [pltpu.with_memory_space_constraint(value, pltpu.HBM) for value in values]

    mright, mleft, own, partial, sent, sums = call(
        rise_kernel,
        "rise",
        (),
        [SMEM] * 2 + [HBM] * 9,
        [
            rows(clusters),
            rows(clusters),
            rows(1),
            rows(half + 1, F32),
            rows(half + 3, F32),
            rows(2, F32),
        ],
        (
            place,
            far_count,
            *at_rest(
                cluster_points,
                far_parents,
                reduce_table,
                right_sides,
                left_sides,
                leaf_basis,
                transfer,
                slab_transfer,
                coupling,
            ),
        ),
        us=5,
        scratch=[
            pltpu.SMEM(cluster_points.shape, jnp.int32),
            pltpu.SMEM(far_parents.shape, jnp.int32),
            pltpu.SMEM(reduce_table.shape, jnp.int32),
            pltpu.VMEM(right_sides.shape, BF),
            pltpu.VMEM(left_sides.shape, BF),
            pltpu.VMEM(leaf_basis.shape, BF),
            pltpu.VMEM(transfer.shape, F32),
            pltpu.VMEM(slab_transfer.shape, F32),
            pltpu.VMEM(coupling.shape, F32),
            pltpu.SemaphoreType.DMA((16,)),
        ],
    )
    came = to_other_core(sent)
    came_own = routed(own, GATHER_STEPS[0])
    back_outer, pair_sent = call(
        near_outer_kernel,
        "near_outer",
        (),
        [SMEM] * 2 + [VMEM] * 3,
        [rows(clusters + 2 * HW, F32), rows(4 * HW)],
        (columns, first, mright, mleft, near_blocks),
        us=1,
    )
    pair = to_other_core(pair_sent)

    def fold(step, came, partial, sums, gathered, *rest, after):
        n = half >> step
        m = 2 if step == 0 or STEPS[step - 1][0] != X else 4
        a = 2 << step
        size = n // 2 * (2 if step >= 2 else 1) + 2 * m + 2 * HW + (a if step < 5 else 0)
        args = (place, came, partial, sums, gathered, *rest)
        return call(
            lambda *refs: fold_kernel(step, *refs[: len(args)], *refs[len(args) + 1 :]),
            "fold",
            (),
            [SMEM] + [VMEM] * (len(args) - 1) + [ANY],
            [rows(size), rows(n // 2, F32), rows(m, F32), rows(a), rows(2 * HW)],
            (*args, after),
            us=0.3,
        )

    payload, partial, sums, gathered, halo = fold(
        0, came, partial, sums, own, came_own, pair, after=back_outer
    )
    came = routed(payload, STEPS[0])
    near_out, near_back = call(
        near_kernel,
        "near",
        (),
        [SMEM] * 2 + [VMEM] * 4 + [ANY],
        [rows(clusters, F32), rows(clusters + 2 * HW, F32)],
        (columns, first, mright, mleft, near_blocks, back_outer, payload),
        us=4,
    )
    after = near_out
    before = came
    for step in range(1, len(STEPS)):
        rest = (halo, before) if STEPS[step - 1][1] else (halo,)
        before = came
        payload, partial, sums, gathered, halo = fold(
            step, came, partial, sums, gathered, *rest, after=after
        )
        came = routed(payload, STEPS[step])
        after = payload
        if step == 1:
            pair_out, pair_back = call(
                edge_pair_kernel,
                "edge_pair",
                (),
                [SMEM] * 3 + [VMEM] * 2 + [ANY],
                [rows(HW, F32)] * 2,
                (place, columns, first, pair, near_blocks, payload),
                us=0.8,
                scratch=[pltpu.VMEM((HW, *block), BF)],
            )
            after = pair_out
    gathered_other = to_other_core(gathered)
    (far_right,) = call(
        forward_kernel,
        "forward",
        (),
        [SMEM] * 4 + [VMEM] * 7 + [ANY],
        [(VMEM, block, F32)],
        (
            place,
            far_count,
            far_parents,
            gather_table,
            gathered,
            gathered_other,
            coupling,
            apex_coupling,
            slab_transfer,
            transfer,
            leaf_basis,
            payload,
        ),
        us=2.5,
        scratch=[pltpu.VMEM((devices, *block), BF)],
    )
    wide = (rhs, clusters * B)
    return call(
        down_kernel,
        "down",
        (),
        [SMEM] * 4 + [VMEM] * 15,
        [(HBM, wide, F32)] * 2,
        (
            place,
            cluster_points,
            columns,
            first,
            far_right,
            partial,
            sums,
            came,
            apex_coupling,
            slab_transfer,
            transfer,
            leaf_basis,
            near_out,
            near_back,
            pair_out,
            pair_back,
            halo,
            before,
            near_blocks,
        ),
        us=4,
        scratch=[
            pltpu.VMEM(wide, F32),
            pltpu.VMEM(wide, F32),
            pltpu.VMEM((HW, *block), BF),
            pltpu.VMEM((HW, *block), F32),
            pltpu.SemaphoreType.DMA((8,)),
        ],
    )


def solution(mesh):
    return jax.shard_map(
        shards,
        mesh=mesh,
        in_specs=(
            P(None, AXES),
            P(None, AXES),
            P(AXES, None, None, None),
            P(AXES, None),
            P(AXES),
            P(AXES, None, None),
            P(AXES, None, None),
            P(AXES, None),
            P(AXES),
            P(AXES, None, None, None),
            P(AXES, None, None),
            P(),
        ),
        out_specs=(P(None, AXES), P(None, AXES)),
        check_vma=False,
    )
```

```python
import functools

import jax
import jax.numpy as jnp
import numpy as np
from jax import lax
from jax.experimental import pallas as pl
from jax.experimental.pallas import tpu as pltpu
from jax.sharding import PartitionSpec as P

B = 128
HW = 4
AXES = ("slab", "leaf")
BF = jnp.bfloat16
F32 = jnp.float32

Z, Y, X = 1, 3, 5
CORE_1 = {Y: Z, Z: Y, X: X}
STEPS = ((Y, 0), (Y, 1), (Z, 0), (Z, 1), (X, 0), (X, 1))
GATHER_STEPS = (STEPS[4], *STEPS[:4], STEPS[5])


def routed(block, step):
    axis, turn = step
    route = []
    for i in range(lax.axis_size(AXES)):
        pairing = 1 if (i & 1) == turn else 3
        route.append((i, i ^ (pairing << (CORE_1[axis] if i & 1 else axis))))
    return lax.ppermute(block, AXES, route)


def to_other_core(block):
    return lax.ppermute(block, AXES, [(i, i ^ 1) for i in range(lax.axis_size(AXES))])


def to_other_chips(block):
    devices = range(lax.axis_size(AXES))
    route = [(i, i + 2 - 4 * (i & 1)) for i in devices]
    return lax.ppermute(block, AXES, [(i, j) for i, j in route if j in devices])


def slot_tables(devices):
    def table(order):
        slots = np.zeros((2, devices), np.int32)
        for core in range(2):
            for difference in range(devices):
                other = difference & 1
                for place, (axis, turn) in enumerate(order):
                    axis = CORE_1[axis] if core ^ other else axis
                    low, high = (difference >> axis) & 1, (difference >> (axis + 1)) & 1
                    by_one = turn == core ^ other
                    slots[core, difference] |= (low ^ high if by_one else high) << place
                slots[core, difference] |= other << len(order)
        return jnp.asarray(slots.reshape(-1))

    return table(STEPS[::-1]), table(GATHER_STEPS)


def slot_in(table, parents, f, me, devices):
    return table[(me & 1) * devices + (parents[0, f] ^ me)]


def two(value):
    high = value.astype(BF)
    return high, (value - high.astype(F32)).astype(BF)


NN = (((1,), (0,)), ((), ()))
NT = (((1,), (1,)), ((), ()))


def dot(a, b, how):
    return lax.dot_general(a, b, how, preferred_element_type=F32)


def dot3(a, b, how):
    (ah, al), (bh, bl) = two(a), two(b)
    left = jnp.concatenate([ah, al, ah], axis=1)
    right = jnp.concatenate([bh, bh, bl], axis=1 if how is NT else 0)
    return dot(left, right, how)


def stacked(value):
    high, low = two(value)
    upper = jnp.concatenate([high, high], axis=1)
    return jnp.concatenate([upper, jnp.concatenate([low, jnp.zeros_like(low)], axis=1)], axis=0)


def both(value):
    half = value.shape[0] // 2
    return value[:half] + value[half:]


def diagonal(a, b):
    upper = jnp.concatenate([a, jnp.zeros_like(a)], axis=1)
    return jnp.concatenate([upper, jnp.concatenate([jnp.zeros_like(b), b], axis=1)], axis=0)


def pair_mask(points, c, rows):
    lane = lax.broadcasted_iota(jnp.int32, (rows, 2 * B), 1)
    return lane < jnp.where(lane < B, points[c], B + points[c + 1])


def rise_kernel(
    place,
    count,
    points_hbm,
    parents_hbm,
    table_hbm,
    right_hbm,
    left_hbm,
    basis_hbm,
    transfer_hbm,
    lift_hbm,
    coupling_hbm,
    mright,
    mleft,
    pright,
    keep,
    send,
    sums,
    points,
    parents,
    table,
    right,
    left,
    basis,
    transfer,
    lift,
    coupling,
    done,
):
    rhs = right.shape[0]
    clusters = basis.shape[0]
    far_slots = coupling.shape[1]
    half = keep.shape[0] - 1
    pieces, far_pieces = 2, 4
    count_of = iter(range(done.shape[0]))

    def fetch(source, target, index):
        return pltpu.make_async_copy(source.at[index], target.at[index], done.at[next(count_of)])

    per = clusters // pieces
    early = []
    for j in range(pieces):
        some = pl.ds(j * per, per)
        columns = (slice(None), pl.ds(j * per * B, per * B))
        early.append(
            [
                fetch(right_hbm, right, columns),
                fetch(left_hbm, left, columns),
                fetch(basis_hbm, basis, some),
                fetch(transfer_hbm, transfer, some),
            ]
        )
    early[0].append(fetch(points_hbm, points, slice(None)))
    early[1].append(fetch(parents_hbm, parents, slice(None)))
    early[1].append(fetch(table_hbm, table, slice(None)))
    early[1].append(fetch(lift_hbm, lift, slice(None)))
    far_per = far_slots // far_pieces
    late = [
        fetch(coupling_hbm, coupling, (slice(None), pl.ds(j * far_per, far_per)))
        for j in range(far_pieces)
    ]
    for copy in [*early[0], *early[1]]:
        copy.start()
    keep[...] = jnp.zeros_like(keep)
    send[...] = jnp.zeros_like(send)

    part = jnp.zeros((4 * rhs, B), F32)
    for j in range(pieces):
        for copy in early[j]:
            copy.wait()
        if j == 0:
            for copy in late:
                copy.start()
        for c in range(j * per, (j + 1) * per, 2):
            mask = pair_mask(points, c, rhs)
            columns = slice(c * B, (c + 2) * B)
            xr = jnp.where(mask, right[:, columns].astype(F32), 0.0).astype(BF)
            xl = jnp.where(mask, left[:, columns].astype(F32), 0.0).astype(BF)
            for q in range(2):
                mright[c + q] = xr[:, q * B : (q + 1) * B]
                mleft[c + q] = xl[:, q * B : (q + 1) * B]
            leaf = dot(jnp.concatenate([xr, xl], axis=0), diagonal(basis[c], basis[c + 1]), NT)
            high, low = two(jnp.concatenate([transfer[c], transfer[c + 1]], axis=0))
            part = part + dot(stacked(leaf), jnp.concatenate([high, low], axis=0), NN)
    total = both(part)
    pright[0] = total[:rhs].astype(BF)
    shares = dot3(total, lift[0], NN)
    for q in range(2):
        value = shares[q * rhs : (q + 1) * rhs]
        send[half + 1 + q] = value
        sums[q] = value

    wide = stacked(total[rhs:])
    me = place[0]
    group = 8
    for j in range(far_pieces):
        late[j].wait()
        for start in range(j * far_per, (j + 1) * far_per, group):
            values = []
            for f in range(start, start + group, 2):
                (ah, al), (bh, bl) = two(coupling[0, f]), two(coupling[0, f + 1])
                high, low = (jnp.concatenate(pair, axis=1) for pair in ((ah, bh), (al, bl)))
                value = both(dot(wide, jnp.concatenate([high, low], axis=0), NN))
                values += [value[:, :B], value[:, B:]]
            for q, value in enumerate(values):
                f = start + q
                slot = slot_in(table, parents, f, me, 2 * half)
                live = f < count[0]
                own = jnp.where(live & (slot < half), slot, half)
                other = jnp.where(live & (slot >= half), slot - half, half)
                keep[own] = value
                send[other] = value

def lay_out(payload, going, exact, sums, *rest):
    high, low = two(going)
    start = going.shape[0]
    payload[:start] = high
    if exact:
        payload[start : 2 * start] = low
        start = 2 * start
    for part in (*two(sums), *rest):
        payload[start : start + part.shape[0]] = part
        start = start + part.shape[0]


def fold_kernel(step, place, came, partial, sums, *refs):
    if step == 0:
        gathered, came_own, pair, _, payload, keep, sums_next, gathered_next, halo = refs
    elif step < 5:
        gathered, _, payload, keep, sums_next, gathered_next = refs
    else:
        gathered, _, payload, keep, sums_next = refs
    n = 2 * keep.shape[0]
    m = sums.shape[0]
    if step == 0:
        total = partial[:n] + came[:n]
        got = came[n + 1 :]
        other = HW * (1 - (place[0] & 1))
        halo[:HW] = pair[pl.ds(other, HW)]
        halo[HW:] = pair[pl.ds(2 * HW + other, HW)]
        more = came_own[...]
    else:
        total = partial[...] + came[:n].astype(F32)
        start = n
        if step >= 3:
            total = total + came[n : 2 * n].astype(F32)
            start = 2 * n
        got = came[start : start + m].astype(F32) + came[start + m : start + 2 * m].astype(F32)
        more = came[start + 2 * m :] if step < 5 else None
    if sums_next.shape[0] == m:
        sums_next[...] = sums[...] + got
    else:
        sums_next[:m] = sums[...]
        sums_next[m:] = got
    keep[...] = total[: n // 2]
    if step < 5:
        a = gathered.shape[0]
        gathered_next[:a] = gathered[...]
        gathered_next[a:] = more
    parts = [gathered if step == 5 else gathered_next] if step != 4 else []
    lay_out(payload, total[n // 2 :], step >= 2, sums_next[...], *(part[...] for part in parts))


def join_kernel(a, b, out):
    n = a.shape[0]
    out[:n] = a[...]
    out[n:] = b[b.shape[0] - n :]


def rows_of(blocks, c):
    return jnp.concatenate([blocks[c, s] for s in range(blocks.shape[1])], axis=1)


def add_back(columns, first, mleft, blocks, clusters, back):
    done = []
    for c in clusters:
        places = [columns[s, c] - first[0] for s in range(blocks.shape[1])]
        done.append((places, dot(mleft[c], rows_of(blocks, c), NN)))
    for places, value in done:
        held = [back[place] for place in places]
        for s, place in enumerate(places):
            back[place] = held[s] + value[:, s * B : (s + 1) * B]


def near_outer_kernel(columns, first, mright, mleft, blocks, back, sent):
    clusters = mleft.shape[0]
    back[...] = jnp.zeros_like(back)
    add_back(columns, first, mleft, blocks, range(HW), back)
    add_back(columns, first, mleft, blocks, range(clusters - HW, clusters), back)
    sent[:HW] = mright[:HW]
    sent[HW : 2 * HW] = mright[clusters - HW :]
    sent[2 * HW : 3 * HW] = back[:HW].astype(BF)
    sent[3 * HW :] = back[clusters + HW :].astype(BF)


def near_kernel(
    columns, first, mright, mleft, blocks, back_outer, halo, _, out, back, halo_on
):
    clusters = mright.shape[0]
    slots = blocks.shape[1]
    back[...] = back_outer[...]
    halo_on[...] = halo[...]
    for start in range(0, clusters, 4):
        group = range(start, start + 4)
        for c in group:
            inside = []
            for s in range(slots):
                own = columns[s, c] - first[0] - HW
                value = mright[jnp.clip(own, 0, clusters - 1)]
                is_own = (own >= 0) & (own < clusters)
                inside.append(jnp.where(is_own, value, jnp.zeros_like(value)))
            out[c] = dot(rows_of(blocks, c), jnp.concatenate(inside, axis=1), NT).T
        if HW <= start < clusters - HW:
            add_back(columns, first, mleft, blocks, group, back)


def edge(low, columns, first, halo, blocks, out):
    slots = blocks.shape[1]
    clusters = columns.shape[1]
    start = jnp.where(low, 0, clusters - HW)
    row_start = first[0] + jnp.where(low, 0, clusters + HW)
    for g in range(HW):
        c = start + g
        values = []
        for s in range(slots):
            row = columns[s, c] - row_start
            value = halo[jnp.clip(row, 0, HW - 1)]
            is_there = (row >= 0) & (row < HW)
            values.append(jnp.where(is_there, value, jnp.zeros_like(value)))
        out[g] = dot(rows_of(blocks, c), jnp.concatenate(values, axis=1), NT).T


def edge_pair_kernel(place, columns, first, pair, blocks, _, out, back, halo):
    core = place[0] & 1
    halo[...] = pair[pl.ds(HW * core, HW)]
    edge(core == 1, columns, first, halo, blocks, out)
    back[...] = pair[pl.ds(2 * HW + HW * core, HW)].astype(F32)


def edge_chain_kernel(place, columns, first, came, blocks, _, out, back):
    edge((place[0] & 1) == 0, columns, first, came, blocks, out)
    back[...] = came[HW:].astype(F32)


def forward_kernel(place, count, parents, table, own, other, coupling, *rest):
    out, all_of = rest[-2:]
    far_slots = coupling.shape[1]
    half = all_of.shape[0] // 2
    all_of[:half] = own[:half]
    all_of[half:] = other[:half]
    me = place[0]
    total = jnp.zeros((B, own.shape[1]), F32)
    group = 48
    for start in range(0, far_slots, group):
        rows, values = [], []
        for f in range(start, start + group):
            value = all_of[slot_in(table, parents, f, me, 2 * half)]
            value = jnp.where(f < count[0], value, jnp.zeros_like(value))
            values += [value, value]
            rows += two(coupling[0, f])
        total = total + dot(
            jnp.concatenate(rows, axis=1), jnp.concatenate(values, axis=1), NT
        )
    out[...] = total.T


def down_kernel(
    place,
    points,
    far_right,
    partial,
    sums,
    came,
    apex,
    lift,
    transfer,
    basis,
    near_out,
    near_back,
    pair_out,
    pair_back,
    chain_out,
    chain_back,
    product_hbm,
    adjoint_hbm,
    product,
    adjoint,
    done,
):
    clusters, rhs = near_out.shape[:2]
    core = place[0] & 1
    slab = place[0] >> X
    got = came[2:6].astype(F32) + came[6:10].astype(F32)
    slabs = [sums[2], sums[3], got[0], got[1], got[2], got[3]]
    top_right = jnp.zeros((rhs, B), F32)
    top_left = jnp.zeros((rhs, B), F32)
    for t, mask in enumerate((1 + 2 * core, 3 - 2 * core, 2)):
        top_right = top_right + dot3(slabs[2 * t], apex[slab, slab ^ mask], NT)
        top_left = top_left + dot3(slabs[2 * t + 1], apex[slab ^ mask, slab], NN)
    far_left = partial[0] + (came[0].astype(F32) + came[1].astype(F32))
    hats = stacked(
        jnp.concatenate([far_right[...], far_left], axis=0)
        + dot3(jnp.concatenate([top_right, top_left], axis=0), lift[0], NT)
    )

    pieces = done.shape[0] // 2
    per = clusters // pieces
    copies = []
    for j in range(pieces):
        for c in range(j * per, (j + 1) * per, 2):
            high, low = two(jnp.concatenate([transfer[c], transfer[c + 1]], axis=0))
            down = both(dot(hats, jnp.concatenate([high, low], axis=1), NT))
            high, low = two(down)
            two_bases = diagonal(basis[c], basis[c + 1])
            far = dot(
                jnp.concatenate([high, low], axis=1),
                jnp.concatenate([two_bases, two_bases], axis=0),
                NN,
            )
            for q in range(2):
                k, g = c + q, (c + q) % HW
                out, back = near_out[k], near_back[HW + k]
                if k < HW or k >= clusters - HW:
                    in_chip = core == (1 if k < HW else 0)
                    out = out + jnp.where(in_chip, pair_out[g], chain_out[g])
                    back = back + jnp.where(in_chip, pair_back[g], chain_back[g])
                mask = lax.broadcasted_iota(jnp.int32, (rhs, B), 1) < points[k]
                lanes = slice(q * B, (q + 1) * B)
                place_of = slice(k * B, (k + 1) * B)
                product[:, place_of] = jnp.where(mask, out + far[:rhs, lanes], 0.0)
                adjoint[:, place_of] = jnp.where(mask, back + far[rhs:, lanes], 0.0)
        index = (slice(None), pl.ds(j * per * B, per * B))
        for q, (source, target) in enumerate(((product, product_hbm), (adjoint, adjoint_hbm))):
            copy = pltpu.make_async_copy(source.at[index], target.at[index], done.at[2 * j + q])
            copy.start()
            copies.append(copy)
    for copy in copies:
        copy.wait()


SMEM = pl.BlockSpec(memory_space=pltpu.SMEM)
HBM = pl.BlockSpec(memory_space=pltpu.HBM)
ANY = pl.BlockSpec(memory_space=pl.ANY)
VMEM = pl.BlockSpec(memory_space=pltpu.VMEM)
MIB = 1024 * 1024


def shape(dims, kind):
    return jax.ShapeDtypeStruct(dims, kind)


def whole(*dims):
    return pl.BlockSpec(dims, lambda *_: (0,) * len(dims))


def call(kernel, name, grid, ins, outs, args, us, scratch=(), vmem=20):
    results = pl.pallas_call(
        kernel,
        grid=grid,
        out_shape=tuple(shape(dims, kind) for _, dims, kind in outs),
        in_specs=ins,
        out_specs=tuple(spec for spec, _, _ in outs),
        scratch_shapes=list(scratch),
        compiler_params=pltpu.CompilerParams(vmem_limit_bytes=vmem * MIB),
        cost_estimate=pl.CostEstimate(
            flops=1000, bytes_accessed=int(us * 3.6e6), transcendentals=0
        ),
        name=name,
    )(*args)
    return results


def shards(
    right_sides,
    left_sides,
    near_blocks,
    near_columns,
    cluster_points,
    leaf_basis,
    transfer,
    far_parents,
    far_count,
    coupling,
    slab_transfer,
    apex_coupling,
):
    rhs = right_sides.shape[0]
    clusters = near_blocks.shape[0]
    me = lax.axis_index(AXES)
    devices = lax.axis_size(AXES)
    block = (rhs, B)
    all_clusters = (clusters, *block)
    half = devices // 2
    place = me.astype(jnp.int32)[None]
    first = place * clusters - HW
    columns = near_columns.T
    reduce_table, gather_table = slot_tables(devices)

    def rows(n, kind=BF):
        return (VMEM, (n, *block), kind)

    def at_rest(*values):
        return [pltpu.with_memory_space_constraint(value, pltpu.HBM) for value in values]

    mright, mleft, own, partial, sent, sums = call(
        rise_kernel,
        "rise",
        (),
        [SMEM] * 2 + [HBM] * 9,
        [
            rows(clusters),
            rows(clusters),
            rows(1),
            rows(half + 1, F32),
            rows(half + 3, F32),
            rows(2, F32),
        ],
        (
            place,
            far_count,
            *at_rest(
                cluster_points,
                far_parents,
                reduce_table,
                right_sides,
                left_sides,
                leaf_basis,
                transfer,
                slab_transfer,
                coupling,
            ),
        ),
        us=5,
        scratch=[
            pltpu.SMEM(cluster_points.shape, jnp.int32),
            pltpu.SMEM(far_parents.shape, jnp.int32),
            pltpu.SMEM(reduce_table.shape, jnp.int32),
            pltpu.VMEM(right_sides.shape, BF),
            pltpu.VMEM(left_sides.shape, BF),
            pltpu.VMEM(leaf_basis.shape, BF),
            pltpu.VMEM(transfer.shape, F32),
            pltpu.VMEM(slab_transfer.shape, F32),
            pltpu.VMEM(coupling.shape, F32),
            pltpu.SemaphoreType.DMA((16,)),
        ],
    )
    came = to_other_core(sent)
    came_own = routed(own, GATHER_STEPS[0])
    back_outer, pair_sent = call(
        near_outer_kernel,
        "near_outer",
        (),
        [SMEM] * 2 + [VMEM] * 3,
        [rows(clusters + 2 * HW, F32), rows(4 * HW)],
        (columns, first, mright, mleft, near_blocks),
        us=1,
    )
    pair = to_other_core(pair_sent)

    def fold(step, came, partial, sums, *rest, after):
        n = half >> step
        m = 2 if step == 0 or STEPS[step - 1][0] != X else 4
        a = 2 << step
        size = n // 2 * (2 if step >= 2 else 1) + 2 * m
        size += (a, 0, half // 2)[max(step - 3, 0)]
        args = (place, came, partial, sums, *rest)
        return call(
            functools.partial(fold_kernel, step),
            "fold",
            (),
            [SMEM] + [VMEM] * (len(args) - 1) + [ANY],
            [
                rows(size),
                rows(n // 2, F32),
                rows(m, F32),
                *([rows(a)] if step < 5 else []),
                *([rows(2 * HW)] if step == 0 else []),
            ],
            (*args, after),
            us=0.3,
        )

    payload, partial, sums, gathered, halo = fold(
        0, came, partial, sums, own, came_own, pair, after=back_outer
    )
    came = routed(payload, STEPS[0])
    near_out, near_back, halo = call(
        near_kernel,
        "near",
        (),
        [SMEM] * 2 + [VMEM] * 5 + [ANY],
        [rows(clusters, F32), rows(clusters + 2 * HW, F32), rows(2 * HW)],
        (columns, first, mright, mleft, near_blocks, back_outer, halo, payload),
        us=4,
    )
    halo_came = to_other_chips(halo)
    after = near_out
    for step in range(1, 5):
        payload, partial, sums, gathered = fold(
            step, came, partial, sums, gathered, after=after
        )
        came = routed(payload, STEPS[step])
        after = payload
        if step == 1:
            pair_out, pair_back = call(
                edge_pair_kernel,
                "edge_pair",
                (),
                [SMEM] * 3 + [VMEM] * 2 + [ANY],
                [rows(HW, F32)] * 2,
                (place, columns, first, pair, near_blocks, payload),
                us=0.8,
                scratch=[pltpu.VMEM((HW, *block), BF)],
            )
            after = pair_out
    chain_out, chain_back = call(
        edge_chain_kernel,
        "edge_chain",
        (),
        [SMEM] * 3 + [VMEM] * 2 + [ANY],
        [rows(HW, F32)] * 2,
        (place, columns, first, halo_came, near_blocks, payload),
        us=0.8,
    )
    payload, partial, sums = fold(5, came, partial, sums, gathered, after=chain_out)
    came = routed(payload, STEPS[5])
    (gathered,) = call(
        join_kernel, "join", (), [VMEM] * 2, [rows(half)], (gathered, came), us=0.2
    )
    gathered_other = to_other_core(gathered)
    (far_right,) = call(
        forward_kernel,
        "forward",
        (),
        [SMEM] * 4 + [VMEM] * 7 + [ANY],
        [(VMEM, block, F32)],
        (
            place,
            far_count,
            far_parents,
            gather_table,
            gathered,
            gathered_other,
            coupling,
            apex_coupling,
            slab_transfer,
            transfer,
            leaf_basis,
            came,
        ),
        us=2.5,
        scratch=[pltpu.VMEM((devices, *block), BF)],
    )
    wide = (rhs, clusters * B)
    return call(
        down_kernel,
        "down",
        (),
        [SMEM] * 2 + [VMEM] * 14,
        [(HBM, wide, F32)] * 2,
        (
            place,
            cluster_points,
            far_right,
            partial,
            sums,
            came,
            apex_coupling,
            slab_transfer,
            transfer,
            leaf_basis,
            near_out,
            near_back,
            pair_out,
            pair_back,
            chain_out,
            chain_back,
        ),
        us=4,
        scratch=[
            pltpu.VMEM(wide, F32),
            pltpu.VMEM(wide, F32),
            pltpu.SemaphoreType.DMA((8,)),
        ],
    )


def solution(mesh):
    return jax.shard_map(
        shards,
        mesh=mesh,
        in_specs=(
            P(None, AXES),
            P(None, AXES),
            P(AXES, None, None, None),
            P(AXES, None),
            P(AXES),
            P(AXES, None, None),
            P(AXES, None, None),
            P(AXES, None),
            P(AXES),
            P(AXES, None, None, None),
            P(AXES, None, None),
            P(),
        ),
        out_specs=(P(None, AXES), P(None, AXES)),
        check_vma=False,
    )
```

```python
import functools

import jax
import jax.numpy as jnp
import numpy as np
from jax import lax
from jax.experimental import pallas as pl
from jax.experimental.pallas import tpu as pltpu
from jax.sharding import PartitionSpec as P

B = 128
HW = 4
AXES = ("slab", "leaf")
BF = jnp.bfloat16
F32 = jnp.float32

Z, Y, X = 1, 3, 5
CORE_1 = {Y: Z, Z: Y, X: X}
STEPS = ((Y, 0), (Y, 1), (Z, 0), (Z, 1), (X, 0), (X, 1))
GATHER_STEPS = (STEPS[5], *STEPS[:5])


def routed(block, step):
    axis, turn = step
    route = []
    for i in range(lax.axis_size(AXES)):
        pairing = 1 if (i & 1) == turn else 3
        route.append((i, i ^ (pairing << (CORE_1[axis] if i & 1 else axis))))
    return lax.ppermute(block, AXES, route)


def to_other_core(block):
    return lax.ppermute(block, AXES, [(i, i ^ 1) for i in range(lax.axis_size(AXES))])


def to_other_chips(block):
    devices = range(lax.axis_size(AXES))
    route = [(i, i + 2 - 4 * (i & 1)) for i in devices]
    return lax.ppermute(block, AXES, [(i, j) for i, j in route if j in devices])


def slot_tables(devices):
    def table(order):
        slots = np.zeros((2, devices), np.int32)
        for core in range(2):
            for difference in range(devices):
                other = difference & 1
                for place, (axis, turn) in enumerate(order):
                    axis = CORE_1[axis] if core ^ other else axis
                    low, high = (difference >> axis) & 1, (difference >> (axis + 1)) & 1
                    by_one = turn == core ^ other
                    slots[core, difference] |= (low ^ high if by_one else high) << place
                slots[core, difference] |= other << len(order)
        return jnp.asarray(slots.reshape(-1))

    return table(STEPS[::-1]), table(GATHER_STEPS)


def slot_in(table, parents, f, me, devices):
    return table[(me & 1) * devices + (parents[0, f] ^ me)]


def two(value):
    high = value.astype(BF)
    return high, (value - high.astype(F32)).astype(BF)


NN = (((1,), (0,)), ((), ()))
NT = (((1,), (1,)), ((), ()))


def dot(a, b, how):
    return lax.dot_general(a, b, how, preferred_element_type=F32)


def dot3(a, b, how):
    (ah, al), (bh, bl) = two(a), two(b)
    left = jnp.concatenate([ah, al, ah], axis=1)
    right = jnp.concatenate([bh, bh, bl], axis=1 if how is NT else 0)
    return dot(left, right, how)


def stacked(value):
    high, low = two(value)
    upper = jnp.concatenate([high, high], axis=1)
    return jnp.concatenate([upper, jnp.concatenate([low, jnp.zeros_like(low)], axis=1)], axis=0)


def both(value):
    half = value.shape[0] // 2
    return value[:half] + value[half:]


def diagonal(a, b):
    upper = jnp.concatenate([a, jnp.zeros_like(a)], axis=1)
    return jnp.concatenate([upper, jnp.concatenate([jnp.zeros_like(b), b], axis=1)], axis=0)


def pair_mask(points, c, rows):
    lane = lax.broadcasted_iota(jnp.int32, (rows, 2 * B), 1)
    return lane < jnp.where(lane < B, points[c], B + points[c + 1])


def rise_kernel(
    place,
    count,
    points_hbm,
    parents_hbm,
    table_hbm,
    right_hbm,
    left_hbm,
    basis_hbm,
    transfer_hbm,
    lift_hbm,
    coupling_hbm,
    mright,
    mleft,
    pright,
    keep,
    send,
    sums,
    points,
    parents,
    table,
    right,
    left,
    basis,
    transfer,
    lift,
    coupling,
    done,
):
    rhs = right.shape[0]
    clusters = basis.shape[0]
    far_slots = coupling.shape[1]
    half = keep.shape[0] - 1
    pieces, far_pieces = 2, 4
    count_of = iter(range(done.shape[0]))

    def fetch(source, target, index):
        return pltpu.make_async_copy(source.at[index], target.at[index], done.at[next(count_of)])

    per = clusters // pieces
    early = []
    for j in range(pieces):
        some = pl.ds(j * per, per)
        columns = (slice(None), pl.ds(j * per * B, per * B))
        early.append(
            [
                fetch(right_hbm, right, columns),
                fetch(left_hbm, left, columns),
                fetch(basis_hbm, basis, some),
                fetch(transfer_hbm, transfer, some),
            ]
        )
    early[0].append(fetch(points_hbm, points, slice(None)))
    early[1].append(fetch(parents_hbm, parents, slice(None)))
    early[1].append(fetch(table_hbm, table, slice(None)))
    early[1].append(fetch(lift_hbm, lift, slice(None)))
    far_per = far_slots // far_pieces
    late = [
        fetch(coupling_hbm, coupling, (slice(None), pl.ds(j * far_per, far_per)))
        for j in range(far_pieces)
    ]
    for copy in [*early[0], *early[1]]:
        copy.start()
    keep[...] = jnp.zeros_like(keep)
    send[...] = jnp.zeros_like(send)

    part = jnp.zeros((4 * rhs, B), F32)
    for j in range(pieces):
        for copy in early[j]:
            copy.wait()
        if j == 0:
            for copy in late:
                copy.start()
        for c in range(j * per, (j + 1) * per, 2):
            mask = pair_mask(points, c, rhs)
            columns = slice(c * B, (c + 2) * B)
            xr = jnp.where(mask, right[:, columns].astype(F32), 0.0).astype(BF)
            xl = jnp.where(mask, left[:, columns].astype(F32), 0.0).astype(BF)
            for q in range(2):
                mright[c + q] = xr[:, q * B : (q + 1) * B]
                mleft[c + q] = xl[:, q * B : (q + 1) * B]
            leaf = dot(jnp.concatenate([xr, xl], axis=0), diagonal(basis[c], basis[c + 1]), NT)
            high, low = two(jnp.concatenate([transfer[c], transfer[c + 1]], axis=0))
            part = part + dot(stacked(leaf), jnp.concatenate([high, low], axis=0), NN)
    total = both(part)
    pright[0] = total[:rhs].astype(BF)
    shares = dot3(total, lift[0], NN)
    for q in range(2):
        value = shares[q * rhs : (q + 1) * rhs]
        send[half + 1 + q] = value
        sums[q] = value

    wide = stacked(total[rhs:])
    me = place[0]
    group = 8
    for j in range(far_pieces):
        late[j].wait()
        for start in range(j * far_per, (j + 1) * far_per, group):
            values = []
            for f in range(start, start + group, 2):
                (ah, al), (bh, bl) = two(coupling[0, f]), two(coupling[0, f + 1])
                high, low = (jnp.concatenate(pair, axis=1) for pair in ((ah, bh), (al, bl)))
                value = both(dot(wide, jnp.concatenate([high, low], axis=0), NN))
                values += [value[:, :B], value[:, B:]]
            for q, value in enumerate(values):
                f = start + q
                slot = slot_in(table, parents, f, me, 2 * half)
                live = f < count[0]
                own = jnp.where(live & (slot < half), slot, half)
                other = jnp.where(live & (slot >= half), slot - half, half)
                keep[own] = value
                send[other] = value

def lay_out(payload, going, exact, sums, *rest):
    high, low = two(going)
    start = going.shape[0]
    payload[:start] = high
    if exact:
        payload[start : 2 * start] = low
        start = 2 * start
    for part in (*two(sums), *rest):
        payload[start : start + part.shape[0]] = part
        start = start + part.shape[0]


def fold_kernel(step, came, partial, sums, *refs):
    gathered = refs[0]
    payload, keep, sums_next, gathered_next = refs[-4:]
    n = 2 * keep.shape[0]
    m = sums.shape[0]
    if step == 0:
        total = partial[:n] + came[:n]
        got = came[n + 1 :]
        more = refs[1][...]
    else:
        total = partial[...] + came[:n].astype(F32)
        start = n
        if step >= 3:
            total = total + came[n : 2 * n].astype(F32)
            start = 2 * n
        got = came[start : start + m].astype(F32) + came[start + m : start + 2 * m].astype(F32)
        more = came[start + 2 * m :]
    if sums_next.shape[0] == m:
        sums_next[...] = sums[...] + got
    else:
        sums_next[:m] = sums[...]
        sums_next[m:] = got
    keep[...] = total[: n // 2]
    a = gathered.shape[0]
    gathered_next[:a] = gathered[...]
    gathered_next[a:] = more
    parts = [gathered_next[...]] if step < 5 else []
    lay_out(payload, total[n // 2 :], step >= 2, sums_next[...], *parts)


def rows_of(blocks, c):
    return jnp.concatenate([blocks[c, s] for s in range(blocks.shape[1])], axis=1)


def add_back(columns, first, mleft, blocks, clusters, back):
    done = []
    for c in clusters:
        places = [columns[s, c] - first[0] for s in range(blocks.shape[1])]
        done.append((places, dot(mleft[c], rows_of(blocks, c), NN)))
    for places, value in done:
        held = [back[place] for place in places]
        for s, place in enumerate(places):
            back[place] = held[s] + value[:, s * B : (s + 1) * B]


def near_kernel(columns, first, mright, mleft, blocks, _, out, back, sent):
    clusters = mright.shape[0]
    slots = blocks.shape[1]
    back[...] = jnp.zeros_like(back)
    for start in range(0, clusters, 4):
        group = range(start, start + 4)
        for c in group:
            inside = []
            for s in range(slots):
                own = columns[s, c] - first[0] - HW
                value = mright[jnp.clip(own, 0, clusters - 1)]
                is_own = (own >= 0) & (own < clusters)
                inside.append(jnp.where(is_own, value, jnp.zeros_like(value)))
            out[c] = dot(rows_of(blocks, c), jnp.concatenate(inside, axis=1), NT).T
        add_back(columns, first, mleft, blocks, group, back)
    sent[:HW] = mright[:HW]
    sent[HW : 2 * HW] = mright[clusters - HW :]
    sent[2 * HW : 3 * HW] = back[:HW].astype(BF)
    sent[3 * HW :] = back[clusters + HW :].astype(BF)


def edge(low, columns, first, halo, blocks, out):
    slots = blocks.shape[1]
    clusters = columns.shape[1]
    start = jnp.where(low, 0, clusters - HW)
    row_start = first[0] + jnp.where(low, 0, clusters + HW)
    for g in range(HW):
        c = start + g
        values = []
        for s in range(slots):
            row = columns[s, c] - row_start
            value = halo[jnp.clip(row, 0, HW - 1)]
            is_there = (row >= 0) & (row < HW)
            values.append(jnp.where(is_there, value, jnp.zeros_like(value)))
        out[g] = dot(rows_of(blocks, c), jnp.concatenate(values, axis=1), NT).T


def edge_pair_kernel(place, columns, first, pair, blocks, _, out, back, message, halo):
    core = place[0] & 1
    message[:HW] = pair[pl.ds(HW * (1 - core), HW)]
    message[HW:] = pair[pl.ds(2 * HW + HW * (1 - core), HW)]
    halo[...] = pair[pl.ds(HW * core, HW)]
    edge(core == 1, columns, first, halo, blocks, out)
    back[...] = pair[pl.ds(2 * HW + HW * core, HW)].astype(F32)


def edge_chain_kernel(place, columns, first, came, blocks, _, out, back):
    edge((place[0] & 1) == 0, columns, first, came, blocks, out)
    back[...] = came[HW:].astype(F32)


def forward_kernel(place, count, parents, table, own, other, coupling, *rest):
    out, all_of = rest[-2:]
    far_slots = coupling.shape[1]
    half = all_of.shape[0] // 2
    all_of[:half] = own[:half]
    all_of[half:] = other[:half]
    me = place[0]
    total = jnp.zeros((B, own.shape[1]), F32)
    group = 48
    for start in range(0, far_slots, group):
        rows, values = [], []
        for f in range(start, start + group):
            value = all_of[slot_in(table, parents, f, me, 2 * half)]
            value = jnp.where(f < count[0], value, jnp.zeros_like(value))
            values += [value, value]
            rows += two(coupling[0, f])
        total = total + dot(
            jnp.concatenate(rows, axis=1), jnp.concatenate(values, axis=1), NT
        )
    out[...] = total.T


def down_kernel(
    place,
    points,
    far_right,
    partial,
    sums,
    came,
    apex,
    lift,
    transfer,
    basis,
    near_out,
    near_back,
    pair_out,
    pair_back,
    chain_out,
    chain_back,
    product_hbm,
    adjoint_hbm,
    product,
    adjoint,
    done,
):
    clusters, rhs = near_out.shape[:2]
    core = place[0] & 1
    slab = place[0] >> X
    got = came[2:6].astype(F32) + came[6:10].astype(F32)
    slabs = [sums[2], sums[3], got[0], got[1], got[2], got[3]]
    top_right = jnp.zeros((rhs, B), F32)
    top_left = jnp.zeros((rhs, B), F32)
    for t, mask in enumerate((1 + 2 * core, 3 - 2 * core, 2)):
        top_right = top_right + dot3(slabs[2 * t], apex[slab, slab ^ mask], NT)
        top_left = top_left + dot3(slabs[2 * t + 1], apex[slab ^ mask, slab], NN)
    far_left = partial[0] + (came[0].astype(F32) + came[1].astype(F32))
    hats = stacked(
        jnp.concatenate([far_right[...], far_left], axis=0)
        + dot3(jnp.concatenate([top_right, top_left], axis=0), lift[0], NT)
    )

    pieces = done.shape[0] // 2
    per = clusters // pieces
    copies = []
    for j in range(pieces):
        for c in range(j * per, (j + 1) * per, 2):
            high, low = two(jnp.concatenate([transfer[c], transfer[c + 1]], axis=0))
            down = both(dot(hats, jnp.concatenate([high, low], axis=1), NT))
            high, low = two(down)
            two_bases = diagonal(basis[c], basis[c + 1])
            far = dot(
                jnp.concatenate([high, low], axis=1),
                jnp.concatenate([two_bases, two_bases], axis=0),
                NN,
            )
            for q in range(2):
                k, g = c + q, (c + q) % HW
                out, back = near_out[k], near_back[HW + k]
                if k < HW or k >= clusters - HW:
                    in_chip = core == (1 if k < HW else 0)
                    out = out + jnp.where(in_chip, pair_out[g], chain_out[g])
                    back = back + jnp.where(in_chip, pair_back[g], chain_back[g])
                mask = lax.broadcasted_iota(jnp.int32, (rhs, B), 1) < points[k]
                lanes = slice(q * B, (q + 1) * B)
                place_of = slice(k * B, (k + 1) * B)
                product[:, place_of] = jnp.where(mask, out + far[:rhs, lanes], 0.0)
                adjoint[:, place_of] = jnp.where(mask, back + far[rhs:, lanes], 0.0)
        index = (slice(None), pl.ds(j * per * B, per * B))
        for q, (source, target) in enumerate(((product, product_hbm), (adjoint, adjoint_hbm))):
            copy = pltpu.make_async_copy(source.at[index], target.at[index], done.at[2 * j + q])
            copy.start()
            copies.append(copy)
    for copy in copies:
        copy.wait()


SMEM = pl.BlockSpec(memory_space=pltpu.SMEM)
HBM = pl.BlockSpec(memory_space=pltpu.HBM)
ANY = pl.BlockSpec(memory_space=pl.ANY)
VMEM = pl.BlockSpec(memory_space=pltpu.VMEM)
MIB = 1024 * 1024


def shape(dims, kind):
    return jax.ShapeDtypeStruct(dims, kind)


def whole(*dims):
    return pl.BlockSpec(dims, lambda *_: (0,) * len(dims))


def call(kernel, name, grid, ins, outs, args, us, scratch=(), vmem=20):
    results = pl.pallas_call(
        kernel,
        grid=grid,
        out_shape=tuple(shape(dims, kind) for _, dims, kind in outs),
        in_specs=ins,
        out_specs=tuple(spec for spec, _, _ in outs),
        scratch_shapes=list(scratch),
        compiler_params=pltpu.CompilerParams(vmem_limit_bytes=vmem * MIB),
        cost_estimate=pl.CostEstimate(
            flops=1000, bytes_accessed=int(us * 3.6e6), transcendentals=0
        ),
        name=name,
    )(*args)
    return results


def shards(
    right_sides,
    left_sides,
    near_blocks,
    near_columns,
    cluster_points,
    leaf_basis,
    transfer,
    far_parents,
    far_count,
    coupling,
    slab_transfer,
    apex_coupling,
):
    rhs = right_sides.shape[0]
    clusters = near_blocks.shape[0]
    me = lax.axis_index(AXES)
    devices = lax.axis_size(AXES)
    block = (rhs, B)
    all_clusters = (clusters, *block)
    half = devices // 2
    place = me.astype(jnp.int32)[None]
    first = place * clusters - HW
    columns = near_columns.T
    reduce_table, gather_table = slot_tables(devices)

    def rows(n, kind=BF):
        return (VMEM, (n, *block), kind)

    def at_rest(*values):
        return [pltpu.with_memory_space_constraint(value, pltpu.HBM) for value in values]

    mright, mleft, own, partial, sent, sums = call(
        rise_kernel,
        "rise",
        (),
        [SMEM] * 2 + [HBM] * 9,
        [
            rows(clusters),
            rows(clusters),
            rows(1),
            rows(half + 1, F32),
            rows(half + 3, F32),
            rows(2, F32),
        ],
        (
            place,
            far_count,
            *at_rest(
                cluster_points,
                far_parents,
                reduce_table,
                right_sides,
                left_sides,
                leaf_basis,
                transfer,
                slab_transfer,
                coupling,
            ),
        ),
        us=5,
        scratch=[
            pltpu.SMEM(cluster_points.shape, jnp.int32),
            pltpu.SMEM(far_parents.shape, jnp.int32),
            pltpu.SMEM(reduce_table.shape, jnp.int32),
            pltpu.VMEM(right_sides.shape, BF),
            pltpu.VMEM(left_sides.shape, BF),
            pltpu.VMEM(leaf_basis.shape, BF),
            pltpu.VMEM(transfer.shape, F32),
            pltpu.VMEM(slab_transfer.shape, F32),
            pltpu.VMEM(coupling.shape, F32),
            pltpu.SemaphoreType.DMA((16,)),
        ],
    )
    came = to_other_core(sent)
    came_own = routed(own, GATHER_STEPS[0])
    def fold(step, came, partial, sums, *rest, after):
        n = half >> step
        m = 2 if step == 0 or STEPS[step - 1][0] != X else 4
        a = 2 << step
        size = n // 2 * (2 if step >= 2 else 1) + 2 * m + (a if step < 5 else 0)
        args = (came, partial, sums, *rest)
        return call(
            functools.partial(fold_kernel, step),
            "fold",
            (),
            [VMEM] * len(args) + [ANY],
            [rows(size), rows(n // 2, F32), rows(m, F32), rows(a)],
            (*args, after),
            us=0.3,
        )

    payload, partial, sums, gathered = fold(0, came, partial, sums, own, came_own, after=own)
    came = routed(payload, STEPS[0])
    near_out, near_back, pair_sent = call(
        near_kernel,
        "near",
        (),
        [SMEM] * 2 + [VMEM] * 3 + [ANY],
        [rows(clusters, F32), rows(clusters + 2 * HW, F32), rows(4 * HW)],
        (columns, first, mright, mleft, near_blocks, payload),
        us=5,
    )
    pair = to_other_core(pair_sent)
    after = near_out
    for step in range(1, len(STEPS)):
        payload, partial, sums, gathered = fold(
            step, came, partial, sums, gathered, after=after
        )
        came = routed(payload, STEPS[step])
        after = payload
        if step == 2:
            pair_out, pair_back, message = call(
                edge_pair_kernel,
                "edge_pair",
                (),
                [SMEM] * 3 + [VMEM] * 2 + [ANY],
                [rows(HW, F32)] * 2 + [rows(2 * HW)],
                (place, columns, first, pair, near_blocks, payload),
                us=0.8,
                scratch=[pltpu.VMEM((HW, *block), BF)],
            )
            after = pair_out
            halo_came = to_other_chips(message)
        if step == 4:
            chain_out, chain_back = call(
                edge_chain_kernel,
                "edge_chain",
                (),
                [SMEM] * 3 + [VMEM] * 2 + [ANY],
                [rows(HW, F32)] * 2,
                (place, columns, first, halo_came, near_blocks, payload),
                us=0.8,
            )
            after = chain_out
    gathered_other = to_other_core(gathered)
    (far_right,) = call(
        forward_kernel,
        "forward",
        (),
        [SMEM] * 4 + [VMEM] * 7 + [ANY],
        [(VMEM, block, F32)],
        (
            place,
            far_count,
            far_parents,
            gather_table,
            gathered,
            gathered_other,
            coupling,
            apex_coupling,
            slab_transfer,
            transfer,
            leaf_basis,
            payload,
        ),
        us=2.5,
        scratch=[pltpu.VMEM((devices, *block), BF)],
    )
    wide = (rhs, clusters * B)
    return call(
        down_kernel,
        "down",
        (),
        [SMEM] * 2 + [VMEM] * 14,
        [(HBM, wide, F32)] * 2,
        (
            place,
            cluster_points,
            far_right,
            partial,
            sums,
            came,
            apex_coupling,
            slab_transfer,
            transfer,
            leaf_basis,
            near_out,
            near_back,
            pair_out,
            pair_back,
            chain_out,
            chain_back,
        ),
        us=4,
        scratch=[
            pltpu.VMEM(wide, F32),
            pltpu.VMEM(wide, F32),
            pltpu.SemaphoreType.DMA((8,)),
        ],
    )


def solution(mesh):
    return jax.shard_map(
        shards,
        mesh=mesh,
        in_specs=(
            P(None, AXES),
            P(None, AXES),
            P(AXES, None, None, None),
            P(AXES, None),
            P(AXES),
            P(AXES, None, None),
            P(AXES, None, None),
            P(AXES, None),
            P(AXES),
            P(AXES, None, None, None),
            P(AXES, None, None),
            P(),
        ),
        out_specs=(P(None, AXES), P(None, AXES)),
        check_vma=False,
    )
```

```python
import functools

import jax
import jax.numpy as jnp
import numpy as np
from jax import lax
from jax.experimental import pallas as pl
from jax.experimental.pallas import tpu as pltpu
from jax.sharding import PartitionSpec as P

B = 128
HW = 4
AXES = ("slab", "leaf")
BF = jnp.bfloat16
F32 = jnp.float32

Z, Y, X = 1, 3, 5
CORE_1 = {Y: Z, Z: Y, X: X}
STEPS = ((Y, 0), (Y, 1), (Z, 0), (Z, 1), (X, 0), (X, 1))
GATHER_STEPS = (STEPS[5], *STEPS[:5])


def routed(block, step):
    axis, turn = step
    route = []
    for i in range(lax.axis_size(AXES)):
        pairing = 1 if (i & 1) == turn else 3
        route.append((i, i ^ (pairing << (CORE_1[axis] if i & 1 else axis))))
    return lax.ppermute(block, AXES, route)


def to_other_core(block):
    return lax.ppermute(block, AXES, [(i, i ^ 1) for i in range(lax.axis_size(AXES))])


def to_other_chips(block):
    devices = range(lax.axis_size(AXES))
    route = [(i, i - 1 + 2 * (i & 1)) for i in devices]
    return lax.ppermute(block, AXES, [(i, j) for i, j in route if j in devices])


def slot_tables(devices):
    def table(order):
        slots = np.zeros((2, devices), np.int32)
        for core in range(2):
            for difference in range(devices):
                other = difference & 1
                for place, (axis, turn) in enumerate(order):
                    axis = CORE_1[axis] if core ^ other else axis
                    low, high = (difference >> axis) & 1, (difference >> (axis + 1)) & 1
                    by_one = turn == core ^ other
                    slots[core, difference] |= (low ^ high if by_one else high) << place
                slots[core, difference] |= other << len(order)
        return jnp.asarray(slots.reshape(-1))

    return table(STEPS[::-1]), table(GATHER_STEPS)


def slot_in(table, parents, f, me, devices):
    return table[(me & 1) * devices + (parents[0, f] ^ me)]


def two(value):
    high = value.astype(BF)
    return high, (value - high.astype(F32)).astype(BF)


NN = (((1,), (0,)), ((), ()))
NT = (((1,), (1,)), ((), ()))


def dot(a, b, how):
    return lax.dot_general(a, b, how, preferred_element_type=F32)


def dot3(a, b, how):
    (ah, al), (bh, bl) = two(a), two(b)
    left = jnp.concatenate([ah, al, ah], axis=1)
    right = jnp.concatenate([bh, bh, bl], axis=1 if how is NT else 0)
    return dot(left, right, how)


def stacked(value):
    high, low = two(value)
    upper = jnp.concatenate([high, high], axis=1)
    return jnp.concatenate([upper, jnp.concatenate([low, jnp.zeros_like(low)], axis=1)], axis=0)


def both(value):
    half = value.shape[0] // 2
    return value[:half] + value[half:]


def diagonal(a, b):
    upper = jnp.concatenate([a, jnp.zeros_like(a)], axis=1)
    return jnp.concatenate([upper, jnp.concatenate([jnp.zeros_like(b), b], axis=1)], axis=0)


def pair_mask(points, c, rows):
    lane = lax.broadcasted_iota(jnp.int32, (rows, 2 * B), 1)
    return lane < jnp.where(lane < B, points[c], B + points[c + 1])


def rise_kernel(
    place,
    count,
    points_hbm,
    parents_hbm,
    table_hbm,
    right_hbm,
    left_hbm,
    basis_hbm,
    transfer_hbm,
    lift_hbm,
    coupling_hbm,
    mright,
    mleft,
    pright,
    keep,
    send,
    sums,
    points,
    parents,
    table,
    right,
    left,
    basis,
    transfer,
    lift,
    coupling,
    done,
):
    rhs = right.shape[0]
    clusters = basis.shape[0]
    far_slots = coupling.shape[1]
    half = keep.shape[0] - 1
    pieces, far_pieces = 2, 4
    count_of = iter(range(done.shape[0]))

    def fetch(source, target, index):
        return pltpu.make_async_copy(source.at[index], target.at[index], done.at[next(count_of)])

    per = clusters // pieces
    early = []
    for j in range(pieces):
        some = pl.ds(j * per, per)
        columns = (slice(None), pl.ds(j * per * B, per * B))
        early.append(
            [
                fetch(right_hbm, right, columns),
                fetch(left_hbm, left, columns),
                fetch(basis_hbm, basis, some),
                fetch(transfer_hbm, transfer, some),
            ]
        )
    early[0].append(fetch(points_hbm, points, slice(None)))
    early[1].append(fetch(parents_hbm, parents, slice(None)))
    early[1].append(fetch(table_hbm, table, slice(None)))
    early[1].append(fetch(lift_hbm, lift, slice(None)))
    far_per = far_slots // far_pieces
    late = [
        fetch(coupling_hbm, coupling, (slice(None), pl.ds(j * far_per, far_per)))
        for j in range(far_pieces)
    ]
    for copy in [*early[0], *early[1]]:
        copy.start()
    keep[...] = jnp.zeros_like(keep)
    send[...] = jnp.zeros_like(send)

    part = jnp.zeros((4 * rhs, B), F32)
    for j in range(pieces):
        for copy in early[j]:
            copy.wait()
        if j == 0:
            for copy in late:
                copy.start()
        for c in range(j * per, (j + 1) * per, 2):
            mask = pair_mask(points, c, rhs)
            columns = slice(c * B, (c + 2) * B)
            xr = jnp.where(mask, right[:, columns].astype(F32), 0.0).astype(BF)
            xl = jnp.where(mask, left[:, columns].astype(F32), 0.0).astype(BF)
            for q in range(2):
                mright[c + q] = xr[:, q * B : (q + 1) * B]
                mleft[c + q] = xl[:, q * B : (q + 1) * B]
            leaf = dot(jnp.concatenate([xr, xl], axis=0), diagonal(basis[c], basis[c + 1]), NT)
            high, low = two(jnp.concatenate([transfer[c], transfer[c + 1]], axis=0))
            part = part + dot(stacked(leaf), jnp.concatenate([high, low], axis=0), NN)
    total = both(part)
    pright[0] = total[:rhs].astype(BF)
    shares = dot3(total, lift[0], NN)
    for q in range(2):
        value = shares[q * rhs : (q + 1) * rhs]
        send[half + 1 + q] = value
        sums[q] = value

    wide = stacked(total[rhs:])
    me = place[0]
    group = 8
    for j in range(far_pieces):
        late[j].wait()
        for start in range(j * far_per, (j + 1) * far_per, group):
            values = []
            for f in range(start, start + group, 2):
                (ah, al), (bh, bl) = two(coupling[0, f]), two(coupling[0, f + 1])
                high, low = (jnp.concatenate(pair, axis=1) for pair in ((ah, bh), (al, bl)))
                value = both(dot(wide, jnp.concatenate([high, low], axis=0), NN))
                values += [value[:, :B], value[:, B:]]
            for q, value in enumerate(values):
                f = start + q
                slot = slot_in(table, parents, f, me, 2 * half)
                live = f < count[0]
                own = jnp.where(live & (slot < half), slot, half)
                other = jnp.where(live & (slot >= half), slot - half, half)
                keep[own] = value
                send[other] = value

def lay_out(payload, going, exact, sums, *rest):
    high, low = two(going)
    start = going.shape[0]
    payload[:start] = high
    if exact:
        payload[start : 2 * start] = low
        start = 2 * start
    for part in (*two(sums), *rest):
        payload[start : start + part.shape[0]] = part
        start = start + part.shape[0]


def fold_kernel(step, came, partial, sums, *refs):
    gathered = refs[0]
    payload, keep, sums_next, gathered_next = refs[-4:]
    n = 2 * keep.shape[0]
    m = sums.shape[0]
    if step == 0:
        total = partial[:n] + came[:n]
        got = came[n + 1 :]
        more = refs[1][...]
    else:
        total = partial[...] + came[:n].astype(F32)
        start = n
        if step >= 3:
            total = total + came[n : 2 * n].astype(F32)
            start = 2 * n
        got = came[start : start + m].astype(F32) + came[start + m : start + 2 * m].astype(F32)
        more = came[start + 2 * m :]
    if sums_next.shape[0] == m:
        sums_next[...] = sums[...] + got
    else:
        sums_next[:m] = sums[...]
        sums_next[m:] = got
    keep[...] = total[: n // 2]
    a = gathered.shape[0]
    gathered_next[:a] = gathered[...]
    gathered_next[a:] = more
    parts = [gathered_next[...]] if step < 5 else []
    lay_out(payload, total[n // 2 :], step >= 2, sums_next[...], *parts)


def rows_of(blocks, c):
    return jnp.concatenate([blocks[c, s] for s in range(blocks.shape[1])], axis=1)


def add_back(columns, first, mleft, blocks, clusters, back):
    done = []
    for c in clusters:
        places = [columns[s, c] - first[0] for s in range(blocks.shape[1])]
        done.append((places, dot(mleft[c], rows_of(blocks, c), NN)))
    for places, value in done:
        held = [back[place] for place in places]
        for s, place in enumerate(places):
            back[place] = held[s] + value[:, s * B : (s + 1) * B]


def near_kernel(place, columns, first, mright, mleft, blocks, _, out, back, to_chip, to_core):
    clusters = mright.shape[0]
    slots = blocks.shape[1]
    back[...] = jnp.zeros_like(back)
    for start in range(0, clusters, 4):
        group = range(start, start + 4)
        for c in group:
            inside = []
            for s in range(slots):
                own = columns[s, c] - first[0] - HW
                value = mright[jnp.clip(own, 0, clusters - 1)]
                is_own = (own >= 0) & (own < clusters)
                inside.append(jnp.where(is_own, value, jnp.zeros_like(value)))
            out[c] = dot(rows_of(blocks, c), jnp.concatenate(inside, axis=1), NT).T
        add_back(columns, first, mleft, blocks, group, back)
    core = place[0] & 1
    for side, sent in ((core, to_chip), (1 - core, to_core)):
        sent[:HW] = mright[pl.ds(side * (clusters - HW), HW)]
        sent[HW:] = back[pl.ds(side * (clusters + HW), HW)].astype(BF)


def edge(low, columns, first, halo, blocks, out):
    slots = blocks.shape[1]
    clusters = columns.shape[1]
    start = jnp.where(low, 0, clusters - HW)
    row_start = first[0] + jnp.where(low, 0, clusters + HW)
    for g in range(HW):
        c = start + g
        values = []
        for s in range(slots):
            row = columns[s, c] - row_start
            value = halo[jnp.clip(row, 0, HW - 1)]
            is_there = (row >= 0) & (row < HW)
            values.append(jnp.where(is_there, value, jnp.zeros_like(value)))
        out[g] = dot(rows_of(blocks, c), jnp.concatenate(values, axis=1), NT).T


def edge_kernel(low_core, place, columns, first, came, blocks, _, out, back):
    edge((place[0] & 1) == low_core, columns, first, came, blocks, out)
    back[...] = came[HW:].astype(F32)


def forward_kernel(place, count, parents, table, own, other, coupling, *rest):
    out, all_of = rest[-2:]
    far_slots = coupling.shape[1]
    half = all_of.shape[0] // 2
    all_of[:half] = own[:half]
    all_of[half:] = other[:half]
    me = place[0]
    total = jnp.zeros((B, own.shape[1]), F32)
    group = 48
    for start in range(0, far_slots, group):
        rows, values = [], []
        for f in range(start, start + group):
            value = all_of[slot_in(table, parents, f, me, 2 * half)]
            value = jnp.where(f < count[0], value, jnp.zeros_like(value))
            values += [value, value]
            rows += two(coupling[0, f])
        total = total + dot(
            jnp.concatenate(rows, axis=1), jnp.concatenate(values, axis=1), NT
        )
    out[...] = total.T


def down_kernel(
    place,
    points,
    far_right,
    partial,
    sums,
    came,
    apex,
    lift,
    transfer,
    basis,
    near_out,
    near_back,
    pair_out,
    pair_back,
    chain_out,
    chain_back,
    product_hbm,
    adjoint_hbm,
    product,
    adjoint,
    done,
):
    clusters, rhs = near_out.shape[:2]
    core = place[0] & 1
    slab = place[0] >> X
    got = came[2:6].astype(F32) + came[6:10].astype(F32)
    slabs = [sums[2], sums[3], got[0], got[1], got[2], got[3]]
    top_right = jnp.zeros((rhs, B), F32)
    top_left = jnp.zeros((rhs, B), F32)
    for t, mask in enumerate((1 + 2 * core, 3 - 2 * core, 2)):
        top_right = top_right + dot3(slabs[2 * t], apex[slab, slab ^ mask], NT)
        top_left = top_left + dot3(slabs[2 * t + 1], apex[slab ^ mask, slab], NN)
    far_left = partial[0] + (came[0].astype(F32) + came[1].astype(F32))
    hats = stacked(
        jnp.concatenate([far_right[...], far_left], axis=0)
        + dot3(jnp.concatenate([top_right, top_left], axis=0), lift[0], NT)
    )

    pieces = done.shape[0] // 2
    per = clusters // pieces
    copies = []
    for j in range(pieces):
        for c in range(j * per, (j + 1) * per, 2):
            high, low = two(jnp.concatenate([transfer[c], transfer[c + 1]], axis=0))
            down = both(dot(hats, jnp.concatenate([high, low], axis=1), NT))
            high, low = two(down)
            two_bases = diagonal(basis[c], basis[c + 1])
            far = dot(
                jnp.concatenate([high, low], axis=1),
                jnp.concatenate([two_bases, two_bases], axis=0),
                NN,
            )
            for q in range(2):
                k, g = c + q, (c + q) % HW
                out, back = near_out[k], near_back[HW + k]
                if k < HW or k >= clusters - HW:
                    in_chip = core == (1 if k < HW else 0)
                    out = out + jnp.where(in_chip, pair_out[g], chain_out[g])
                    back = back + jnp.where(in_chip, pair_back[g], chain_back[g])
                mask = lax.broadcasted_iota(jnp.int32, (rhs, B), 1) < points[k]
                lanes = slice(q * B, (q + 1) * B)
                place_of = slice(k * B, (k + 1) * B)
                product[:, place_of] = jnp.where(mask, out + far[:rhs, lanes], 0.0)
                adjoint[:, place_of] = jnp.where(mask, back + far[rhs:, lanes], 0.0)
        index = (slice(None), pl.ds(j * per * B, per * B))
        for q, (source, target) in enumerate(((product, product_hbm), (adjoint, adjoint_hbm))):
            copy = pltpu.make_async_copy(source.at[index], target.at[index], done.at[2 * j + q])
            copy.start()
            copies.append(copy)
    for copy in copies:
        copy.wait()


SMEM = pl.BlockSpec(memory_space=pltpu.SMEM)
HBM = pl.BlockSpec(memory_space=pltpu.HBM)
ANY = pl.BlockSpec(memory_space=pl.ANY)
VMEM = pl.BlockSpec(memory_space=pltpu.VMEM)
MIB = 1024 * 1024


def shape(dims, kind):
    return jax.ShapeDtypeStruct(dims, kind)


def whole(*dims):
    return pl.BlockSpec(dims, lambda *_: (0,) * len(dims))


def call(kernel, name, grid, ins, outs, args, us, scratch=(), vmem=20):
    results = pl.pallas_call(
        kernel,
        grid=grid,
        out_shape=tuple(shape(dims, kind) for _, dims, kind in outs),
        in_specs=ins,
        out_specs=tuple(spec for spec, _, _ in outs),
        scratch_shapes=list(scratch),
        compiler_params=pltpu.CompilerParams(vmem_limit_bytes=vmem * MIB),
        cost_estimate=pl.CostEstimate(
            flops=1000, bytes_accessed=int(us * 3.6e6), transcendentals=0
        ),
        name=name,
    )(*args)
    return results


def shards(
    right_sides,
    left_sides,
    near_blocks,
    near_columns,
    cluster_points,
    leaf_basis,
    transfer,
    far_parents,
    far_count,
    coupling,
    slab_transfer,
    apex_coupling,
):
    rhs = right_sides.shape[0]
    clusters = near_blocks.shape[0]
    me = lax.axis_index(AXES)
    devices = lax.axis_size(AXES)
    block = (rhs, B)
    all_clusters = (clusters, *block)
    half = devices // 2
    place = me.astype(jnp.int32)[None]
    first = place * clusters - HW
    columns = near_columns.T
    reduce_table, gather_table = slot_tables(devices)

    def rows(n, kind=BF):
        return (VMEM, (n, *block), kind)

    def at_rest(*values):
        return [pltpu.with_memory_space_constraint(value, pltpu.HBM) for value in values]

    mright, mleft, own, partial, sent, sums = call(
        rise_kernel,
        "rise",
        (),
        [SMEM] * 2 + [HBM] * 9,
        [
            rows(clusters),
            rows(clusters),
            rows(1),
            rows(half + 1, F32),
            rows(half + 3, F32),
            rows(2, F32),
        ],
        (
            place,
            far_count,
            *at_rest(
                cluster_points,
                far_parents,
                reduce_table,
                right_sides,
                left_sides,
                leaf_basis,
                transfer,
                slab_transfer,
                coupling,
            ),
        ),
        us=5,
        scratch=[
            pltpu.SMEM(cluster_points.shape, jnp.int32),
            pltpu.SMEM(far_parents.shape, jnp.int32),
            pltpu.SMEM(reduce_table.shape, jnp.int32),
            pltpu.VMEM(right_sides.shape, BF),
            pltpu.VMEM(left_sides.shape, BF),
            pltpu.VMEM(leaf_basis.shape, BF),
            pltpu.VMEM(transfer.shape, F32),
            pltpu.VMEM(slab_transfer.shape, F32),
            pltpu.VMEM(coupling.shape, F32),
            pltpu.SemaphoreType.DMA((16,)),
        ],
    )
    came = to_other_core(sent)
    came_own = routed(own, GATHER_STEPS[0])
    def fold(step, came, partial, sums, *rest, after):
        n = half >> step
        m = 2 if step == 0 or STEPS[step - 1][0] != X else 4
        a = 2 << step
        size = n // 2 * (2 if step >= 2 else 1) + 2 * m + (a if step < 5 else 0)
        args = (came, partial, sums, *rest)
        return call(
            functools.partial(fold_kernel, step),
            "fold",
            (),
            [VMEM] * len(args) + [ANY],
            [rows(size), rows(n // 2, F32), rows(m, F32), rows(a)],
            (*args, after),
            us=0.3,
        )

    payload, partial, sums, gathered = fold(0, came, partial, sums, own, came_own, after=own)
    came = routed(payload, STEPS[0])
    near_out, near_back, to_chip, to_core = call(
        near_kernel,
        "near",
        (),
        [SMEM] * 3 + [VMEM] * 3 + [ANY],
        [rows(clusters, F32), rows(clusters + 2 * HW, F32), rows(2 * HW), rows(2 * HW)],
        (place, columns, first, mright, mleft, near_blocks, payload),
        us=5,
    )
    chip_came = to_other_chips(to_chip)
    core_came = to_other_core(to_core)

    def edges(low_core, came, after):
        return call(
            functools.partial(edge_kernel, low_core),
            "edge",
            (),
            [SMEM] * 3 + [VMEM] * 2 + [ANY],
            [rows(HW, F32)] * 2,
            (place, columns, first, came, near_blocks, after),
            us=0.8,
        )

    after = near_out
    for step in range(1, len(STEPS)):
        payload, partial, sums, gathered = fold(
            step, came, partial, sums, gathered, after=after
        )
        came = routed(payload, STEPS[step])
        after = payload
        if step == 1:
            chain_out, chain_back = edges(0, chip_came, payload)
            after = chain_out
        if step == 2:
            pair_out, pair_back = edges(1, core_came, payload)
            after = pair_out
    gathered_other = to_other_core(gathered)
    (far_right,) = call(
        forward_kernel,
        "forward",
        (),
        [SMEM] * 4 + [VMEM] * 7 + [ANY],
        [(VMEM, block, F32)],
        (
            place,
            far_count,
            far_parents,
            gather_table,
            gathered,
            gathered_other,
            coupling,
            apex_coupling,
            slab_transfer,
            transfer,
            leaf_basis,
            payload,
        ),
        us=2.5,
        scratch=[pltpu.VMEM((devices, *block), BF)],
    )
    wide = (rhs, clusters * B)
    return call(
        down_kernel,
        "down",
        (),
        [SMEM] * 2 + [VMEM] * 14,
        [(HBM, wide, F32)] * 2,
        (
            place,
            cluster_points,
            far_right,
            partial,
            sums,
            came,
            apex_coupling,
            slab_transfer,
            transfer,
            leaf_basis,
            near_out,
            near_back,
            pair_out,
            pair_back,
            chain_out,
            chain_back,
        ),
        us=4,
        scratch=[
            pltpu.VMEM(wide, F32),
            pltpu.VMEM(wide, F32),
            pltpu.SemaphoreType.DMA((8,)),
        ],
    )


def solution(mesh):
    return jax.shard_map(
        shards,
        mesh=mesh,
        in_specs=(
            P(None, AXES),
            P(None, AXES),
            P(AXES, None, None, None),
            P(AXES, None),
            P(AXES),
            P(AXES, None, None),
            P(AXES, None, None),
            P(AXES, None),
            P(AXES),
            P(AXES, None, None, None),
            P(AXES, None, None),
            P(),
        ),
        out_specs=(P(None, AXES), P(None, AXES)),
        check_vma=False,
    )
```

```python
import functools

import jax
import jax.numpy as jnp
import numpy as np
from jax import lax
from jax.experimental import pallas as pl
from jax.experimental.pallas import tpu as pltpu
from jax.sharding import PartitionSpec as P

B = 128
HW = 4
AXES = ("slab", "leaf")
BF = jnp.bfloat16
F32 = jnp.float32

Z, Y, X = 1, 3, 5
CORE_1 = {Y: Z, Z: Y, X: X}
STEPS = ((Y, 0), (Y, 1), (Z, 0), (Z, 1), (X, 0), (X, 1))
GATHER_STEPS = (STEPS[5], *STEPS[:5])


def routed(block, step):
    axis, turn = step
    route = []
    for i in range(lax.axis_size(AXES)):
        pairing = 1 if (i & 1) == turn else 3
        route.append((i, i ^ (pairing << (CORE_1[axis] if i & 1 else axis))))
    return lax.ppermute(block, AXES, route)


def to_other_core(block):
    return lax.ppermute(block, AXES, [(i, i ^ 1) for i in range(lax.axis_size(AXES))])


def to_other_chips(block):
    devices = range(lax.axis_size(AXES))
    route = [(i, i - 1 + 2 * (i & 1)) for i in devices]
    return lax.ppermute(block, AXES, [(i, j) for i, j in route if j in devices])


def slot_tables(devices):
    def table(order):
        slots = np.zeros((2, devices), np.int32)
        for core in range(2):
            for difference in range(devices):
                other = difference & 1
                for place, (axis, turn) in enumerate(order):
                    axis = CORE_1[axis] if core ^ other else axis
                    low, high = (difference >> axis) & 1, (difference >> (axis + 1)) & 1
                    by_one = turn == core ^ other
                    slots[core, difference] |= (low ^ high if by_one else high) << place
                slots[core, difference] |= other << len(order)
        return jnp.asarray(slots.reshape(-1))

    return table(STEPS[::-1]), table(GATHER_STEPS)


def slot_in(table, parents, f, me, devices):
    return table[(me & 1) * devices + (parents[0, f] ^ me)]


def two(value):
    high = value.astype(BF)
    return high, (value - high.astype(F32)).astype(BF)


NN = (((1,), (0,)), ((), ()))
NT = (((1,), (1,)), ((), ()))


def dot(a, b, how):
    return lax.dot_general(a, b, how, preferred_element_type=F32)


def dot3(a, b, how):
    (ah, al), (bh, bl) = two(a), two(b)
    left = jnp.concatenate([ah, al, ah], axis=1)
    right = jnp.concatenate([bh, bh, bl], axis=1 if how is NT else 0)
    return dot(left, right, how)


def stacked(value):
    high, low = two(value)
    upper = jnp.concatenate([high, high], axis=1)
    return jnp.concatenate([upper, jnp.concatenate([low, jnp.zeros_like(low)], axis=1)], axis=0)


def both(value):
    half = value.shape[0] // 2
    return value[:half] + value[half:]


def diagonal(a, b):
    upper = jnp.concatenate([a, jnp.zeros_like(a)], axis=1)
    return jnp.concatenate([upper, jnp.concatenate([jnp.zeros_like(b), b], axis=1)], axis=0)


def pair_mask(points, c, rows):
    lane = lax.broadcasted_iota(jnp.int32, (rows, 2 * B), 1)
    return lane < jnp.where(lane < B, points[c], B + points[c + 1])


def rise_kernel(
    place,
    count,
    points_hbm,
    parents_hbm,
    table_hbm,
    right_hbm,
    left_hbm,
    basis_hbm,
    transfer_hbm,
    lift_hbm,
    coupling_hbm,
    mright,
    mleft,
    pright,
    keep,
    send,
    sums,
    points,
    parents,
    table,
    right,
    left,
    basis,
    transfer,
    lift,
    coupling,
    done,
):
    rhs = right.shape[0]
    clusters = basis.shape[0]
    far_slots = coupling.shape[1]
    half = keep.shape[0] - 1
    pieces, far_pieces = 2, 4
    count_of = iter(range(done.shape[0]))

    def fetch(source, target, index):
        return pltpu.make_async_copy(source.at[index], target.at[index], done.at[next(count_of)])

    per = clusters // pieces
    early = []
    for j in range(pieces):
        some = pl.ds(j * per, per)
        columns = (slice(None), pl.ds(j * per * B, per * B))
        early.append(
            [
                fetch(right_hbm, right, columns),
                fetch(left_hbm, left, columns),
                fetch(basis_hbm, basis, some),
                fetch(transfer_hbm, transfer, some),
            ]
        )
    early[0].append(fetch(points_hbm, points, slice(None)))
    early[1].append(fetch(parents_hbm, parents, slice(None)))
    early[1].append(fetch(table_hbm, table, slice(None)))
    early[1].append(fetch(lift_hbm, lift, slice(None)))
    far_per = far_slots // far_pieces
    late = [
        fetch(coupling_hbm, coupling, (slice(None), pl.ds(j * far_per, far_per)))
        for j in range(far_pieces)
    ]
    for copy in [*early[0], *early[1]]:
        copy.start()
    keep[...] = jnp.zeros_like(keep)
    send[...] = jnp.zeros_like(send)

    part = jnp.zeros((4 * rhs, B), F32)
    for j in range(pieces):
        for copy in early[j]:
            copy.wait()
        if j == 0:
            for copy in late:
                copy.start()
        for c in range(j * per, (j + 1) * per, 2):
            mask = pair_mask(points, c, rhs)
            columns = slice(c * B, (c + 2) * B)
            xr = jnp.where(mask, right[:, columns].astype(F32), 0.0).astype(BF)
            xl = jnp.where(mask, left[:, columns].astype(F32), 0.0).astype(BF)
            for q in range(2):
                mright[c + q] = xr[:, q * B : (q + 1) * B]
                mleft[c + q] = xl[:, q * B : (q + 1) * B]
            leaf = dot(jnp.concatenate([xr, xl], axis=0), diagonal(basis[c], basis[c + 1]), NT)
            high, low = two(jnp.concatenate([transfer[c], transfer[c + 1]], axis=0))
            part = part + dot(stacked(leaf), jnp.concatenate([high, low], axis=0), NN)
    total = both(part)
    pright[0] = total[:rhs].astype(BF)
    shares = dot3(total, lift[0], NN)
    for q in range(2):
        value = shares[q * rhs : (q + 1) * rhs]
        send[half + 1 + q] = value
        sums[q] = value

    wide = stacked(total[rhs:])
    me = place[0]
    group = 8
    for j in range(far_pieces):
        late[j].wait()
        for start in range(j * far_per, (j + 1) * far_per, group):
            values = []
            for f in range(start, start + group, 2):
                (ah, al), (bh, bl) = two(coupling[0, f]), two(coupling[0, f + 1])
                high, low = (jnp.concatenate(pair, axis=1) for pair in ((ah, bh), (al, bl)))
                value = both(dot(wide, jnp.concatenate([high, low], axis=0), NN))
                values += [value[:, :B], value[:, B:]]
            for q, value in enumerate(values):
                f = start + q
                slot = slot_in(table, parents, f, me, 2 * half)
                live = f < count[0]
                own = jnp.where(live & (slot < half), slot, half)
                other = jnp.where(live & (slot >= half), slot - half, half)
                keep[own] = value
                send[other] = value

def lay_out(payload, going, exact, sums, *rest):
    high, low = two(going)
    start = going.shape[0]
    payload[:start] = high
    if exact:
        payload[start : 2 * start] = low
        start = 2 * start
    for part in (*two(sums), *rest):
        payload[start : start + part.shape[0]] = part
        start = start + part.shape[0]


def fold_kernel(step, came, partial, sums, *refs):
    gathered = refs[0]
    payload, keep, sums_next, gathered_next = refs[-4:]
    n = 2 * keep.shape[0]
    m = sums.shape[0]
    if step == 0:
        total = partial[:n] + came[:n]
        got = came[n + 1 :]
        more = refs[1][...]
    else:
        total = partial[...] + came[:n].astype(F32)
        start = n
        if step >= 3:
            total = total + came[n : 2 * n].astype(F32)
            start = 2 * n
        got = came[start : start + m].astype(F32) + came[start + m : start + 2 * m].astype(F32)
        more = came[start + 2 * m :]
    if sums_next.shape[0] == m:
        sums_next[...] = sums[...] + got
    else:
        sums_next[:m] = sums[...]
        sums_next[m:] = got
    keep[...] = total[: n // 2]
    a = gathered.shape[0]
    gathered_next[:a] = gathered[...]
    gathered_next[a:] = more
    parts = [gathered_next[...]] if step < 5 else []
    lay_out(payload, total[n // 2 :], step >= 2, sums_next[...], *parts)


def rows_of(blocks, c):
    return jnp.concatenate([blocks[c, s] for s in range(blocks.shape[1])], axis=1)


def add_back(columns, first, mleft, blocks, clusters, back):
    done = []
    for c in clusters:
        places = [columns[s, c] - first[0] for s in range(blocks.shape[1])]
        done.append((places, dot(mleft[c], rows_of(blocks, c), NN)))
    for places, value in done:
        held = [back[place] for place in places]
        for s, place in enumerate(places):
            back[place] = held[s] + value[:, s * B : (s + 1) * B]


def near_kernel(place, columns, first, mright, mleft, blocks, _, out, back, to_chip, to_core):
    clusters = mright.shape[0]
    slots = blocks.shape[1]
    back[...] = jnp.zeros_like(back)
    for start in range(0, clusters, 4):
        group = range(start, start + 4)
        for c in group:
            inside = []
            for s in range(slots):
                own = columns[s, c] - first[0] - HW
                value = mright[jnp.clip(own, 0, clusters - 1)]
                is_own = (own >= 0) & (own < clusters)
                inside.append(jnp.where(is_own, value, jnp.zeros_like(value)))
            out[c] = dot(rows_of(blocks, c), jnp.concatenate(inside, axis=1), NT).T
        add_back(columns, first, mleft, blocks, group, back)
    core = place[0] & 1
    for side, sent in ((core, to_chip), (1 - core, to_core)):
        sent[:HW] = mright[pl.ds(side * (clusters - HW), HW)]
        sent[HW:] = back[pl.ds(side * (clusters + HW), HW)].astype(BF)


def edge(low, columns, first, halo, blocks, out):
    slots = blocks.shape[1]
    clusters = columns.shape[1]
    start = jnp.where(low, 0, clusters - HW)
    row_start = first[0] + jnp.where(low, 0, clusters + HW)
    for g in range(HW):
        c = start + g
        values = []
        for s in range(slots):
            row = columns[s, c] - row_start
            value = halo[jnp.clip(row, 0, HW - 1)]
            is_there = (row >= 0) & (row < HW)
            values.append(jnp.where(is_there, value, jnp.zeros_like(value)))
        out[g] = dot(rows_of(blocks, c), jnp.concatenate(values, axis=1), NT).T


def edge_kernel(low_core, place, columns, first, came, blocks, _, out, back):
    edge((place[0] & 1) == low_core, columns, first, came, blocks, out)
    back[...] = came[HW:].astype(F32)


def forward_kernel(place, count, parents, table, own, other, coupling, *rest):
    out, all_of = rest[-2:]
    far_slots = coupling.shape[1]
    half = all_of.shape[0] // 2
    all_of[:half] = own[:half]
    all_of[half:] = other[:half]
    me = place[0]
    total = jnp.zeros((B, own.shape[1]), F32)
    group = 48
    for start in range(0, far_slots, group):
        rows, values = [], []
        for f in range(start, start + group):
            value = all_of[slot_in(table, parents, f, me, 2 * half)]
            value = jnp.where(f < count[0], value, jnp.zeros_like(value))
            values += [value, value]
            rows += two(coupling[0, f])
        total = total + dot(
            jnp.concatenate(rows, axis=1), jnp.concatenate(values, axis=1), NT
        )
    out[...] = total.T


def down_kernel(
    place,
    points,
    far_right,
    partial,
    sums,
    came,
    apex,
    lift,
    transfer,
    basis,
    near_out,
    near_back,
    pair_out,
    pair_back,
    chain_out,
    chain_back,
    product_hbm,
    adjoint_hbm,
    product,
    adjoint,
    done,
):
    clusters, rhs = near_out.shape[:2]
    core = place[0] & 1
    slab = place[0] >> X
    got = came[2:6].astype(F32) + came[6:10].astype(F32)
    slabs = [sums[2], sums[3], got[0], got[1], got[2], got[3]]
    top_right = jnp.zeros((rhs, B), F32)
    top_left = jnp.zeros((rhs, B), F32)
    for t, mask in enumerate((1 + 2 * core, 3 - 2 * core, 2)):
        top_right = top_right + dot3(slabs[2 * t], apex[slab, slab ^ mask], NT)
        top_left = top_left + dot3(slabs[2 * t + 1], apex[slab ^ mask, slab], NN)
    far_left = partial[0] + (came[0].astype(F32) + came[1].astype(F32))
    hats = stacked(
        jnp.concatenate([far_right[...], far_left], axis=0)
        + dot3(jnp.concatenate([top_right, top_left], axis=0), lift[0], NT)
    )

    pieces = done.shape[0] // 2
    per = clusters // pieces
    copies = []
    for j in range(pieces):
        for c in range(j * per, (j + 1) * per, 2):
            high, low = two(jnp.concatenate([transfer[c], transfer[c + 1]], axis=0))
            down = both(dot(hats, jnp.concatenate([high, low], axis=1), NT))
            high, low = two(down)
            two_bases = diagonal(basis[c], basis[c + 1])
            far = dot(
                jnp.concatenate([high, low], axis=1),
                jnp.concatenate([two_bases, two_bases], axis=0),
                NN,
            )
            for q in range(2):
                k, g = c + q, (c + q) % HW
                out, back = near_out[k], near_back[HW + k]
                if k < HW or k >= clusters - HW:
                    in_chip = core == (1 if k < HW else 0)
                    out = out + jnp.where(in_chip, pair_out[g], chain_out[g])
                    back = back + jnp.where(in_chip, pair_back[g], chain_back[g])
                mask = lax.broadcasted_iota(jnp.int32, (rhs, B), 1) < points[k]
                lanes = slice(q * B, (q + 1) * B)
                place_of = slice(k * B, (k + 1) * B)
                product[:, place_of] = jnp.where(mask, out + far[:rhs, lanes], 0.0)
                adjoint[:, place_of] = jnp.where(mask, back + far[rhs:, lanes], 0.0)
        index = (slice(None), pl.ds(j * per * B, per * B))
        for q, (source, target) in enumerate(((product, product_hbm), (adjoint, adjoint_hbm))):
            copy = pltpu.make_async_copy(source.at[index], target.at[index], done.at[2 * j + q])
            copy.start()
            copies.append(copy)
    for copy in copies:
        copy.wait()


SMEM = pl.BlockSpec(memory_space=pltpu.SMEM)
HBM = pl.BlockSpec(memory_space=pltpu.HBM)
ANY = pl.BlockSpec(memory_space=pl.ANY)
VMEM = pl.BlockSpec(memory_space=pltpu.VMEM)
MIB = 1024 * 1024


def shape(dims, kind):
    return jax.ShapeDtypeStruct(dims, kind)


def whole(*dims):
    return pl.BlockSpec(dims, lambda *_: (0,) * len(dims))


def call(kernel, name, grid, ins, outs, args, us, scratch=(), vmem=20):
    results = pl.pallas_call(
        kernel,
        grid=grid,
        out_shape=tuple(shape(dims, kind) for _, dims, kind in outs),
        in_specs=ins,
        out_specs=tuple(spec for spec, _, _ in outs),
        scratch_shapes=list(scratch),
        compiler_params=pltpu.CompilerParams(vmem_limit_bytes=vmem * MIB),
        cost_estimate=pl.CostEstimate(
            flops=1000, bytes_accessed=int(us * 3.6e6), transcendentals=0
        ),
        name=name,
    )(*args)
    return results


def shards(
    right_sides,
    left_sides,
    near_blocks,
    near_columns,
    cluster_points,
    leaf_basis,
    transfer,
    far_parents,
    far_count,
    coupling,
    slab_transfer,
    apex_coupling,
):
    rhs = right_sides.shape[0]
    clusters = near_blocks.shape[0]
    me = lax.axis_index(AXES)
    devices = lax.axis_size(AXES)
    block = (rhs, B)
    all_clusters = (clusters, *block)
    half = devices // 2
    place = me.astype(jnp.int32)[None]
    first = place * clusters - HW
    columns = near_columns.T
    reduce_table, gather_table = slot_tables(devices)

    def rows(n, kind=BF):
        return (VMEM, (n, *block), kind)

    def at_rest(*values):
        return [pltpu.with_memory_space_constraint(value, pltpu.HBM) for value in values]

    mright, mleft, own, partial, sent, sums = call(
        rise_kernel,
        "rise",
        (),
        [SMEM] * 2 + [HBM] * 9,
        [
            rows(clusters),
            rows(clusters),
            rows(1),
            rows(half + 1, F32),
            rows(half + 3, F32),
            rows(2, F32),
        ],
        (
            place,
            far_count,
            *at_rest(
                cluster_points,
                far_parents,
                reduce_table,
                right_sides,
                left_sides,
                leaf_basis,
                transfer,
                slab_transfer,
                coupling,
            ),
        ),
        us=5,
        scratch=[
            pltpu.SMEM(cluster_points.shape, jnp.int32),
            pltpu.SMEM(far_parents.shape, jnp.int32),
            pltpu.SMEM(reduce_table.shape, jnp.int32),
            pltpu.VMEM(right_sides.shape, BF),
            pltpu.VMEM(left_sides.shape, BF),
            pltpu.VMEM(leaf_basis.shape, BF),
            pltpu.VMEM(transfer.shape, F32),
            pltpu.VMEM(slab_transfer.shape, F32),
            pltpu.VMEM(coupling.shape, F32),
            pltpu.SemaphoreType.DMA((16,)),
        ],
    )
    came = to_other_core(sent)
    came_own = routed(own, GATHER_STEPS[0])
    def fold(step, came, partial, sums, *rest, after):
        n = half >> step
        m = 2 if step == 0 or STEPS[step - 1][0] != X else 4
        a = 2 << step
        size = n // 2 * (2 if step >= 2 else 1) + 2 * m + (a if step < 5 else 0)
        args = (came, partial, sums, *rest)
        return call(
            functools.partial(fold_kernel, step),
            "fold",
            (),
            [VMEM] * len(args) + [ANY],
            [rows(size), rows(n // 2, F32), rows(m, F32), rows(a)],
            (*args, after),
            us=0.3,
        )

    payload, partial, sums, gathered = fold(0, came, partial, sums, own, came_own, after=own)
    came = routed(payload, STEPS[0])
    near_out, near_back, to_chip, to_core = call(
        near_kernel,
        "near",
        (),
        [SMEM] * 3 + [VMEM] * 3 + [ANY],
        [rows(clusters, F32), rows(clusters + 2 * HW, F32), rows(2 * HW), rows(2 * HW)],
        (place, columns, first, mright, mleft, near_blocks, payload),
        us=5,
    )
    chip_came = to_other_chips(to_chip)
    core_came = to_other_core(to_core)

    def edges(low_core, came, after):
        return call(
            functools.partial(edge_kernel, low_core),
            "edge",
            (),
            [SMEM] * 3 + [VMEM] * 2 + [ANY],
            [rows(HW, F32)] * 2,
            (place, columns, first, came, near_blocks, after),
            us=0.8,
        )

    after = near_out
    for step in range(1, len(STEPS)):
        payload, partial, sums, gathered = fold(
            step, came, partial, sums, gathered, after=after
        )
        came = routed(payload, STEPS[step])
        after = payload
        if step == 1:
            pair_out, pair_back = edges(1, core_came, payload)
            after = pair_out
        if step == 2:
            after = chip_came
        if step == 3:
            chain_out, chain_back = edges(0, chip_came, payload)
            after = chain_out
    gathered_other = to_other_core(gathered)
    (far_right,) = call(
        forward_kernel,
        "forward",
        (),
        [SMEM] * 4 + [VMEM] * 7 + [ANY],
        [(VMEM, block, F32)],
        (
            place,
            far_count,
            far_parents,
            gather_table,
            gathered,
            gathered_other,
            coupling,
            apex_coupling,
            slab_transfer,
            transfer,
            leaf_basis,
            payload,
        ),
        us=2.5,
        scratch=[pltpu.VMEM((devices, *block), BF)],
    )
    wide = (rhs, clusters * B)
    return call(
        down_kernel,
        "down",
        (),
        [SMEM] * 2 + [VMEM] * 14,
        [(HBM, wide, F32)] * 2,
        (
            place,
            cluster_points,
            far_right,
            partial,
            sums,
            came,
            apex_coupling,
            slab_transfer,
            transfer,
            leaf_basis,
            near_out,
            near_back,
            pair_out,
            pair_back,
            chain_out,
            chain_back,
        ),
        us=4,
        scratch=[
            pltpu.VMEM(wide, F32),
            pltpu.VMEM(wide, F32),
            pltpu.SemaphoreType.DMA((8,)),
        ],
    )


def solution(mesh):
    return jax.shard_map(
        shards,
        mesh=mesh,
        in_specs=(
            P(None, AXES),
            P(None, AXES),
            P(AXES, None, None, None),
            P(AXES, None),
            P(AXES),
            P(AXES, None, None),
            P(AXES, None, None),
            P(AXES, None),
            P(AXES),
            P(AXES, None, None, None),
            P(AXES, None, None),
            P(),
        ),
        out_specs=(P(None, AXES), P(None, AXES)),
        check_vma=False,
    )
```
